32 devices in a mesh: seq: 16 (over z, x, core), expert: 2 (over y).
Axes of the slice: x: 2, y: 2, z: 4, core: 2. Of those that a mesh axis runs over, the one named last changes fastest.
Arguments:
- query_cols: bfloat16 [256, 32768], P('expert', 'seq'), may hold values from -16 to 16
- key_cols: bfloat16 [256, 32768], P('expert', 'seq'), may hold values from -6 to 6
- value_cols: bfloat16 [256, 32768], P('expert', 'seq'), may hold values from -12 to 12
- block_list: int32 [256, 4], P('seq'), may hold values from 0 to 255, as said below
- residual: bfloat16 [32768, 256], P(('seq', 'expert')), may hold values from -6 to 6
- out_proj: bfloat16 [256, 256], replicated, may hold values from -0.375 to 0.375
- norm_gain: float32 [256], replicated, may hold values from 0.1 to 1.9
- router_weight: bfloat16 [256, 16], replicated, may hold values from -0.375 to 0.375
- expert_ids: int32 [32768, 2], P(('seq', 'expert')), may hold values from 0 to 15, all different within a row; in each aligned block of 1024 rows (0 to 1023, 1024 to 2047, ...) at most 256 rows name the same one
- expert_in: bfloat16 [16, 256, 512], P('expert'), may hold values from -0.375 to 0.375
- expert_out: bfloat16 [16, 512, 256], P('expert'), may hold values from -0.25 to 0.25
- cotangent: bfloat16 [32768, 256], P(('seq', 'expert')), may hold values from -6 to 6
Outputs:
- layer_out: bfloat16 [32768, 256], P(('seq', 'expert'))
- grad_stream: bfloat16 [32768, 256], P(('seq', 'expert'))
- grad_w_in: float32 [16, 256, 512], P('expert')
- grad_w_out: float32 [16, 512, 256], P('expert')
The draws below stay inside these ranges and needn't reach their ends.
Inputs may be any that keep to these rules, and one draw needn't show every extreme that they name: `block_list`: global key block ids. Among the entries of the 16 query blocks of one seq index, no owner index (id // 16) appears more than 8 times, and one owner, the same for every seq index, appears exactly 8 times. A row may repeat a block. `expert_ids`: each row names 2 different experts; in each aligned block of 1024 rows (the rows of one device) no expert is named more than 256 times.
All inputs are finite; a program needn't handle non-finite values.
Results may differ from the reference program's by a relative error of at most 0.0081.
Values may be sent and summed in bfloat16 or wider, within the bound.
No kernel may reach another device: no remote copies, remote signals or barrier semaphores. Data moves between devices by JAX's collectives and lax.ppermute only.
A program may use at most 128 MiB of HBM per device.

```python
import math
import jax
import jax.numpy as jnp
import numpy as np
from jax import lax

D = 256
HEADS = 8
HD = 32
FF = 512
EXPERTS = 16
TOPK = 2
BLOCK = 128
DEG = 4
BLK_SEQ = 16
NBLK = 256
NODES = 32768
T_DEV = 1024
CAP = 8
CAPE = 256


def block_table(key):
    device_count = NBLK // BLK_SEQ
    pair_count = BLK_SEQ * DEG
    slot_count = device_count * CAP
    hot_owner = jax.random.randint(jax.random.fold_in(key, 7), (), 0, device_count)
    slot_owner = jnp.arange(slot_count, dtype=jnp.int32) // CAP
    slot_range = jnp.arange(slot_count, dtype=jnp.int32)

    def one_device(device_index):
        device_key = jax.random.fold_in(key, 100 + device_index)
        ranking = jax.random.permutation(jax.random.fold_in(device_key, 1), slot_count).astype(jnp.int32)
        score_ints = jnp.where(slot_owner == hot_owner, slot_range - slot_count, ranking)
        picked = jnp.argsort(score_ints, stable=True)[:pair_count]
        owners = slot_owner[picked]
        shuffle = jax.random.permutation(jax.random.fold_in(device_key, 2), pair_count)
        owners = owners[shuffle]
        inner_ids = jax.random.randint(jax.random.fold_in(device_key, 3), (pair_count,), 0, BLK_SEQ)
        return (owners * BLK_SEQ + inner_ids).astype(jnp.int32)
    table = jax.vmap(one_device)(jnp.arange(device_count, dtype=jnp.int32))
    return table.reshape(NBLK, DEG)


def drawn_keys(key):
    base_key = jax.random.fold_in(key, 21)
    return jax.random.truncated_normal(jax.random.fold_in(base_key, 1), -6.0, 6.0, (D, NODES), jnp.float32)


def draw_block_list(key, part):
    return block_table(jax.random.fold_in(key, 11))


def draw_key_cols(key, part):
    field = drawn_keys(key)
    return field.astype(jnp.bfloat16)


def draw_query_cols(key, part):
    base_key = jax.random.fold_in(key, 31)
    field = 1.5 * jax.random.truncated_normal(jax.random.fold_in(base_key, 1), -6.0, 6.0, (D, NODES), jnp.float32)
    return field.astype(jnp.bfloat16)


def levels(rng, shape, shards, least, largest):
    loudness, own = 1.0, jax.random.fold_in(rng, 6)
    for dim, blocks in shards:
        steps = jnp.exp(jax.random.uniform(jax.random.fold_in(own, dim), (blocks,), jnp.float32, least / len(shards), largest / len(shards)))
        loudness = loudness * jnp.repeat(steps, shape[dim] // blocks).reshape([-1 if axis == dim else 1 for axis in range(len(shape))])
    return loudness


def assign_block(own_key, own, number, rows, amount, top, most, slope):
    sequence = jax.random.permutation(own_key, amount)
    crowded, ordinary = portions_of(amount, rows * top, most, slope, True), portions_of(amount, rows * top, most, slope, False)
    places = jnp.arange(amount)

    def named(tallies, rotation):
        used = int((tallies > 0).sum())
        fixed = max(1, used // 4)
        shifted = fixed + (places - fixed + rotation * (used - fixed)) % max(1, amount - fixed)
        return jnp.zeros((amount,), jnp.int32).at[sequence[jnp.where(places < fixed, places, shifted)]].set(jnp.asarray(tallies, jnp.int32))

    tallies = jnp.where(number % 4 == 0, named(crowded, number // 4), named(ordinary, number - number // 4 - 1))
    mixed = jax.random.permutation(jax.random.fold_in(own, 3), amount)
    donor, sink = mixed[0:amount // 2 * 2:2], mixed[1:amount // 2 * 2:2]
    room = jnp.minimum(tallies[donor] - 1, most - tallies[sink]) // 2
    room = jnp.where((donor == sequence[0]) | (sink == sequence[0]) | (tallies[sink] == 0), 0, jnp.maximum(room, 0))
    shifted = jax.random.randint(jax.random.fold_in(own, 4), (amount // 2,), 0, 1 << 20) % (room + 1)
    tallies = tallies.at[donor].add(-shifted).at[sink].add(shifted)
    members = jnp.searchsorted(jnp.cumsum(tallies), jnp.arange(rows * top), side="right").astype(jnp.int32)
    table = members.reshape(top, rows).T
    table = table[jax.random.permutation(jax.random.fold_in(own, 1), rows)]
    rotation = jax.random.randint(jax.random.fold_in(own, 2), (rows, 1), 0, top)
    return jnp.take_along_axis(table, (jnp.arange(top)[None, :] + rotation) % top, axis=1)


def portions_of(amount, total, bound, slope, full):
    weights = [(1 << 20) // math.isqrt(rank ** slope) + 1 for rank in range(1, amount + 1)]
    largest = bound if full else min(bound, max(-(-total // amount), total * weights[0] // sum(weights)))
    least = 1 if total - largest >= amount - 1 else 0
    holding, spare = [largest] + [least] * (amount - 1), total - largest - least * (amount - 1)
    while spare > 0:
        movable = [i for i in range(1, amount) if holding[i] < largest] or [i for i in range(1, amount) if holding[i] < bound]
        pool, left = sum([weights[i] for i in movable]), spare
        for i in movable:
            more = min(bound - holding[i], max(1, left * weights[i] // pool), spare)
            holding[i] = holding[i] + more
            spare = spare - more
    return np.array(holding)


def noise(stream_key, shape, spread, most, split=(), held_as=jnp.bfloat16):
    result = spread * jax.random.normal(stream_key, shape, jnp.float32)
    if split:
        result = result * levels(stream_key, shape, split, -0.22, 0.18)
    return jnp.clip(result, -most, most).astype(held_as)


def setup_inputs(seed: int = 0) -> dict:
    key_of = jax.random.split(jax.random.key(seed), 13)
    query_cols = draw_query_cols(jax.random.fold_in(key_of[12], 71), 0)
    key_cols = draw_key_cols(jax.random.fold_in(key_of[12], 71), 0)
    value_cols = noise(key_of[2], (D, NODES), 2.0, 12.0, ((0, 2), (1, 16)))
    block_list = draw_block_list(jax.random.fold_in(key_of[12], 71), 0)
    residual = noise(key_of[4], (NODES, D), 1.0, 6.0, ((0, 32),))
    out_proj = noise(key_of[5], (D, D), D ** -0.5, 0.375)
    norm_gain = jnp.clip(1.0 + 0.18 * jax.random.normal(key_of[6], (D,), jnp.float32), 0.1, 1.9)
    router_weight = noise(key_of[7], (D, EXPERTS), D ** -0.5, 0.375)
    expert_ids_keys = jax.random.split(jax.random.fold_in(key_of[8], 1), NODES // T_DEV)
    expert_ids_turns = jax.random.permutation(jax.random.fold_in(key_of[8], 3), NODES // T_DEV)
    expert_ids = jax.vmap(lambda own, number: assign_block(jax.random.fold_in(key_of[8], 2), own, number, T_DEV, EXPERTS, TOPK, CAPE, 2))(expert_ids_keys, expert_ids_turns).reshape((NODES, TOPK))
    expert_in = noise(key_of[9], (EXPERTS, D, FF), D ** -0.5, 0.375, ((0, 2),))
    expert_out = noise(key_of[10], (EXPERTS, FF, D), FF ** -0.5, 0.25, ((0, 2),))
    cotangent = noise(key_of[11], (NODES, D), 1.0, 6.0, ((0, 32),))
    return dict(query_cols=query_cols, key_cols=key_cols, value_cols=value_cols, block_list=block_list, residual=residual, out_proj=out_proj, norm_gain=norm_gain, router_weight=router_weight, expert_ids=expert_ids, expert_in=expert_in, expert_out=expert_out, cotangent=cotangent)


norm_eps = 1e-05
root_two_pi = 0.7978845608028654
cubic_term = 0.044715

def gelu_value(preact):
    inside = root_two_pi * (preact + cubic_term * preact * preact * preact)
    return 0.5 * preact * (1.0 + jnp.tanh(inside))

def gelu_slope(preact):
    inside = root_two_pi * (preact + cubic_term * preact * preact * preact)
    tanh_value = jnp.tanh(inside)
    return 0.5 * (1.0 + tanh_value) + 0.5 * preact * (1.0 - tanh_value * tanh_value) * root_two_pi * (1.0 + 3.0 * cubic_term * preact * preact)

def as_wide(values):
    return lax.optimization_barrier(values).astype(jnp.float32)

def attend_all(query_cols, key_cols, value_cols, block_list):
    query_blocks = query_cols.reshape(HEADS, HD, NBLK, BLOCK)
    key_blocks = key_cols.reshape(HEADS, HD, NBLK, BLOCK)
    value_blocks = value_cols.reshape(HEADS, HD, NBLK, BLOCK)
    scale_factor = 1.0 / math.sqrt(HD)
    highest = lax.Precision.HIGHEST

    def one_block(inputs):
        block_index, listed = inputs
        queries = lax.dynamic_index_in_dim(query_blocks, block_index, 2, keepdims=False).astype(jnp.float32)
        keys = jnp.take(key_blocks, listed, axis=2).reshape(HEADS, HD, DEG * BLOCK).astype(jnp.float32)
        values = jnp.take(value_blocks, listed, axis=2).reshape(HEADS, HD, DEG * BLOCK).astype(jnp.float32)
        scores = jnp.einsum('hdn,hdj->hnj', queries, keys, precision=highest) * scale_factor
        row_max = lax.optimization_barrier(jnp.max(scores, -1, keepdims=True))
        weights = jnp.exp(scores - row_max)
        row_sum = lax.optimization_barrier(jnp.sum(weights, -1))
        rounded = as_wide(weights.astype(jnp.bfloat16))
        attended = jnp.einsum('hnj,hdj->hdn', rounded, values, precision=highest) / row_sum[:, None, :]
        return attended.astype(jnp.bfloat16)
    outputs = lax.map(one_block, (jnp.arange(NBLK, dtype=jnp.int32), block_list))
    return jnp.transpose(outputs, (1, 2, 0, 3)).reshape(HEADS * HD, NODES)

def reference(query_cols, key_cols, value_cols, block_list, residual, out_proj, norm_gain, router_weight, expert_ids, expert_in, expert_out, cotangent):
    highest = lax.Precision.HIGHEST
    attended = attend_all(query_cols, key_cols, value_cols, block_list)
    projected = jnp.dot(attended.T, out_proj, preferred_element_type=jnp.float32)
    stream = (residual.astype(jnp.float32) + projected).astype(jnp.bfloat16)
    block_count = NODES // T_DEV
    full_in = expert_in.astype(jnp.float32)
    full_out = expert_out.astype(jnp.float32)
    router_float = router_weight.astype(jnp.float32)
    expert_range = jnp.arange(EXPERTS, dtype=jnp.int32)

    def step(carry, inputs):
        stream_rows, id_rows, cot_rows = inputs
        stream_float = stream_rows.astype(jnp.float32)
        inverse_rms = lax.rsqrt(lax.optimization_barrier(jnp.mean(stream_float * stream_float, -1, keepdims=True)) + norm_eps)
        normed = (stream_float * inverse_rms * norm_gain).astype(jnp.bfloat16)
        logits = jnp.dot(normed, router_weight, preferred_element_type=jnp.float32)
        gate_values = jax.nn.sigmoid(jnp.take_along_axis(logits, id_rows, 1))
        flat_ids = id_rows.reshape(-1)
        flat_hot = (flat_ids[:, None] == expert_range[None, :]).astype(jnp.int32)
        slot_rank = lax.optimization_barrier(jnp.sum((jnp.cumsum(flat_hot, 0) - flat_hot) * flat_hot, 1))
        position = flat_ids * CAPE + slot_rank

        def pack_rows(rows):
            filled = jnp.zeros((EXPERTS * CAPE, D), jnp.bfloat16).at[position].set(rows)
            return filled.reshape(EXPERTS, CAPE, D)

        def unpack_rows(buffer):
            return jnp.take(buffer.reshape(EXPERTS * CAPE, D), position, axis=0).reshape(T_DEV, TOPK, D)
        rows_in = as_wide(pack_rows(jnp.repeat(normed, TOPK, 0)))
        preact = jnp.einsum('erd,edf->erf', rows_in, full_in, precision=highest)
        hidden = gelu_value(preact).astype(jnp.bfloat16)
        hidden_wide = as_wide(hidden)
        produced = jnp.einsum('erf,efd->erd', hidden_wide, full_out, precision=highest).astype(jnp.bfloat16)
        expert_rows = as_wide(unpack_rows(produced))
        cot_float = cot_rows.astype(jnp.float32)
        layer_rows = (stream_float + lax.optimization_barrier(jnp.sum(gate_values[:, :, None] * expert_rows, 1))).astype(jnp.bfloat16)
        scaled = (gate_values[:, :, None] * cot_float[:, None, :]).astype(jnp.bfloat16).reshape(T_DEV * TOPK, D)
        cot_buffer = as_wide(pack_rows(scaled))
        grad_out = jnp.einsum('erf,erd->efd', hidden_wide, cot_buffer, precision=highest)
        grad_hidden = jnp.einsum('erd,efd->erf', cot_buffer, full_out, precision=highest)
        grad_pre = as_wide((grad_hidden * gelu_slope(preact)).astype(jnp.bfloat16))
        grad_in = jnp.einsum('erd,erf->edf', rows_in, grad_pre, precision=highest)
        grad_back = jnp.einsum('erf,edf->erd', grad_pre, full_in, precision=highest).astype(jnp.bfloat16)
        grad_gate = lax.optimization_barrier(jnp.sum(cot_float[:, None, :] * expert_rows, -1))
        grad_logit = grad_gate * gate_values * (1.0 - gate_values)
        id_hot = id_rows[:, :, None] == expert_range[None, None, :]
        logit_table = lax.optimization_barrier(jnp.sum(jnp.where(id_hot, grad_logit[:, :, None], 0.0), 1))
        router_term = jnp.dot(logit_table, router_float.T, precision=highest)
        grad_normed = lax.optimization_barrier(jnp.sum(as_wide(unpack_rows(grad_back)), 1)) + router_term
        gained = grad_normed * norm_gain
        grad_rows = cot_float + inverse_rms * gained - stream_float * inverse_rms ** 3 * lax.optimization_barrier(jnp.mean(stream_float * gained, -1, keepdims=True))
        return ((carry[0] + grad_in, carry[1] + grad_out), (layer_rows, grad_rows.astype(jnp.bfloat16)))
    start = (jnp.zeros((EXPERTS, D, FF), jnp.float32), jnp.zeros((EXPERTS, FF, D), jnp.float32))
    inputs = (stream.reshape(block_count, T_DEV, D), expert_ids.reshape(block_count, T_DEV, TOPK), cotangent.reshape(block_count, T_DEV, D))
    (grad_w_in, grad_w_out), (layer_out, grad_stream) = lax.scan(step, start, inputs)
    return (layer_out.reshape(NODES, D), grad_stream.reshape(NODES, D), grad_w_in, grad_w_out)
```

```python
import functools
import math

import jax
import jax.numpy as jnp
from jax import lax
from jax.experimental import pallas as pl
from jax.experimental.pallas import tpu as pltpu
from jax.sharding import PartitionSpec as P

HD = 32
WINDOW = 128
TILE = 128

norm_eps = 1e-05
root_two_pi = 0.7978845608028654
cubic_term = 0.044715

bf16 = jnp.bfloat16
f32 = jnp.float32
VMEM_BYTES = 48 * 1024 * 1024


def params(**kw):
    return pltpu.CompilerParams(vmem_limit_bytes=VMEM_BYTES, **kw)


def contract(a, b, da, db):
    return lax.dot_general(a, b, (((da,), (db,)), ((), ())), preferred_element_type=f32)


def ring_order(seq_count):
    rows = max(1, seq_count // 4)
    if seq_count % 4:
        return list(range(seq_count // 2))
    return [2 * z for z in range(rows)] + [2 * z + 1 for z in reversed(range(rows))]


def ring_pairs(seq_count, step):
    order = ring_order(seq_count)
    n = len(order)
    return [(2 * order[i] + c, 2 * order[(i + step) % n] + c) for i in range(n) for c in range(2)]


def sibling_pairs(seq_count):
    return [(s, s ^ 1) for s in range(seq_count)]


def shift_pairs(count, d):
    return [(i, (i + d) % count) for i in range(count)]


def gather_expert_axis(x, exp_count, axis=0):
    me = lax.axis_index("expert")
    size = x.shape[axis]
    shape = list(x.shape)
    shape[axis] = size * exp_count
    out = jnp.zeros(shape, x.dtype)
    out = lax.dynamic_update_slice_in_dim(out, x, me * size, axis)
    for d in range(1, exp_count):
        got = lax.ppermute(x, "expert", shift_pairs(exp_count, d))
        out = lax.dynamic_update_slice_in_dim(out, got, lax.rem(me + exp_count - d, exp_count) * size, axis)
    return out


def own_slots_kernel(k_ref, v_ref, kbuf_ref, vbuf_ref, sems):
    copies = [
        pltpu.make_async_copy(k_ref, kbuf_ref.at[0], sems.at[0]),
        pltpu.make_async_copy(v_ref, vbuf_ref.at[0], sems.at[1]),
    ]
    for copy in copies:
        copy.start()
    for copy in copies:
        copy.wait()


def own_slots(keys, values, slots):
    shape = jax.ShapeDtypeStruct((slots,) + keys.shape, keys.dtype)
    return pl.pallas_call(
        own_slots_kernel,
        in_specs=[pl.BlockSpec(memory_space=pl.ANY)] * 2,
        out_specs=[pl.BlockSpec(memory_space=pl.ANY)] * 2,
        out_shape=[shape, shape],
        scratch_shapes=[pltpu.SemaphoreType.DMA((2,))],
        name="own_slots",
    )(keys, values)


def ring_gather(keys, values, seq_count):
    n = seq_count // 2
    feat, nodes = keys.shape
    parts = 2 if feat >= 2 * HD else 1
    rows = feat // parts
    kbuf, vbuf = own_slots(keys, values, 2 * n)
    fwd, bwd, sib = ring_pairs(seq_count, 1), ring_pairs(seq_count, -1), sibling_pairs(seq_count)
    held = [(keys[i * rows : (i + 1) * rows], values[i * rows : (i + 1) * rows]) for i in range(parts)]
    for t in range(n):
        nxt = []
        for i, (k, v) in enumerate(held):
            if t > 0:
                k = lax.ppermute(k, "seq", fwd)
                v = lax.ppermute(v, "seq", bwd)
            nxt.append((k, v))
            if t > 0:
                kbuf = lax.dynamic_update_slice(kbuf, k[None], (t, i * rows, 0))
                vbuf = lax.dynamic_update_slice(vbuf, v[None], (t, i * rows, 0))
            ks = lax.ppermute(k, "seq", sib)
            vs = lax.ppermute(v, "seq", sib)
            kbuf = lax.dynamic_update_slice(kbuf, ks[None], (n + t, i * rows, 0))
            vbuf = lax.dynamic_update_slice(vbuf, vs[None], (n + t, i * rows, 0))
        held = nxt
    return kbuf, vbuf


def block_places(block_list, blk_seq, seq_count):
    order = ring_order(seq_count)
    n = len(order)
    inverse = [0] * n
    for i, chip in enumerate(order):
        inverse[chip] = i
    inverse = jnp.asarray(inverse, jnp.int32)
    me = lax.axis_index("seq")
    place = inverse[me // 2]
    owner = block_list // blk_seq
    local = block_list % blk_seq
    other = inverse[owner // 2]
    flag = ((owner ^ me) & 1) * n
    kslot = flag + lax.rem(place - other + n, n)
    vslot = flag + lax.rem(other - place + n, n)
    return kslot, vslot, local


def attention_kernel(degree, heads, kslot, vslot, local, q_ref, *refs):
    k_refs, v_refs, out_ref = refs[:degree], refs[degree : 2 * degree], refs[2 * degree]
    factor = math.log2(math.e) / math.sqrt(HD)
    cols = []
    for h in range(heads):
        rows = slice(h * HD, (h + 1) * HD)
        q = q_ref[rows, :]
        k = jnp.concatenate([r[0, rows, :] for r in k_refs], 1)
        v = jnp.concatenate([r[0, rows, :] for r in v_refs], 1)
        scores = contract(k, q, 0, 0)
        top = jnp.max(scores, 0, keepdims=True)
        probs = jnp.exp2((scores - top) * factor)
        total = jnp.sum(probs, 0, keepdims=True)
        out = jnp.dot(v, probs.astype(bf16), preferred_element_type=f32)
        cols.append(out / total)
    att = jnp.concatenate(cols, 0)
    out_ref[...] = att.T.astype(bf16)


def attention(queries, kbuf, vbuf, places, first, count, block_len):
    kslot, vslot, local = places
    degree = kslot.shape[1]
    feat = queries.shape[0]

    def kv_spec(slots_at, j):
        def index(b, ks, vs, lo):
            return ((ks, vs)[slots_at][b + first, j], 0, lo[b + first, j])

        return pl.BlockSpec((1, feat, block_len), index)

    return pl.pallas_call(
        functools.partial(attention_kernel, degree, feat // HD),
        grid_spec=pltpu.PrefetchScalarGridSpec(
            num_scalar_prefetch=3,
            grid=(count,),
            in_specs=[pl.BlockSpec((feat, block_len), lambda b, *_: (0, b + first))]
            + [kv_spec(0, j) for j in range(degree)]
            + [kv_spec(1, j) for j in range(degree)],
            out_specs=pl.BlockSpec((block_len, feat), lambda b, *_: (b, 0)),
        ),
        out_shape=jax.ShapeDtypeStruct((count * block_len, feat), bf16),
        compiler_params=params(),
        cost_estimate=pl.CostEstimate(
            flops=4 * count * block_len * degree * block_len * feat,
            bytes_accessed=2 * count * feat * block_len * (2 * degree + 2),
            transcendentals=count * block_len * degree * block_len * feat // HD,
        ),
        name="attention",
    )(kslot, vslot, local, queries, *([kbuf] * degree), *([vbuf] * degree))


def window_base(starts, i, e):
    return pl.multiple_of((starts[i, e] // 16) * 16, 16)


def stack_hot(starts, rank_ref, i, experts):
    nodes = rank_ref.shape[1]
    place = lax.broadcasted_iota(jnp.int32, (WINDOW, nodes), 0)
    hots = []
    for e in range(experts):
        rank = rank_ref[e : e + 1, :] - window_base(starts, i, e)
        hots.append(jnp.where(place == rank, 1.0, 0.0).astype(bf16))
    return jnp.concatenate(hots, 0)


def one_hot(rank_row, base):
    place = lax.broadcasted_iota(jnp.int32, (WINDOW, rank_row.shape[1]), 0)
    return jnp.where(place == rank_row - base, 1.0, 0.0).astype(bf16)


def extra_windows(starts, i, e):
    left = starts[i + 1, e] - window_base(starts, i, e)
    return jnp.maximum((left + WINDOW - 1) // WINDOW, 1)


def dispatch_kernel(experts, pieces, starts, rank_ref, res_ref, cot_ref, gain_ref, *refs):
    atts, projs, stream_ref, slots_ref = refs[:pieces], refs[pieces : 2 * pieces], refs[-2], refs[-1]
    i = pl.program_id(0)

    @pl.when(i == 0)
    def _():
        slots_ref[...] = jnp.zeros_like(slots_ref)

    acc = res_ref[...].astype(f32)
    projected = jnp.dot(atts[0][...], projs[0][...], preferred_element_type=f32)
    for a, w in zip(atts[1:], projs[1:]):
        projected = projected + jnp.dot(a[...], w[...], preferred_element_type=f32)
    stream = (acc + projected).astype(bf16)
    stream_ref[...] = stream
    wide = stream.astype(f32)
    inverse_rms = lax.rsqrt(jnp.mean(wide * wide, -1, keepdims=True) + norm_eps)
    normed = (wide * inverse_rms * gain_ref[...]).astype(bf16)
    rows = jnp.concatenate([normed, cot_ref[...]], 1)
    hot = stack_hot(starts, rank_ref, i, experts)
    packed = jnp.dot(hot, rows, preferred_element_type=f32).astype(bf16)
    for e in range(experts):
        at = pl.ds(window_base(starts, i, e), WINDOW)
        slots_ref[e, at, :] = slots_ref[e, at, :] + packed[e * WINDOW : (e + 1) * WINDOW]

    for e in range(experts):

        def more(w, carry, e=e):
            base = pl.multiple_of(window_base(starts, i, e) + w * WINDOW, 16)
            got = jnp.dot(one_hot(rank_ref[e : e + 1, :], base), rows, preferred_element_type=f32)
            at = pl.ds(base, WINDOW)
            slots_ref[e, at, :] = slots_ref[e, at, :] + got.astype(bf16)
            return carry

        lax.fori_loop(1, extra_windows(starts, i, e), more, 0)


def dispatch(starts, rank, residual, cotangent, gain, atts, projs, slot_rows, chunk):
    experts, nodes = rank.shape
    width = residual.shape[1]
    rows = lambda w: pl.BlockSpec((chunk, w), lambda i, s: (i, 0))
    whole = lambda a: pl.BlockSpec(a.shape, lambda i, s: (0,) * a.ndim)
    return pl.pallas_call(
        functools.partial(dispatch_kernel, experts, len(atts)),
        grid_spec=pltpu.PrefetchScalarGridSpec(
            num_scalar_prefetch=1,
            grid=(nodes // chunk,),
            in_specs=[
                pl.BlockSpec((experts, chunk), lambda i, s: (0, i)),
                rows(width),
                rows(width),
                whole(gain),
            ]
            + [rows(a.shape[1]) for a in atts]
            + [whole(w) for w in projs],
            out_specs=[rows(width), pl.BlockSpec((experts, slot_rows, 2 * width), lambda i, s: (0, 0, 0))],
        ),
        out_shape=[
            jax.ShapeDtypeStruct((nodes, width), bf16),
            jax.ShapeDtypeStruct((experts, slot_rows, 2 * width), bf16),
        ],
        compiler_params=params(),
        cost_estimate=pl.CostEstimate(
            flops=4 * nodes * experts * WINDOW * 2 * width,
            bytes_accessed=4 * nodes * width * 2 + 2 * experts * slot_rows * width * 2,
            transcendentals=nodes,
        ),
        name="dispatch",
    )(starts, rank, residual, cotangent, gain, *atts, *projs)


def expert_kernel(first, width, counts, ids, slots_ref, win_ref, wout_ref, router_ref, rcol_ref, rows_ref, grad_ref, acc_in, acc_out):
    step = pl.program_id(0)
    e = step + first
    count = counts[e]
    tiles = (count + TILE - 1) // TILE
    slot_rows = slots_ref.shape[1]
    acc_in[...] = jnp.zeros_like(acc_in)
    acc_out[...] = jnp.zeros_like(acc_out)
    w_in = win_ref[0]
    w_out = wout_ref[0]
    lane = lax.broadcasted_iota(jnp.int32, (TILE, router_ref.shape[1]), 1)
    mine = lane == ids[e]
    column = rcol_ref[0]

    def one(t, carry):
        at = pl.ds(pl.multiple_of(t * TILE, TILE), TILE)
        x = slots_ref[0, at, :width]
        cot = slots_ref[0, at, width:]
        cot_wide = cot.astype(f32)
        logits = jnp.dot(x, router_ref[...], preferred_element_type=f32)
        logit = jnp.sum(jnp.where(mine, logits, 0.0), 1, keepdims=True)
        gate = 1.0 / (1.0 + jnp.exp(-logit))
        scaled = (gate * cot_wide).astype(bf16)
        a = jnp.dot(x, w_in, preferred_element_type=f32)
        grad_hidden = contract(scaled, w_out, 1, 1)
        a2 = a * a
        t1 = jnp.tanh(root_two_pi * (a + cubic_term * a * a2))
        half = 0.5 + 0.5 * t1
        hidden = (a * half).astype(bf16)
        slope = half + (0.5 * root_two_pi) * a * (1.0 - t1 * t1) * (1.0 + (3.0 * cubic_term) * a2)
        grad_pre = (grad_hidden * slope).astype(bf16)
        acc_out[...] += contract(hidden, scaled, 0, 0)
        acc_in[...] += contract(x, grad_pre, 0, 0)
        produced = jnp.dot(hidden, w_out, preferred_element_type=f32).astype(bf16).astype(f32)
        grad_rows = contract(grad_pre, w_in, 1, 1).astype(bf16).astype(f32)
        grad_logit = jnp.sum(cot_wide * produced, 1, keepdims=True) * gate * (1.0 - gate)
        rows_ref[0, at, :width] = (gate * produced).astype(bf16)
        rows_ref[0, at, width:] = (grad_rows + grad_logit * column).astype(bf16)
        return carry

    lax.fori_loop(0, tiles, one, 0)

    def blank(t, carry):
        at = pl.ds(pl.multiple_of(t * TILE, TILE), TILE)
        rows_ref[0, at, :] = jnp.zeros((TILE, 2 * width), bf16)
        return carry

    lax.fori_loop(tiles, slot_rows // TILE, blank, 0)
    ff = acc_in.shape[1]
    grad_ref[0, :width, :] = acc_in[...].astype(bf16)
    parts = ff // width
    for j in range(parts):
        grad_ref[0, width:, j * width : (j + 1) * width] = acc_out[j * width : (j + 1) * width, :].astype(bf16)


def experts_step(counts, ids, slots, w_in, w_out, router, columns, first, count):
    experts, slot_rows, double = slots.shape
    width, ff = w_in.shape[1], w_in.shape[2]
    block = lambda *shape: pl.BlockSpec((1,) + shape, lambda i, *_: (i + first, 0, 0))
    fresh = lambda *shape: pl.BlockSpec((1,) + shape, lambda i, *_: (i, 0, 0))
    return pl.pallas_call(
        functools.partial(expert_kernel, first, width),
        grid_spec=pltpu.PrefetchScalarGridSpec(
            num_scalar_prefetch=2,
            grid=(count,),
            in_specs=[
                block(slot_rows, double),
                block(width, ff),
                block(ff, width),
                pl.BlockSpec(router.shape, lambda i, *_: (0, 0)),
                block(1, width),
            ],
            out_specs=[fresh(slot_rows, double), fresh(2 * width, ff)],
            scratch_shapes=[pltpu.VMEM((width, ff), f32), pltpu.VMEM((ff, width), f32)],
        ),
        out_shape=[
            jax.ShapeDtypeStruct((count, slot_rows, double), bf16),
            jax.ShapeDtypeStruct((count, 2 * width, ff), bf16),
        ],
        compiler_params=params(),
        cost_estimate=pl.CostEstimate(
            flops=count * slot_rows * width * ff * 12,
            bytes_accessed=count * (2 * slot_rows * double + 4 * width * ff) * 2,
            transcendentals=count * slot_rows * ff,
        ),
        name="experts",
    )(counts, ids, slots, w_in, w_out, router, columns)


def combined(starts, rank_ref, rows_refs, i, experts):
    hot = stack_hot(starts, rank_ref, i, experts)
    windows = []
    where = []
    for r in rows_refs:
        for j in range(r.shape[0]):
            where.append((r, j))
    for e, (r, j) in enumerate(where):
        windows.append(r[j, pl.ds(window_base(starts, i, e), WINDOW), :])
    total = contract(hot, jnp.concatenate(windows, 0), 0, 0)
    for e, (r, j) in enumerate(where):

        def more(w, acc, e=e, r=r, j=j):
            base = pl.multiple_of(window_base(starts, i, e) + w * WINDOW, 16)
            return acc + contract(one_hot(rank_ref[e : e + 1, :], base), r[j, pl.ds(base, WINDOW), :], 0, 0)

        total = lax.fori_loop(1, extra_windows(starts, i, e), more, total)
    return total


def send_kernel(experts, parts, chunks, starts, order, rank_ref, *refs):
    i = order[pl.program_id(0)]
    refs[parts][...] = combined(starts, rank_ref, refs[:parts], i, experts).astype(bf16)


def home_kernel(experts, parts, got, starts, order, rank_ref, stream_ref, cot_ref, gain_ref, *refs):
    i = order[pl.program_id(0)]
    rows_refs, got_refs = refs[:parts], refs[parts : parts + got]
    layer_ref, grad_ref = refs[parts + got :]
    total = combined(starts, rank_ref, rows_refs, i, experts)
    for g in got_refs:
        total = total + g[...].astype(f32)
    width = stream_ref.shape[1]
    stream = stream_ref[...].astype(f32)
    inverse_rms = lax.rsqrt(jnp.mean(stream * stream, -1, keepdims=True) + norm_eps)
    layer_ref[...] = (stream + total[:, :width]).astype(bf16)
    gained = total[:, width:] * gain_ref[...]
    mean = jnp.mean(stream * gained, -1, keepdims=True)
    grad = cot_ref[...].astype(f32) + inverse_rms * gained - stream * (inverse_rms * inverse_rms * inverse_rms) * mean
    grad_ref[...] = grad.astype(bf16)


def send_home(starts, order, rank, rows_parts, chunk):
    experts = rank.shape[0]
    count = order.shape[0]
    double = rows_parts[0].shape[2]
    return pl.pallas_call(
        functools.partial(send_kernel, experts, len(rows_parts), count),
        grid_spec=pltpu.PrefetchScalarGridSpec(
            num_scalar_prefetch=2,
            grid=(count,),
            in_specs=[pl.BlockSpec((experts, chunk), lambda i, s, o: (0, o[i]))]
            + [pl.BlockSpec(r.shape, lambda i, s, o: (0, 0, 0)) for r in rows_parts],
            out_specs=pl.BlockSpec((chunk, double), lambda i, s, o: (i, 0)),
        ),
        out_shape=jax.ShapeDtypeStruct((count * chunk, double), bf16),
        compiler_params=params(),
        cost_estimate=pl.CostEstimate(
            flops=2 * count * chunk * experts * WINDOW * double,
            bytes_accessed=sum(r.size for r in rows_parts) * 2 + count * chunk * double * 2,
            transcendentals=0,
        ),
        name="send_home",
    )(starts, order, rank, *rows_parts)


def at_home(starts, order, rank, stream, cotangent, gain, rows_parts, got, chunk):
    experts = rank.shape[0]
    count = order.shape[0]
    double = rows_parts[0].shape[2]
    width = double // 2
    fresh = lambda w: pl.BlockSpec((chunk, w), lambda i, s, o: (i, 0))
    return pl.pallas_call(
        functools.partial(home_kernel, experts, len(rows_parts), len(got)),
        grid_spec=pltpu.PrefetchScalarGridSpec(
            num_scalar_prefetch=2,
            grid=(count,),
            in_specs=[
                pl.BlockSpec((experts, chunk), lambda i, s, o: (0, o[i])),
                pl.BlockSpec((chunk, width), lambda i, s, o: (o[i], 0)),
                fresh(width),
                pl.BlockSpec(gain.shape, lambda i, s, o: (0, 0)),
            ]
            + [pl.BlockSpec(r.shape, lambda i, s, o: (0, 0, 0)) for r in rows_parts]
            + [fresh(double) for _ in got],
            out_specs=[fresh(width), fresh(width)],
        ),
        out_shape=[jax.ShapeDtypeStruct((count * chunk, width), bf16)] * 2,
        compiler_params=params(),
        cost_estimate=pl.CostEstimate(
            flops=2 * count * chunk * experts * WINDOW * double,
            bytes_accessed=sum(r.size for r in rows_parts) * 2 + count * chunk * double * 4,
            transcendentals=0,
        ),
        name="at_home",
    )(starts, order, rank, stream, cotangent, gain, *rows_parts, *got)


def line_pairs(seq_count, d):
    lines = seq_count // 4
    return [(z * 4 + r, ((z + d) % lines) * 4 + r) for z in range(lines) for r in range(4)]


def sum_over_seq(grads, seq_count):
    lines = seq_count // 4
    s = lax.axis_index("seq")
    core, column, line = s % 2, (s // 2) % 2, s // 4
    sib = sibling_pairs(seq_count)
    cross = [(i, i ^ 2) for i in range(seq_count)]

    def halve(a, which, pairs):
        h = a.shape[0] // 2
        mine = lax.dynamic_slice_in_dim(a, which * h, h, 0)
        other = lax.dynamic_slice_in_dim(a, (1 - which) * h, h, 0)
        got = lax.ppermute(other, "seq", pairs)
        return (mine.astype(f32) + got.astype(f32)).astype(bf16)

    a = halve(halve(grads, core, sib), column, cross)
    q = a.shape[0] // lines
    total = lax.dynamic_slice_in_dim(a, line * q, q, 0).astype(f32)
    for d in range(1, lines):
        part = lax.dynamic_slice_in_dim(a, lax.rem(line + d, lines) * q, q, 0)
        total = total + lax.ppermute(part, "seq", line_pairs(seq_count, d)).astype(f32)
    shard = total.astype(bf16)

    out = jnp.zeros((q * lines,) + a.shape[1:], bf16)
    out = lax.dynamic_update_slice_in_dim(out, shard, line * q, 0)
    for d in range(1, lines):
        got = lax.ppermute(shard, "seq", line_pairs(seq_count, d))
        out = lax.dynamic_update_slice_in_dim(out, got, lax.rem(line - d + lines, lines) * q, 0)

    def double(a, which, pairs):
        got = lax.ppermute(a, "seq", pairs)
        return jnp.where(which == 0, jnp.concatenate([a, got], 0), jnp.concatenate([got, a], 0))

    return double(double(out, column, cross), core, sib)


def shards(
    query_cols,
    key_cols,
    value_cols,
    block_list,
    residual,
    out_proj,
    norm_gain,
    router_weight,
    expert_ids,
    expert_in,
    expert_out,
    cotangent,
):
    seq_count = lax.axis_size("seq")
    exp_count = lax.axis_size("expert")
    me = lax.axis_index("expert")
    feat, nodes = query_cols.shape
    blk_seq, degree = block_list.shape
    block_len = nodes // blk_seq
    tok_dev, width = residual.shape
    expert_total = router_weight.shape[1]
    experts = expert_in.shape[0]
    ff = expert_in.shape[2]
    topk = expert_ids.shape[1]
    chunk = min(256, tok_dev)
    capacity = 2 * tok_dev * topk // expert_total * exp_count
    slot_rows = capacity + WINDOW

    kbuf, vbuf = ring_gather(key_cols, value_cols, seq_count)
    places = block_places(block_list, blk_seq, seq_count)

    residual_all = gather_expert_axis(residual, exp_count)
    cotangent_all = gather_expert_axis(cotangent, exp_count)
    ids_all = gather_expert_axis(expert_ids.T, exp_count, 1)
    gain = norm_gain.reshape(1, width)
    local_ids = me * experts + jnp.arange(experts, dtype=jnp.int32)
    hot = jnp.sum((ids_all[None, :, :] == local_ids[:, None, None]).astype(jnp.int32), 1)
    running = jnp.cumsum(hot, 1)
    rank = jnp.where(hot > 0, running - 1, -(1 << 20))
    ends = running[:, chunk - 1 :: chunk]
    starts = jnp.concatenate([jnp.zeros((experts, 1), jnp.int32), ends], 1).T
    counts = running[:, -1]
    router = jnp.pad(router_weight, ((0, 0), (0, -expert_total % 128)))
    columns = lax.dynamic_slice_in_dim(router_weight.T, me * experts, experts, 0).astype(f32).reshape(experts, 1, width)
    projs = [
        lax.dynamic_slice_in_dim(out_proj, lax.rem(me + exp_count - d, exp_count) * feat, feat, 0)
        for d in range(exp_count)
    ]
    chunks_dev = tok_dev // chunk
    in_chunk = jnp.arange(chunks_dev, dtype=jnp.int32)
    own_order = me * chunks_dev + in_chunk

    calls = 2 if blk_seq % 2 == 0 else 1
    per_call = blk_seq // calls
    pieces = [[] for _ in range(exp_count)]
    for c in range(calls):
        part = attention(query_cols, kbuf, vbuf, places, c * per_call, per_call, block_len)
        pieces[0].append(part)
        for d in range(1, exp_count):
            pieces[d].append(lax.ppermute(part, "expert", shift_pairs(exp_count, d)))
    atts = [jnp.concatenate(p, 0) for p in pieces]

    stream, slots = dispatch(starts, rank, residual_all, cotangent_all, gain, atts, projs, slot_rows, chunk)

    groups = 2 if experts % 2 == 0 else 1
    per_group = experts // groups
    rows_parts, sums = [], []
    for g in range(groups):
        rows, grads = experts_step(counts, local_ids, slots, expert_in, expert_out, router, columns, g * per_group, per_group)
        rows_parts.append(rows)
        sums.append(sum_over_seq(grads.reshape(per_group * 2 * width, ff), seq_count).reshape(per_group, 2 * width, ff))

    got = []
    for d in range(1, exp_count):
        target = lax.rem(me + d, exp_count)
        partial = send_home(starts, target * chunks_dev + in_chunk, rank, rows_parts, chunk)
        got.append(lax.ppermute(partial, "expert", shift_pairs(exp_count, d)))
    layer_out, grad_stream = at_home(starts, own_order, rank, stream, cotangent, gain, rows_parts, got, chunk)

    total = jnp.concatenate(sums, 0).astype(f32)
    grad_w_in = total[:, :width, :]
    grad_w_out = jnp.concatenate(
        [total[:, width:, j * width : (j + 1) * width] for j in range(ff // width)], 1
    )
    return layer_out, grad_stream, grad_w_in, grad_w_out


def solution(mesh):
    return jax.shard_map(
        shards,
        mesh=mesh,
        in_specs=(
            P("expert", "seq"),
            P("expert", "seq"),
            P("expert", "seq"),
            P("seq", None),
            P(("seq", "expert"), None),
            P(),
            P(),
            P(),
            P(("seq", "expert"), None),
            P("expert", None, None),
            P("expert", None, None),
            P(("seq", "expert"), None),
        ),
        out_specs=(
            P(("seq", "expert"), None),
            P(("seq", "expert"), None),
            P("expert", None, None),
            P("expert", None, None),
        ),
        check_vma=False,
    )
```

```python
import functools
import math

import jax
import jax.numpy as jnp
from jax import lax
from jax.experimental import pallas as pl
from jax.experimental.pallas import tpu as pltpu
from jax.sharding import PartitionSpec as P

HD = 32
WINDOW = 128
TILE = 128

norm_eps = 1e-05
root_two_pi = 0.7978845608028654
cubic_term = 0.044715

bf16 = jnp.bfloat16
f32 = jnp.float32
VMEM_BYTES = 48 * 1024 * 1024


def params(**kw):
    return pltpu.CompilerParams(vmem_limit_bytes=VMEM_BYTES, **kw)


def contract(a, b, da, db):
    return lax.dot_general(a, b, (((da,), (db,)), ((), ())), preferred_element_type=f32)


def ring_order(seq_count):
    rows = max(1, seq_count // 4)
    if seq_count % 4:
        return list(range(seq_count // 2))
    return [2 * z for z in range(rows)] + [2 * z + 1 for z in reversed(range(rows))]


def ring_pairs(seq_count, step):
    order = ring_order(seq_count)
    n = len(order)
    return [(2 * order[i] + c, 2 * order[(i + step) % n] + c) for i in range(n) for c in range(2)]


def sibling_pairs(seq_count):
    return [(s, s ^ 1) for s in range(seq_count)]


def shift_pairs(count, d):
    return [(i, (i + d) % count) for i in range(count)]


def gather_expert_axis(x, exp_count, axis=0):
    me = lax.axis_index("expert")
    size = x.shape[axis]
    shape = list(x.shape)
    shape[axis] = size * exp_count
    out = jnp.zeros(shape, x.dtype)
    out = lax.dynamic_update_slice_in_dim(out, x, me * size, axis)
    for d in range(1, exp_count):
        got = lax.ppermute(x, "expert", shift_pairs(exp_count, d))
        out = lax.dynamic_update_slice_in_dim(out, got, lax.rem(me + exp_count - d, exp_count) * size, axis)
    return out


def ring_gather(keys, values, seq_count):
    n = seq_count // 2
    fwd, bwd, sib = ring_pairs(seq_count, 1), ring_pairs(seq_count, -1), sibling_pairs(seq_count)
    k, v = keys, values
    own, other = ([], []), ([], [])
    for t in range(n):
        if t > 0:
            k = lax.ppermute(k, "seq", fwd)
            v = lax.ppermute(v, "seq", bwd)
        own[0].append(k)
        own[1].append(v)
        other[0].append(lax.ppermute(k, "seq", sib))
        other[1].append(lax.ppermute(v, "seq", sib))
    return own[0] + other[0], own[1] + other[1]


def sorted_entries(slot, slots):
    count = slot.shape[-1]
    at = jnp.arange(count, dtype=jnp.int32)
    before = (slot[:, None, :] < slot[:, :, None]) | ((slot[:, None, :] == slot[:, :, None]) & (at[None, None, :] < at[None, :, None]))
    rank = jnp.sum(before.astype(jnp.int32), 2)
    order = jnp.sum(jnp.where(rank[:, None, :] == at[None, :, None], at[None, None, :], 0), 2)
    begin = jnp.sum((slot[:, None, :] < jnp.arange(slots + 1, dtype=jnp.int32)[None, :, None]).astype(jnp.int32), 2)
    return order, begin


def block_tables(block_list, blk_seq, seq_count, calls):
    order = ring_order(seq_count)
    n = len(order)
    inverse = [0] * n
    for i, chip in enumerate(order):
        inverse[chip] = i
    inverse = jnp.asarray(inverse, jnp.int32)
    me = lax.axis_index("seq")
    place = inverse[me // 2]
    owner = block_list // blk_seq
    local = (block_list % blk_seq).reshape(calls, -1)
    other = inverse[owner // 2]
    flag = ((owner ^ me) & 1) * n
    kslot = (flag + lax.rem(place - other + n, n)).reshape(calls, -1)
    vslot = (flag + lax.rem(other - place + n, n)).reshape(calls, -1)
    return (local,) + sorted_entries(kslot, 2 * n) + sorted_entries(vslot, 2 * n)


def attention_kernel(degree, heads, sources, local, korder, kbegin, vorder, vbegin, q_ref, *refs):
    k_refs, v_refs = refs[:sources], refs[sources : 2 * sources]
    out_ref, k_all, v_all, sems = refs[2 * sources :]
    block_len = k_all.shape[2] // degree

    def fetch(source, dest, order, begin, s, sem):
        def one(r, carry):
            e = order[r]
            at = pl.ds(pl.multiple_of(local[e] * block_len, block_len), block_len)
            to = pl.ds(pl.multiple_of(lax.rem(e, degree) * block_len, block_len), block_len)
            pltpu.make_async_copy(source.at[:, at], dest.at[lax.div(e, degree), :, to], sem).start()
            return carry

        lax.fori_loop(begin[s], begin[s + 1], one, 0)

    for s in range(sources):
        fetch(k_refs[s], k_all, korder, kbegin, s, sems.at[0])
    for s in range(sources):
        fetch(v_refs[s], v_all, vorder, vbegin, s, sems.at[1])
    pltpu.make_async_copy(k_all, k_all, sems.at[0]).wait()
    pltpu.make_async_copy(v_all, v_all, sems.at[1]).wait()
    factor = math.log2(math.e) / math.sqrt(HD)

    def one_block(b, carry):
        nodes = pl.ds(pl.multiple_of(b * block_len, block_len), block_len)
        cols = []
        for h in range(heads):
            rows = slice(h * HD, (h + 1) * HD)
            scores = contract(k_all[b, rows, :], q_ref[rows, nodes], 0, 0)
            top = jnp.max(scores, 0, keepdims=True)
            probs = jnp.exp2((scores - top) * factor)
            total = jnp.sum(probs, 0, keepdims=True)
            out = jnp.dot(v_all[b, rows, :], probs.astype(bf16), preferred_element_type=f32)
            cols.append(out / total)
        out_ref[nodes, :] = jnp.concatenate(cols, 0).T.astype(bf16)
        return carry

    lax.fori_loop(0, k_all.shape[0], one_block, 0)


def attention(queries, keys, values, tables, call, count, block_len, degree):
    feat = queries.shape[0]
    return pl.pallas_call(
        functools.partial(attention_kernel, degree, feat // HD, len(keys)),
        grid_spec=pltpu.PrefetchScalarGridSpec(
            num_scalar_prefetch=5,
            grid=(1,),
            in_specs=[pl.BlockSpec((feat, count * block_len), lambda i, *_: (0, call))]
            + [pl.BlockSpec(memory_space=pl.ANY)] * (2 * len(keys)),
            out_specs=pl.BlockSpec((count * block_len, feat), lambda i, *_: (0, 0)),
            scratch_shapes=[pltpu.VMEM((count, feat, degree * block_len), bf16)] * 2 + [pltpu.SemaphoreType.DMA((2,))],
        ),
        out_shape=jax.ShapeDtypeStruct((count * block_len, feat), bf16),
        compiler_params=params(),
        cost_estimate=pl.CostEstimate(
            flops=4 * count * block_len * degree * block_len * feat,
            bytes_accessed=2 * count * feat * block_len * (2 * degree + 2),
            transcendentals=count * block_len * degree * block_len * feat // HD,
        ),
        name="attention",
    )(*[t[call] for t in tables], queries, *keys, *values)


def window_base(starts, i, e):
    return pl.multiple_of((starts[i, e] // 16) * 16, 16)


def stack_hot(starts, rank_ref, i, experts):
    nodes = rank_ref.shape[1]
    place = lax.broadcasted_iota(jnp.int32, (WINDOW, nodes), 0)
    hots = []
    for e in range(experts):
        rank = rank_ref[e : e + 1, :] - window_base(starts, i, e)
        hots.append(jnp.where(place == rank, 1.0, 0.0).astype(bf16))
    return jnp.concatenate(hots, 0)


def one_hot(rank_row, base):
    place = lax.broadcasted_iota(jnp.int32, (WINDOW, rank_row.shape[1]), 0)
    return jnp.where(place == rank_row - base, 1.0, 0.0).astype(bf16)


def extra_windows(starts, i, e):
    left = starts[i + 1, e] - window_base(starts, i, e)
    return jnp.maximum((left + WINDOW - 1) // WINDOW, 1)


def dispatch_kernel(experts, pieces, starts, rank_ref, res_ref, cot_ref, gain_ref, *refs):
    atts, projs, stream_ref, slots_ref = refs[:pieces], refs[pieces : 2 * pieces], refs[-2], refs[-1]
    i = pl.program_id(0)

    @pl.when(i == 0)
    def _():
        slots_ref[...] = jnp.zeros_like(slots_ref)

    acc = res_ref[...].astype(f32)
    projected = jnp.dot(atts[0][...], projs[0][...], preferred_element_type=f32)
    for a, w in zip(atts[1:], projs[1:]):
        projected = projected + jnp.dot(a[...], w[...], preferred_element_type=f32)
    stream = (acc + projected).astype(bf16)
    stream_ref[...] = stream
    wide = stream.astype(f32)
    inverse_rms = lax.rsqrt(jnp.mean(wide * wide, -1, keepdims=True) + norm_eps)
    normed = (wide * inverse_rms * gain_ref[...]).astype(bf16)
    rows = jnp.concatenate([normed, cot_ref[...]], 1)
    hot = stack_hot(starts, rank_ref, i, experts)
    packed = jnp.dot(hot, rows, preferred_element_type=f32).astype(bf16)
    for e in range(experts):
        at = pl.ds(window_base(starts, i, e), WINDOW)
        slots_ref[e, at, :] = slots_ref[e, at, :] + packed[e * WINDOW : (e + 1) * WINDOW]

    for e in range(experts):

        def more(w, carry, e=e):
            base = pl.multiple_of(window_base(starts, i, e) + w * WINDOW, 16)
            got = jnp.dot(one_hot(rank_ref[e : e + 1, :], base), rows, preferred_element_type=f32)
            at = pl.ds(base, WINDOW)
            slots_ref[e, at, :] = slots_ref[e, at, :] + got.astype(bf16)
            return carry

        lax.fori_loop(1, extra_windows(starts, i, e), more, 0)


def dispatch(starts, rank, residual, cotangent, gain, atts, projs, slot_rows, chunk):
    experts, nodes = rank.shape
    width = residual.shape[1]
    rows = lambda w: pl.BlockSpec((chunk, w), lambda i, s: (i, 0))
    whole = lambda a: pl.BlockSpec(a.shape, lambda i, s: (0,) * a.ndim)
    return pl.pallas_call(
        functools.partial(dispatch_kernel, experts, len(atts)),
        grid_spec=pltpu.PrefetchScalarGridSpec(
            num_scalar_prefetch=1,
            grid=(nodes // chunk,),
            in_specs=[
                pl.BlockSpec((experts, chunk), lambda i, s: (0, i)),
                rows(width),
                rows(width),
                whole(gain),
            ]
            + [rows(a.shape[1]) for a in atts]
            + [whole(w) for w in projs],
            out_specs=[rows(width), pl.BlockSpec((experts, slot_rows, 2 * width), lambda i, s: (0, 0, 0))],
        ),
        out_shape=[
            jax.ShapeDtypeStruct((nodes, width), bf16),
            jax.ShapeDtypeStruct((experts, slot_rows, 2 * width), bf16),
        ],
        compiler_params=params(),
        cost_estimate=pl.CostEstimate(
            flops=4 * nodes * experts * WINDOW * 2 * width,
            bytes_accessed=4 * nodes * width * 2 + 2 * experts * slot_rows * width * 2,
            transcendentals=nodes,
        ),
        name="dispatch",
    )(starts, rank, residual, cotangent, gain, *atts, *projs)


def expert_kernel(first, width, counts, ids, slots_ref, win_ref, wout_ref, router_ref, rcol_ref, rows_ref, grad_ref, acc_in, acc_out):
    step = pl.program_id(0)
    e = step + first
    count = counts[e]
    tiles = (count + TILE - 1) // TILE
    slot_rows = slots_ref.shape[1]
    acc_in[...] = jnp.zeros_like(acc_in)
    acc_out[...] = jnp.zeros_like(acc_out)
    w_in = win_ref[0]
    w_out = wout_ref[0]
    lane = lax.broadcasted_iota(jnp.int32, (TILE, router_ref.shape[1]), 1)
    mine = lane == ids[e]
    column = rcol_ref[0]

    def one(t, carry):
        at = pl.ds(pl.multiple_of(t * TILE, TILE), TILE)
        x = slots_ref[0, at, :width]
        cot = slots_ref[0, at, width:]
        cot_wide = cot.astype(f32)
        logits = jnp.dot(x, router_ref[...], preferred_element_type=f32)
        logit = jnp.sum(jnp.where(mine, logits, 0.0), 1, keepdims=True)
        gate = 1.0 / (1.0 + jnp.exp(-logit))
        scaled = (gate * cot_wide).astype(bf16)
        a = jnp.dot(x, w_in, preferred_element_type=f32)
        grad_hidden = contract(scaled, w_out, 1, 1)
        a2 = a * a
        t1 = jnp.tanh(root_two_pi * (a + cubic_term * a * a2))
        half = 0.5 + 0.5 * t1
        hidden = (a * half).astype(bf16)
        slope = half + (0.5 * root_two_pi) * a * (1.0 - t1 * t1) * (1.0 + (3.0 * cubic_term) * a2)
        grad_pre = (grad_hidden * slope).astype(bf16)
        acc_out[...] += contract(hidden, scaled, 0, 0)
        acc_in[...] += contract(x, grad_pre, 0, 0)
        produced = jnp.dot(hidden, w_out, preferred_element_type=f32).astype(bf16).astype(f32)
        grad_rows = contract(grad_pre, w_in, 1, 1).astype(bf16).astype(f32)
        grad_logit = jnp.sum(cot_wide * produced, 1, keepdims=True) * gate * (1.0 - gate)
        rows_ref[0, at, :width] = (gate * produced).astype(bf16)
        rows_ref[0, at, width:] = (grad_rows + grad_logit * column).astype(bf16)
        return carry

    lax.fori_loop(0, tiles, one, 0)

    def blank(t, carry):
        at = pl.ds(pl.multiple_of(t * TILE, TILE), TILE)
        rows_ref[0, at, :] = jnp.zeros((TILE, 2 * width), bf16)
        return carry

    lax.fori_loop(tiles, slot_rows // TILE, blank, 0)
    ff = acc_in.shape[1]
    grad_ref[0, :width, :] = acc_in[...].astype(bf16)
    parts = ff // width
    for j in range(parts):
        grad_ref[0, width:, j * width : (j + 1) * width] = acc_out[j * width : (j + 1) * width, :].astype(bf16)


def experts_step(counts, ids, slots, w_in, w_out, router, columns, first, count):
    experts, slot_rows, double = slots.shape
    width, ff = w_in.shape[1], w_in.shape[2]
    block = lambda *shape: pl.BlockSpec((1,) + shape, lambda i, *_: (i + first, 0, 0))
    fresh = lambda *shape: pl.BlockSpec((1,) + shape, lambda i, *_: (i, 0, 0))
    return pl.pallas_call(
        functools.partial(expert_kernel, first, width),
        grid_spec=pltpu.PrefetchScalarGridSpec(
            num_scalar_prefetch=2,
            grid=(count,),
            in_specs=[
                block(slot_rows, double),
                block(width, ff),
                block(ff, width),
                pl.BlockSpec(router.shape, lambda i, *_: (0, 0)),
                block(1, width),
            ],
            out_specs=[fresh(slot_rows, double), fresh(2 * width, ff)],
            scratch_shapes=[pltpu.VMEM((width, ff), f32), pltpu.VMEM((ff, width), f32)],
        ),
        out_shape=[
            jax.ShapeDtypeStruct((count, slot_rows, double), bf16),
            jax.ShapeDtypeStruct((count, 2 * width, ff), bf16),
        ],
        compiler_params=params(),
        cost_estimate=pl.CostEstimate(
            flops=count * slot_rows * width * ff * 12,
            bytes_accessed=count * (2 * slot_rows * double + 4 * width * ff) * 2,
            transcendentals=count * slot_rows * ff,
        ),
        name="experts",
    )(counts, ids, slots, w_in, w_out, router, columns)


def combined(starts, rank_ref, rows_refs, i, experts):
    hot = stack_hot(starts, rank_ref, i, experts)
    windows = []
    where = []
    for r in rows_refs:
        for j in range(r.shape[0]):
            where.append((r, j))
    for e, (r, j) in enumerate(where):
        windows.append(r[j, pl.ds(window_base(starts, i, e), WINDOW), :])
    total = contract(hot, jnp.concatenate(windows, 0), 0, 0)
    for e, (r, j) in enumerate(where):

        def more(w, acc, e=e, r=r, j=j):
            base = pl.multiple_of(window_base(starts, i, e) + w * WINDOW, 16)
            return acc + contract(one_hot(rank_ref[e : e + 1, :], base), r[j, pl.ds(base, WINDOW), :], 0, 0)

        total = lax.fori_loop(1, extra_windows(starts, i, e), more, total)
    return total


def send_kernel(experts, parts, chunks, starts, order, rank_ref, *refs):
    i = order[pl.program_id(0)]
    refs[parts][...] = combined(starts, rank_ref, refs[:parts], i, experts).astype(bf16)


def home_kernel(experts, parts, got, starts, order, rank_ref, stream_ref, cot_ref, gain_ref, *refs):
    i = order[pl.program_id(0)]
    rows_refs, got_refs = refs[:parts], refs[parts : parts + got]
    layer_ref, grad_ref = refs[parts + got :]
    total = combined(starts, rank_ref, rows_refs, i, experts)
    for g in got_refs:
        total = total + g[...].astype(f32)
    width = stream_ref.shape[1]
    stream = stream_ref[...].astype(f32)
    inverse_rms = lax.rsqrt(jnp.mean(stream * stream, -1, keepdims=True) + norm_eps)
    layer_ref[...] = (stream + total[:, :width]).astype(bf16)
    gained = total[:, width:] * gain_ref[...]
    mean = jnp.mean(stream * gained, -1, keepdims=True)
    grad = cot_ref[...].astype(f32) + inverse_rms * gained - stream * (inverse_rms * inverse_rms * inverse_rms) * mean
    grad_ref[...] = grad.astype(bf16)


def send_home(starts, order, rank, rows_parts, chunk):
    experts = rank.shape[0]
    count = order.shape[0]
    double = rows_parts[0].shape[2]
    return pl.pallas_call(
        functools.partial(send_kernel, experts, len(rows_parts), count),
        grid_spec=pltpu.PrefetchScalarGridSpec(
            num_scalar_prefetch=2,
            grid=(count,),
            in_specs=[pl.BlockSpec((experts, chunk), lambda i, s, o: (0, o[i]))]
            + [pl.BlockSpec(r.shape, lambda i, s, o: (0, 0, 0)) for r in rows_parts],
            out_specs=pl.BlockSpec((chunk, double), lambda i, s, o: (i, 0)),
        ),
        out_shape=jax.ShapeDtypeStruct((count * chunk, double), bf16),
        compiler_params=params(),
        cost_estimate=pl.CostEstimate(
            flops=2 * count * chunk * experts * WINDOW * double,
            bytes_accessed=sum(r.size for r in rows_parts) * 2 + count * chunk * double * 2,
            transcendentals=0,
        ),
        name="send_home",
    )(starts, order, rank, *rows_parts)


def at_home(starts, order, rank, stream, cotangent, gain, rows_parts, got, chunk):
    experts = rank.shape[0]
    count = order.shape[0]
    double = rows_parts[0].shape[2]
    width = double // 2
    fresh = lambda w: pl.BlockSpec((chunk, w), lambda i, s, o: (i, 0))
    return pl.pallas_call(
        functools.partial(home_kernel, experts, len(rows_parts), len(got)),
        grid_spec=pltpu.PrefetchScalarGridSpec(
            num_scalar_prefetch=2,
            grid=(count,),
            in_specs=[
                pl.BlockSpec((experts, chunk), lambda i, s, o: (0, o[i])),
                pl.BlockSpec((chunk, width), lambda i, s, o: (o[i], 0)),
                fresh(width),
                pl.BlockSpec(gain.shape, lambda i, s, o: (0, 0)),
            ]
            + [pl.BlockSpec(r.shape, lambda i, s, o: (0, 0, 0)) for r in rows_parts]
            + [fresh(double) for _ in got],
            out_specs=[fresh(width), fresh(width)],
        ),
        out_shape=[jax.ShapeDtypeStruct((count * chunk, width), bf16)] * 2,
        compiler_params=params(),
        cost_estimate=pl.CostEstimate(
            flops=2 * count * chunk * experts * WINDOW * double,
            bytes_accessed=sum(r.size for r in rows_parts) * 2 + count * chunk * double * 4,
            transcendentals=0,
        ),
        name="at_home",
    )(starts, order, rank, stream, cotangent, gain, *rows_parts, *got)


def line_pairs(seq_count, d):
    lines = seq_count // 4
    return [(z * 4 + r, ((z + d) % lines) * 4 + r) for z in range(lines) for r in range(4)]


def sum_over_seq(grads, seq_count):
    lines = seq_count // 4
    s = lax.axis_index("seq")
    core, column, line = s % 2, (s // 2) % 2, s // 4
    sib = sibling_pairs(seq_count)
    cross = [(i, i ^ 2) for i in range(seq_count)]

    def halve(a, which, pairs):
        h = a.shape[0] // 2
        mine = lax.dynamic_slice_in_dim(a, which * h, h, 0)
        other = lax.dynamic_slice_in_dim(a, (1 - which) * h, h, 0)
        got = lax.ppermute(other, "seq", pairs)
        return (mine.astype(f32) + got.astype(f32)).astype(bf16)

    a = halve(halve(grads, core, sib), column, cross)
    q = a.shape[0] // lines
    total = lax.dynamic_slice_in_dim(a, line * q, q, 0).astype(f32)
    for d in range(1, lines):
        part = lax.dynamic_slice_in_dim(a, lax.rem(line + d, lines) * q, q, 0)
        total = total + lax.ppermute(part, "seq", line_pairs(seq_count, d)).astype(f32)
    shard = total.astype(bf16)

    out = jnp.zeros((q * lines,) + a.shape[1:], bf16)
    out = lax.dynamic_update_slice_in_dim(out, shard, line * q, 0)
    for d in range(1, lines):
        got = lax.ppermute(shard, "seq", line_pairs(seq_count, d))
        out = lax.dynamic_update_slice_in_dim(out, got, lax.rem(line - d + lines, lines) * q, 0)

    def double(a, which, pairs):
        got = lax.ppermute(a, "seq", pairs)
        return jnp.where(which == 0, jnp.concatenate([a, got], 0), jnp.concatenate([got, a], 0))

    return double(double(out, column, cross), core, sib)


def shards(
    query_cols,
    key_cols,
    value_cols,
    block_list,
    residual,
    out_proj,
    norm_gain,
    router_weight,
    expert_ids,
    expert_in,
    expert_out,
    cotangent,
):
    seq_count = lax.axis_size("seq")
    exp_count = lax.axis_size("expert")
    me = lax.axis_index("expert")
    feat, nodes = query_cols.shape
    blk_seq, degree = block_list.shape
    block_len = nodes // blk_seq
    tok_dev, width = residual.shape
    expert_total = router_weight.shape[1]
    experts = expert_in.shape[0]
    ff = expert_in.shape[2]
    topk = expert_ids.shape[1]
    chunk = min(256, tok_dev)
    capacity = 2 * tok_dev * topk // expert_total * exp_count
    slot_rows = capacity + WINDOW

    calls = 2 if blk_seq % 2 == 0 else 1
    keys, values = ring_gather(key_cols, value_cols, seq_count)
    tables = block_tables(block_list, blk_seq, seq_count, calls)

    residual_all = gather_expert_axis(residual, exp_count)
    cotangent_all = gather_expert_axis(cotangent, exp_count)
    ids_all = gather_expert_axis(expert_ids.T, exp_count, 1)
    gain = norm_gain.reshape(1, width)
    local_ids = me * experts + jnp.arange(experts, dtype=jnp.int32)
    hot = jnp.sum((ids_all[None, :, :] == local_ids[:, None, None]).astype(jnp.int32), 1)
    running = jnp.cumsum(hot, 1)
    rank = jnp.where(hot > 0, running - 1, -(1 << 20))
    ends = running[:, chunk - 1 :: chunk]
    starts = jnp.concatenate([jnp.zeros((experts, 1), jnp.int32), ends], 1).T
    counts = running[:, -1]
    router = jnp.pad(router_weight, ((0, 0), (0, -expert_total % 128)))
    columns = lax.dynamic_slice_in_dim(router_weight.T, me * experts, experts, 0).astype(f32).reshape(experts, 1, width)
    projs = [
        lax.dynamic_slice_in_dim(out_proj, lax.rem(me + exp_count - d, exp_count) * feat, feat, 0)
        for d in range(exp_count)
    ]
    chunks_dev = tok_dev // chunk
    in_chunk = jnp.arange(chunks_dev, dtype=jnp.int32)
    own_order = me * chunks_dev + in_chunk

    per_call = blk_seq // calls
    pieces = [[] for _ in range(exp_count)]
    for c in range(calls):
        part = attention(query_cols, keys, values, tables, c, per_call, block_len, degree)
        pieces[0].append(part)
        for d in range(1, exp_count):
            pieces[d].append(lax.ppermute(part, "expert", shift_pairs(exp_count, d)))
    atts = [jnp.concatenate(p, 0) for p in pieces]

    stream, slots = dispatch(starts, rank, residual_all, cotangent_all, gain, atts, projs, slot_rows, chunk)

    groups = 2 if experts % 2 == 0 else 1
    per_group = experts // groups
    rows_parts, sums = [], []
    for g in range(groups):
        rows, grads = experts_step(counts, local_ids, slots, expert_in, expert_out, router, columns, g * per_group, per_group)
        rows_parts.append(rows)
        sums.append(sum_over_seq(grads.reshape(per_group * 2 * width, ff), seq_count).reshape(per_group, 2 * width, ff))

    got = []
    for d in range(1, exp_count):
        target = lax.rem(me + d, exp_count)
        partial = send_home(starts, target * chunks_dev + in_chunk, rank, rows_parts, chunk)
        got.append(lax.ppermute(partial, "expert", shift_pairs(exp_count, d)))
    layer_out, grad_stream = at_home(starts, own_order, rank, stream, cotangent, gain, rows_parts, got, chunk)

    total = jnp.concatenate(sums, 0).astype(f32)
    grad_w_in = total[:, :width, :]
    grad_w_out = jnp.concatenate(
        [total[:, width:, j * width : (j + 1) * width] for j in range(ff // width)], 1
    )
    return layer_out, grad_stream, grad_w_in, grad_w_out


def solution(mesh):
    return jax.shard_map(
        shards,
        mesh=mesh,
        in_specs=(
            P("expert", "seq"),
            P("expert", "seq"),
            P("expert", "seq"),
            P("seq", None),
            P(("seq", "expert"), None),
            P(),
            P(),
            P(),
            P(("seq", "expert"), None),
            P("expert", None, None),
            P("expert", None, None),
            P(("seq", "expert"), None),
        ),
        out_specs=(
            P(("seq", "expert"), None),
            P(("seq", "expert"), None),
            P("expert", None, None),
            P("expert", None, None),
        ),
        check_vma=False,
    )
```

```python
import functools
import math

import jax
import jax.numpy as jnp
from jax import lax
from jax.experimental import pallas as pl
from jax.experimental.pallas import tpu as pltpu
from jax.sharding import PartitionSpec as P

HD = 32
WINDOW = 128
TILE = 256
EAGER = 32

norm_eps = 1e-05
root_two_pi = 0.7978845608028654
cubic_term = 0.044715

bf16 = jnp.bfloat16
f32 = jnp.float32
VMEM_BYTES = 48 * 1024 * 1024


def params(**kw):
    return pltpu.CompilerParams(vmem_limit_bytes=VMEM_BYTES, **kw)


def contract(a, b, da, db):
    return lax.dot_general(a, b, (((da,), (db,)), ((), ())), preferred_element_type=f32)


def ring_order(seq_count):
    rows = max(1, seq_count // 4)
    if seq_count % 4:
        return list(range(seq_count // 2))
    return [2 * z for z in range(rows)] + [2 * z + 1 for z in reversed(range(rows))]


def ring_pairs(seq_count, step):
    order = ring_order(seq_count)
    n = len(order)
    return [(2 * order[i] + c, 2 * order[(i + step) % n] + c) for i in range(n) for c in range(2)]


def sibling_pairs(seq_count):
    return [(s, s ^ 1) for s in range(seq_count)]


def shift_pairs(count, d):
    return [(i, (i + d) % count) for i in range(count)]


def gather_expert_axis(x, exp_count, axis=0):
    me = lax.axis_index("expert")
    size = x.shape[axis]
    shape = list(x.shape)
    shape[axis] = size * exp_count
    out = jnp.zeros(shape, x.dtype)
    out = lax.dynamic_update_slice_in_dim(out, x, me * size, axis)
    for d in range(1, exp_count):
        got = lax.ppermute(x, "expert", shift_pairs(exp_count, d))
        out = lax.dynamic_update_slice_in_dim(out, got, lax.rem(me + exp_count - d, exp_count) * size, axis)
    return out


def ring_gather(keys, values, seq_count):
    n = seq_count // 2
    fwd, bwd, sib = ring_pairs(seq_count, 1), ring_pairs(seq_count, -1), sibling_pairs(seq_count)
    k, v = keys, values
    own, other = ([], []), ([], [])
    for t in range(n):
        if t > 0:
            k = lax.ppermute(k, "seq", fwd)
            v = lax.ppermute(v, "seq", bwd)
        own[0].append(k)
        own[1].append(v)
        other[0].append(lax.ppermute(k, "seq", sib))
        other[1].append(lax.ppermute(v, "seq", sib))
    return own[0] + other[0], own[1] + other[1]


def sorted_entries(slot, slots):
    count = slot.shape[-1]
    at = jnp.arange(count, dtype=jnp.int32)
    before = (slot[:, None, :] < slot[:, :, None]) | ((slot[:, None, :] == slot[:, :, None]) & (at[None, None, :] < at[None, :, None]))
    rank = jnp.sum(before.astype(jnp.int32), 2)
    order = jnp.sum(jnp.where(rank[:, None, :] == at[None, :, None], at[None, None, :], 0), 2)
    begin = jnp.sum((slot[:, None, :] < jnp.arange(slots + 1, dtype=jnp.int32)[None, :, None]).astype(jnp.int32), 2)
    return order, begin


def block_tables(block_list, blk_seq, seq_count, calls):
    order = ring_order(seq_count)
    n = len(order)
    inverse = [0] * n
    for i, chip in enumerate(order):
        inverse[chip] = i
    inverse = jnp.asarray(inverse, jnp.int32)
    me = lax.axis_index("seq")
    place = inverse[me // 2]
    owner = block_list // blk_seq
    local = (block_list % blk_seq).reshape(calls, -1)
    other = inverse[owner // 2]
    flag = ((owner ^ me) & 1) * n
    kslot = (flag + lax.rem(place - other + n, n)).reshape(calls, -1)
    vslot = (flag + lax.rem(other - place + n, n)).reshape(calls, -1)
    return (local,) + sorted_entries(kslot, 2 * n) + sorted_entries(vslot, 2 * n)


def attention_kernel(degree, heads, sources, local, korder, kbegin, vorder, vbegin, q_ref, *refs):
    k_refs, v_refs = refs[:sources], refs[sources : 2 * sources]
    out_ref, k_all, v_all, sems = refs[2 * sources :]
    block_len = k_all.shape[2] // degree

    def fetch(source, dest, order, begin, s, sem):
        def one(r, carry):
            e = order[r]
            at = pl.ds(pl.multiple_of(local[e] * block_len, block_len), block_len)
            to = pl.ds(pl.multiple_of(lax.rem(e, degree) * block_len, block_len), block_len)
            pltpu.make_async_copy(source.at[:, at], dest.at[lax.div(e, degree), :, to], sem).start()
            return carry

        lax.fori_loop(begin[s], begin[s + 1], one, 0)

    for s in range(sources):
        fetch(k_refs[s], k_all, korder, kbegin, s, sems.at[0])
    for s in range(sources):
        fetch(v_refs[s], v_all, vorder, vbegin, s, sems.at[1])
    pltpu.make_async_copy(k_all, k_all, sems.at[0]).wait()
    pltpu.make_async_copy(v_all, v_all, sems.at[1]).wait()
    factor = math.log2(math.e) / math.sqrt(HD)

    feat = heads * HD
    head_row = lax.broadcasted_iota(jnp.int32, (feat, heads * block_len), 0) // HD
    head_col = lax.broadcasted_iota(jnp.int32, (feat, heads * block_len), 1) // block_len
    diagonal = head_row == head_col

    def one_block(b, carry):
        nodes = pl.ds(pl.multiple_of(b * block_len, block_len), block_len)
        q = jnp.concatenate([q_ref[:, nodes]] * heads, 1)
        scores = contract(k_all[b], jnp.where(diagonal, q, jnp.zeros_like(q)), 0, 0)
        top = jnp.max(scores, 0, keepdims=True)
        probs = jnp.exp2((scores - top) * factor)
        total = jnp.sum(probs, 0, keepdims=True)
        probs = probs.astype(bf16)
        cols = []
        for h in range(heads):
            rows, own = slice(h * HD, (h + 1) * HD), slice(h * block_len, (h + 1) * block_len)
            cols.append(jnp.dot(v_all[b, rows, :], probs[:, own], preferred_element_type=f32) / total[:, own])
        out_ref[nodes, :] = jnp.concatenate(cols, 0).T.astype(bf16)
        return carry

    count = k_all.shape[0]
    lax.fori_loop(0, count, one_block, 0, unroll=4 if count % 4 == 0 else 1)


def attention(queries, keys, values, tables, call, count, block_len, degree):
    feat = queries.shape[0]
    return pl.pallas_call(
        functools.partial(attention_kernel, degree, feat // HD, len(keys)),
        grid_spec=pltpu.PrefetchScalarGridSpec(
            num_scalar_prefetch=5,
            grid=(1,),
            in_specs=[pl.BlockSpec((feat, count * block_len), lambda i, *_: (0, call))]
            + [pl.BlockSpec(memory_space=pl.ANY)] * (2 * len(keys)),
            out_specs=pl.BlockSpec((count * block_len, feat), lambda i, *_: (0, 0)),
            scratch_shapes=[pltpu.VMEM((count, feat, degree * block_len), bf16)] * 2 + [pltpu.SemaphoreType.DMA((2,))],
        ),
        out_shape=jax.ShapeDtypeStruct((count * block_len, feat), bf16),
        compiler_params=params(),
        cost_estimate=pl.CostEstimate(
            flops=4 * count * block_len * degree * block_len * feat,
            bytes_accessed=2 * count * feat * block_len * (2 * degree + 2),
            transcendentals=count * block_len * degree * block_len * feat // HD,
        ),
        name="attention",
    )(*[t[call] for t in tables], queries, *keys, *values)


def window_base(starts, i, e):
    return pl.multiple_of((starts[i, e] // 16) * 16, 16)


def further_windows(starts, i, e):
    left = starts[i + 1, e] - window_base(starts, i, e)
    return jnp.maximum((left + WINDOW - 1) // WINDOW, 1)


def any_further(starts, i, first, count):
    most = further_windows(starts, i, first)
    for e in range(first + 1, first + count):
        most = jnp.maximum(most, further_windows(starts, i, e))
    return most > 1


def one_hot(rank_row, base):
    place = lax.broadcasted_iota(jnp.int32, (WINDOW, rank_row.shape[1]), 0)
    return jnp.where(place == rank_row - base, 1.0, 0.0).astype(bf16)


def stack_hot(starts, rank, i, first, count):
    return jnp.concatenate([one_hot(rank[e : e + 1, :], window_base(starts, i, e)) for e in range(first, first + count)], 0)


def group_kernel(first, count, pieces, chunk, lines, owners, counts, ids, perm, starts, order, line, *refs):
    refs = list(refs)
    rank_ref, cot_ref, gain_ref, router_ref, win_ref, wout_ref, rcol_ref = [refs.pop(0) for _ in range(7)]
    if pieces:
        res_ref = refs.pop(0)
        atts = [refs.pop(0) for _ in range(pieces)]
        projs = [refs.pop(0) for _ in range(pieces)]
        stream_ref = None
    else:
        stream_ref = refs.pop(0)
        partial_refs = [refs.pop(0) for _ in range(owners)]
        refs.pop(0)
    if pieces:
        out_stream = refs.pop(0)
    out_refs = [refs.pop(0) for _ in range(owners)]
    grad_refs, (rows_ref, slots, acc_in, acc_out) = refs[:-4], refs[-4:]
    nodes, width = cot_ref.shape
    step = pl.program_id(0)

    @pl.when(step == 0)
    def _():
        slots[...] = jnp.zeros_like(slots)

        def place(i, carry):
            at = pl.ds(pl.multiple_of(i * chunk, chunk), chunk)
            if pieces:
                projected = jnp.dot(atts[0][at, :], projs[0][...], preferred_element_type=f32)
                for a, w in zip(atts[1:], projs[1:]):
                    projected = projected + jnp.dot(a[at, :], w[...], preferred_element_type=f32)
                stream = (res_ref[at, :].astype(f32) + projected).astype(bf16)
                out_stream[at, :] = stream
            else:
                stream = stream_ref[at, :]
            wide = stream.astype(f32)
            inverse_rms = lax.rsqrt(jnp.mean(wide * wide, -1, keepdims=True) + norm_eps)
            rows_ref[:, :width] = (wide * inverse_rms * gain_ref[...]).astype(bf16)
            rows_ref[:, width:] = cot_ref[at, :]
            rank = rank_ref[:, at]
            packed = jnp.dot(stack_hot(starts, rank, i, first, count), rows_ref[...], preferred_element_type=f32).astype(bf16)
            for e in range(count):
                to = pl.ds(window_base(starts, i, first + e), WINDOW)
                slots[e, to, :] = slots[e, to, :] + packed[e * WINDOW : (e + 1) * WINDOW]

            @pl.when(any_further(starts, i, first, count))
            def _():
                for e in range(count):

                    def more(w, carry, e=e):
                        base = pl.multiple_of(window_base(starts, i, first + e) + w * WINDOW, 16)
                        hot = one_hot(rank[first + e : first + e + 1, :], base)
                        got = jnp.dot(hot, rows_ref[...], preferred_element_type=f32)
                        to = pl.ds(base, WINDOW)
                        slots[e, to, :] = slots[e, to, :] + got.astype(bf16)
                        return carry

                    lax.fori_loop(1, further_windows(starts, i, first + e), more, 0)

            return carry

        lax.fori_loop(0, nodes // chunk, place, 0)

    e = step + first
    tiles = (counts[e] + TILE - 1) // TILE
    acc_in[...] = jnp.zeros_like(acc_in)
    acc_out[...] = jnp.zeros_like(acc_out)
    w_in = win_ref[0]
    w_out = wout_ref[0]
    mine = lax.broadcasted_iota(jnp.int32, (TILE, router_ref.shape[1]), 1) == ids[e]
    column = rcol_ref[0]

    def one(t, carry):
        at = pl.ds(pl.multiple_of(t * TILE, TILE), TILE)
        x = slots[step, at, :width]
        cot = slots[step, at, width:]
        cot_wide = cot.astype(f32)
        logits = jnp.dot(x, router_ref[...], preferred_element_type=f32)
        logit = jnp.sum(jnp.where(mine, logits, 0.0), 1, keepdims=True)
        gate = 1.0 / (1.0 + jnp.exp(-logit))
        scaled = (gate * cot_wide).astype(bf16)
        a = jnp.dot(x, w_in, preferred_element_type=f32)
        grad_hidden = contract(scaled, w_out, 1, 1)
        a2 = a * a
        t1 = jnp.tanh(a * (root_two_pi + (root_two_pi * cubic_term) * a2))
        half = 0.5 + 0.5 * t1
        hidden = (a * half).astype(bf16)
        slope = half + (a * (1.0 - t1 * t1)) * (0.5 * root_two_pi + (1.5 * root_two_pi * cubic_term) * a2)
        grad_pre = (grad_hidden * slope).astype(bf16)
        acc_out[...] += contract(hidden, scaled, 0, 0)
        acc_in[...] += contract(x, grad_pre, 0, 0)
        produced = jnp.dot(hidden, w_out, preferred_element_type=f32).astype(bf16).astype(f32)
        grad_rows = contract(grad_pre, w_in, 1, 1).astype(bf16).astype(f32)
        grad_logit = jnp.sum(cot_wide * produced, 1, keepdims=True) * gate * (1.0 - gate)
        slots[step, at, :width] = (gate * produced).astype(bf16)
        slots[step, at, width:] = (grad_rows + grad_logit * column).astype(bf16)
        return carry

    lax.fori_loop(0, tiles, one, 0)

    ff = acc_in.shape[1]
    part = 2 * width // lines

    def write(grad_ref):
        for p in range(lines):
            where = lax.rem(p - line[0] + lines, lines)
            at = pl.ds(pl.multiple_of(where * part, part), part)
            low = p * part
            if low < width:
                grad_ref[0, at, :] = acc_in[low : low + part, :].astype(bf16)
            else:
                low = low - width
                for j in range(ff // width):
                    cols = slice(j * width, (j + 1) * width)
                    grad_ref[0, at, cols] = acc_out[j * width + low : j * width + low + part, :].astype(bf16)

    each = count // len(grad_refs)
    for k, grad_ref in enumerate(grad_refs):
        pl.when((step >= k * each) & (step < (k + 1) * each))(functools.partial(write, grad_ref))

    @pl.when(step == count - 1)
    def _():
        chunks = nodes // chunk // owners

        for d in range(owners):

            def gather(c, carry, d=d):
                i = order[d] * chunks + c
                rank = rank_ref[:, pl.ds(pl.multiple_of(i * chunk, chunk), chunk)]
                windows = [slots[e, pl.ds(window_base(starts, i, first + e), WINDOW), :] for e in range(count)]
                total = contract(stack_hot(starts, rank, i, first, count), jnp.concatenate(windows, 0), 0, 0)

                def further(total):
                    for e in range(count):

                        def more(w, acc, e=e):
                            base = pl.multiple_of(window_base(starts, i, first + e) + w * WINDOW, 16)
                            hot = one_hot(rank[first + e : first + e + 1, :], base)
                            return acc + contract(hot, slots[e, pl.ds(base, WINDOW), :], 0, 0)

                        total = lax.fori_loop(1, further_windows(starts, i, first + e), more, total)
                    return total

                total = lax.cond(any_further(starts, i, first, count), further, lambda total: total, total)
                at = pl.ds(pl.multiple_of(c * chunk, chunk), chunk)
                if not pieces:
                    total = total + partial_refs[d][at, :].astype(f32)
                out_refs[d][at, :] = total.astype(bf16)
                return carry

            lax.fori_loop(0, chunks, gather, 0)


def expert_group(scalars, common, weights, first, count, head, tail, lines, slot_rows, chunk):
    counts, ids, perm, starts, order, line = scalars
    rank, cotangent, gain, router = common
    w_in, w_out, columns = weights
    nodes, width = cotangent.shape
    ff = w_in.shape[2]
    owners = order.shape[0]
    whole = lambda a: pl.BlockSpec(a.shape, lambda i, *_: (0,) * a.ndim)
    listed = lambda *shape: pl.BlockSpec((1,) + shape, lambda i, c, d, perm, *_: (perm[i + first], 0, 0))
    args = [rank, cotangent, gain, router, w_in, w_out, columns]
    specs = [whole(a) for a in args[:4]] + [listed(width, ff), listed(ff, width), listed(1, width)]
    out_shape, out_specs = [], []
    if head:
        residual, atts, projs = head
        extra = [residual, *atts, *projs]
        specs += [whole(a) for a in extra]
        out_shape.append(jax.ShapeDtypeStruct((nodes, width), bf16))
        pieces = len(atts)
    else:
        stream, partials, after = tail
        extra = [stream, *partials, after]
        specs += [whole(stream)] + [whole(p) for p in partials] + [pl.BlockSpec(memory_space=pl.ANY)]
        pieces = 0
    out_shape += [jax.ShapeDtypeStruct((nodes // owners, 2 * width), bf16)] * owners
    out_specs = [pl.BlockSpec(o.shape, lambda i, *_: (0, 0)) for o in out_shape]
    parts = 4 if count % 4 == 0 else count
    each = count // parts
    out_shape += [jax.ShapeDtypeStruct((each, 2 * width, ff), bf16)] * parts
    for k in range(parts):
        out_specs.append(
            pl.BlockSpec((1, 2 * width, ff), lambda i, *_, k=k: (jnp.clip(i - k * each, 0, each - 1), 0, 0))
        )
    return pl.pallas_call(
        functools.partial(group_kernel, first, count, pieces, chunk, lines, owners),
        grid_spec=pltpu.PrefetchScalarGridSpec(
            num_scalar_prefetch=6,
            grid=(count,),
            in_specs=specs,
            out_specs=out_specs,
            scratch_shapes=[
                pltpu.VMEM((chunk, 2 * width), bf16),
                pltpu.VMEM((count, slot_rows, 2 * width), bf16),
                pltpu.VMEM((width, ff), f32),
                pltpu.VMEM((ff, width), f32),
            ],
        ),
        out_shape=out_shape,
        compiler_params=params(),
        cost_estimate=pl.CostEstimate(flops=1000, bytes_accessed=1000, transcendentals=0),
        name="experts",
    )(counts, ids, perm, starts, order, line, *args, *extra)


def home_kernel(parts, stream_ref, cot_ref, gain_ref, *refs):
    layer_ref, grad_ref = refs[parts:]
    total = refs[0][...].astype(f32)
    for g in refs[1:parts]:
        total = total + g[...].astype(f32)
    width = stream_ref.shape[1]
    stream = stream_ref[...].astype(f32)
    inverse_rms = lax.rsqrt(jnp.mean(stream * stream, -1, keepdims=True) + norm_eps)
    layer_ref[...] = (stream + total[:, :width]).astype(bf16)
    gained = total[:, width:] * gain_ref[...]
    mean = jnp.mean(stream * gained, -1, keepdims=True)
    grad = cot_ref[...].astype(f32) + inverse_rms * gained - stream * (inverse_rms * inverse_rms * inverse_rms) * mean
    grad_ref[...] = grad.astype(bf16)


def at_home(me, stream, cotangent, gain, parts, chunk):
    tok_dev, width = cotangent.shape
    steps = tok_dev // chunk
    fresh = lambda w: pl.BlockSpec((chunk, w), lambda i, me: (i, 0))
    return pl.pallas_call(
        lambda me, *refs: home_kernel(len(parts), *refs),
        grid_spec=pltpu.PrefetchScalarGridSpec(
            num_scalar_prefetch=1,
            grid=(steps,),
            in_specs=[
                pl.BlockSpec((chunk, width), lambda i, me: (me[0] * steps + i, 0)),
                fresh(width),
                pl.BlockSpec(gain.shape, lambda i, me: (0, 0)),
            ]
            + [fresh(2 * width) for _ in parts],
            out_specs=[fresh(width), fresh(width)],
        ),
        out_shape=[jax.ShapeDtypeStruct((tok_dev, width), bf16)] * 2,
        compiler_params=params(),
        cost_estimate=pl.CostEstimate(
            flops=EAGER * tok_dev * width * 1000, bytes_accessed=tok_dev * width * 16, transcendentals=0
        ),
        name="at_home",
    )(me.reshape(1), stream, cotangent, gain, *parts)


def line_pairs(seq_count, d):
    lines = seq_count // 4
    return [(z * 4 + r, ((z + d) % lines) * 4 + r) for z in range(lines) for r in range(4)]


def seq_place():
    s = lax.axis_index("seq")
    return s % 2, (s // 2) % 2, s // 4


def add_bf16(*terms):
    total = terms[0].astype(f32)
    for t in terms[1:]:
        total = total + t.astype(f32)
    return total.astype(bf16)


def token_spec():
    return pl.BlockSpec((8, 128), lambda i: (0, 0)), jax.ShapeDtypeStruct((8, 128), f32)


def sum_kernel(terms, cuts, *refs):
    outs = refs[-1 - cuts : -1]
    total = refs[0][...].astype(f32)
    for r in refs[1:terms]:
        total = total + r[...].astype(f32)
    total = total.astype(bf16)
    part = total.shape[1] // cuts
    for k, out in enumerate(outs):
        out[...] = total[:, k * part : (k + 1) * part]
    refs[-1][...] = jnp.zeros_like(refs[-1])


def sum_blocks(terms, cuts, after, name):
    shape = terms[0].shape
    whole = lambda s: pl.BlockSpec(s, lambda i: (0, 0, 0))
    piece = (shape[0], shape[1] // cuts, shape[2])
    token, token_shape = token_spec()
    found = pl.pallas_call(
        functools.partial(sum_kernel, len(terms), cuts),
        grid=(1,),
        in_specs=[whole(shape)] * len(terms) + [pl.BlockSpec(memory_space=pl.ANY)] * len(after),
        out_specs=[whole(piece)] * cuts + [token],
        out_shape=[jax.ShapeDtypeStruct(piece, bf16)] * cuts + [token_shape],
        compiler_params=params(),
        cost_estimate=pl.CostEstimate(flops=1000, bytes_accessed=1000, transcendentals=0),
        name=name,
    )(*terms, *after)
    return found[:-1], found[-1]


def stack_kernel(count, *refs):
    for k in range(count):
        refs[-1][k] = refs[k][...]


def stack_pieces(pieces, after):
    shape = pieces[0].shape
    return pl.pallas_call(
        functools.partial(stack_kernel, len(pieces)),
        grid=(1,),
        in_specs=[pl.BlockSpec(shape, lambda i: (0, 0, 0))] * len(pieces) + [pl.BlockSpec(memory_space=pl.ANY)] * len(after),
        out_specs=pl.BlockSpec((len(pieces),) + shape, lambda i: (0, 0, 0, 0)),
        out_shape=jax.ShapeDtypeStruct((len(pieces),) + shape, bf16),
        compiler_params=params(),
        cost_estimate=pl.CostEstimate(flops=1000, bytes_accessed=1000, transcendentals=0),
        name="stack_pieces",
    )(*pieces, *after)


class SeqSum:
    def __init__(self, grads, seq_count):
        self.grads, self.seq_count, self.lines = grads, seq_count, seq_count // 4
        self.sib = sibling_pairs(seq_count)
        self.cross = [(i, i ^ 2) for i in range(seq_count)]

    def over_core(self, after):
        self.got = [lax.ppermute(g, "seq", self.sib) for g in self.grads[:2]]
        (first,), token = sum_blocks([self.grads[2], self.got[0]], 1, after, "sum_core")
        self.crossed = lax.ppermute(first, "seq", self.cross)
        return token

    def over_x(self):
        self.parts, token = sum_blocks([self.grads[3], self.got[1], self.crossed], self.lines, [], "sum_x")
        return token

    def over_lines(self):
        shard = self.parts[0].astype(f32)
        for d in range(1, self.lines):
            shard = shard + lax.ppermute(self.parts[d], "seq", line_pairs(self.seq_count, d)).astype(f32)
        self.shard = shard.astype(bf16)

    def back(self, after):
        pieces = [self.shard]
        for d in range(1, self.lines):
            pieces.append(lax.ppermute(self.shard, "seq", line_pairs(self.seq_count, d)))
        own = stack_pieces(pieces, after)
        other = lax.ppermute(own, "seq", self.cross)
        return [own, other, lax.ppermute(own, "seq", self.sib), lax.ppermute(other, "seq", self.sib)]


def unpack_kernel(lines, each, width, where, line, *refs):
    win_ref, wout_ref = refs[-2:]
    step = pl.program_id(0)
    for a in range(4):
        for i in range(each):

            @pl.when(step == a * each + i)
            def _(a=a, i=i):
                for p in range(lines):
                    block = refs[a][lax.rem(line[0] - p + lines, lines), i].astype(f32)
                    part, ff = block.shape
                    low = p * part
                    if low < width:
                        win_ref[0, low : low + part, :] = block
                    else:
                        low = low - width
                        for j in range(ff // width):
                            wout_ref[0, j * width + low : j * width + low + part, :] = block[:, j * width : (j + 1) * width]


def unpack(where, line, blocks, experts, width, ff, into):
    lines, each = blocks[0].shape[:2]
    whole = pl.BlockSpec(blocks[0].shape, lambda i, *_: (0, 0, 0, 0))
    out = lambda *shape: pl.BlockSpec((1,) + shape, lambda i, where, line: (where[i], 0, 0))
    return pl.pallas_call(
        functools.partial(unpack_kernel, lines, each, width),
        grid_spec=pltpu.PrefetchScalarGridSpec(
            num_scalar_prefetch=2,
            grid=(4 * each,),
            in_specs=[whole] * 4 + [pl.BlockSpec(memory_space=pl.ANY)] * len(into),
            out_specs=[out(width, ff), out(ff, width)],
        ),
        out_shape=[
            jax.ShapeDtypeStruct((experts, width, ff), f32),
            jax.ShapeDtypeStruct((experts, ff, width), f32),
        ],
        input_output_aliases={6 + i: i for i in range(len(into))},
        compiler_params=params(),
        cost_estimate=pl.CostEstimate(flops=EAGER * 4 * each * 2 * width * ff * 6, bytes_accessed=4 * each * 2 * width * ff * 6, transcendentals=0),
        name="unpack",
    )(where, line, *blocks, *into)


def sum_any(grads, seq_count):
    lines = seq_count // 4
    core, column, line = seq_place()
    sib = sibling_pairs(seq_count)
    cross = [(i, i ^ 2) for i in range(seq_count)]

    def halve(a, which, pairs):
        h = a.shape[0] // 2
        mine = lax.dynamic_slice_in_dim(a, which * h, h, 0)
        other = lax.dynamic_slice_in_dim(a, (1 - which) * h, h, 0)
        return add_bf16(mine, lax.ppermute(other, "seq", pairs))

    a = halve(halve(grads, core, sib), column, cross)
    q = a.shape[0] // lines
    total = lax.dynamic_slice_in_dim(a, line * q, q, 0).astype(f32)
    for d in range(1, lines):
        part = lax.dynamic_slice_in_dim(a, lax.rem(line + d, lines) * q, q, 0)
        total = total + lax.ppermute(part, "seq", line_pairs(seq_count, d)).astype(f32)
    shard = total.astype(bf16)

    out = jnp.zeros((q * lines,) + a.shape[1:], bf16)
    out = lax.dynamic_update_slice_in_dim(out, shard, line * q, 0)
    for d in range(1, lines):
        got = lax.ppermute(shard, "seq", line_pairs(seq_count, d))
        out = lax.dynamic_update_slice_in_dim(out, got, lax.rem(line - d + lines, lines) * q, 0)

    def double(a, which, pairs):
        got = lax.ppermute(a, "seq", pairs)
        return jnp.where(which == 0, jnp.concatenate([a, got], 0), jnp.concatenate([got, a], 0))

    return double(double(out, column, cross), core, sib)


def shards(
    query_cols,
    key_cols,
    value_cols,
    block_list,
    residual,
    out_proj,
    norm_gain,
    router_weight,
    expert_ids,
    expert_in,
    expert_out,
    cotangent,
):
    seq_count = lax.axis_size("seq")
    exp_count = lax.axis_size("expert")
    me = lax.axis_index("expert")
    feat, nodes = query_cols.shape
    blk_seq, degree = block_list.shape
    block_len = nodes // blk_seq
    tok_dev, width = residual.shape
    expert_total = router_weight.shape[1]
    experts = expert_in.shape[0]
    ff = expert_in.shape[2]
    topk = expert_ids.shape[1]
    chunk = min(256, tok_dev)
    capacity = 2 * tok_dev * topk // expert_total * exp_count
    slot_rows = capacity + WINDOW

    calls = 2 if blk_seq % 2 == 0 else 1
    keys, values = ring_gather(key_cols, value_cols, seq_count)
    tables = block_tables(block_list, blk_seq, seq_count, calls)

    residual_all = gather_expert_axis(residual, exp_count)
    cotangent_all = gather_expert_axis(cotangent, exp_count)
    ids_all = gather_expert_axis(expert_ids.T, exp_count, 1)
    gain = norm_gain.reshape(1, width)
    core, column, line_at = seq_place()
    lines = seq_count // 4
    line = line_at.reshape(1).astype(jnp.int32)
    groups = 2 if experts % 8 == 0 else 1
    per_group = experts // groups
    tuned = per_group % 4 == 0 and (2 * width) % (16 * lines) == 0 and lines > 1
    each = per_group // 4
    at = jnp.arange(experts, dtype=jnp.int32)
    first_of = lambda dest, i: at // per_group * per_group + dest * each + i
    dests = jnp.stack([(1 - core) * 2 + 1 - column, (1 - core) * 2 + column, core * 2 + 1 - column, core * 2 + column])
    outs = jnp.stack([core * 2 + column, core * 2 + 1 - column, (1 - core) * 2 + column, (1 - core) * 2 + 1 - column])
    if tuned:
        perm = first_of(jnp.tile(jnp.repeat(dests, each), groups), at % each).astype(jnp.int32)
        where = first_of(jnp.tile(jnp.repeat(outs, each), groups), at % each).astype(jnp.int32)
    else:
        perm = at
        line = jnp.zeros_like(line)
    local_ids = me * experts + perm
    hot = jnp.sum((ids_all[None, :, :] == local_ids[:, None, None]).astype(jnp.int32), 1)
    running = jnp.cumsum(hot, 1)
    rank = jnp.where(hot > 0, running - 1, -(1 << 20))
    ends = running[:, chunk - 1 :: chunk]
    starts = jnp.concatenate([jnp.zeros((experts, 1), jnp.int32), ends], 1).T
    counts = running[:, -1]
    router = jnp.pad(router_weight, ((0, 0), (0, -expert_total % 128)))
    columns = lax.dynamic_slice_in_dim(router_weight.T, me * experts, experts, 0).astype(f32).reshape(experts, 1, width)
    projs = [
        lax.dynamic_slice_in_dim(out_proj, lax.rem(me + exp_count - d, exp_count) * feat, feat, 0)
        for d in range(exp_count)
    ]
    owner_order = lax.rem(me + jnp.arange(exp_count, dtype=jnp.int32), exp_count)

    per_call = blk_seq // calls
    pieces = [[] for _ in range(exp_count)]
    for c in range(calls):
        part = attention(query_cols, keys, values, tables, c, per_call, block_len, degree)
        pieces[0].append(part)
        for d in range(1, exp_count):
            pieces[d].append(lax.ppermute(part, "expert", shift_pairs(exp_count, d)))
    atts = [jnp.concatenate(p, 0) for p in pieces]

    scalars = (counts, local_ids, perm, starts, owner_order, line)
    common = (rank, cotangent_all, gain, router)
    weights = (expert_in, expert_out, columns)
    into, sums, after, stream, partials = [], [], None, None, None
    for g in range(groups):
        head = (residual_all, atts, projs) if g == 0 else None
        tail = (stream, partials, after)
        found = list(
            expert_group(scalars, common, weights, g * per_group, per_group, head, tail, lines, slot_rows, chunk)
        )
        if g == 0:
            stream = found.pop(0)
        partials, grads = found[:exp_count], found[exp_count:]
        if tuned:
            sums.append(SeqSum(grads, seq_count))
            after = sums[-1].over_core([sums[-2].over_x()] if g > 0 else [])
        else:
            into.append(sum_any(jnp.concatenate(grads, 0).reshape(per_group * 2 * width, ff), seq_count))
    parts = partials[:1] + [lax.ppermute(partials[d], "expert", shift_pairs(exp_count, d)) for d in range(1, exp_count)]
    layer_out, grad_stream = at_home(me, stream, cotangent, gain, parts, chunk)
    if tuned:
        sums[-1].over_x()
        for g, each_sum in enumerate(sums):
            each_sum.over_lines()
            blocks = each_sum.back([layer_out] if g == 0 else [])
            into = unpack(where[g * per_group : (g + 1) * per_group], line, blocks, experts, width, ff, into)
    if tuned:
        grad_w_in, grad_w_out = into
    else:
        total = jnp.concatenate(into, 0).reshape(experts, 2 * width, ff).astype(f32)
        grad_w_in = total[:, :width, :]
        grad_w_out = jnp.concatenate([total[:, width:, j * width : (j + 1) * width] for j in range(ff // width)], 1)

    return layer_out, grad_stream, grad_w_in, grad_w_out


def solution(mesh):
    return jax.shard_map(
        shards,
        mesh=mesh,
        in_specs=(
            P("expert", "seq"),
            P("expert", "seq"),
            P("expert", "seq"),
            P("seq", None),
            P(("seq", "expert"), None),
            P(),
            P(),
            P(),
            P(("seq", "expert"), None),
            P("expert", None, None),
            P("expert", None, None),
            P(("seq", "expert"), None),
        ),
        out_specs=(
            P(("seq", "expert"), None),
            P(("seq", "expert"), None),
            P("expert", None, None),
            P("expert", None, None),
        ),
        check_vma=False,
    )
```

```python
import functools
import math

import jax
import jax.numpy as jnp
from jax import lax
from jax.experimental import pallas as pl
from jax.experimental.pallas import tpu as pltpu
from jax.sharding import PartitionSpec as P

HD = 32
WINDOW = 128
TILE = 256
EAGER = 32

norm_eps = 1e-05
root_two_pi = 0.7978845608028654
cubic_term = 0.044715

bf16 = jnp.bfloat16
f32 = jnp.float32


def params(mebibytes=32):
    return pltpu.CompilerParams(vmem_limit_bytes=mebibytes * 1024 * 1024)


def contract(a, b, da, db):
    return lax.dot_general(a, b, (((da,), (db,)), ((), ())), preferred_element_type=f32)


def ring_order(seq_count):
    rows = max(1, seq_count // 4)
    if seq_count % 4:
        return list(range(seq_count // 2))
    return [2 * z for z in range(rows)] + [2 * z + 1 for z in reversed(range(rows))]


def ring_pairs(seq_count, step):
    order = ring_order(seq_count)
    n = len(order)
    return [(2 * order[i] + c, 2 * order[(i + step) % n] + c) for i in range(n) for c in range(2)]


def sibling_pairs(seq_count):
    return [(s, s ^ 1) for s in range(seq_count)]


def shift_pairs(count, d):
    return [(i, (i + d) % count) for i in range(count)]


def gather_expert_axis(x, exp_count, axis=0):
    me = lax.axis_index("expert")
    size = x.shape[axis]
    shape = list(x.shape)
    shape[axis] = size * exp_count
    out = jnp.zeros(shape, x.dtype)
    out = lax.dynamic_update_slice_in_dim(out, x, me * size, axis)
    for d in range(1, exp_count):
        got = lax.ppermute(x, "expert", shift_pairs(exp_count, d))
        out = lax.dynamic_update_slice_in_dim(out, got, lax.rem(me + exp_count - d, exp_count) * size, axis)
    return out


def ring_gather(keys, values, seq_count):
    n = seq_count // 2
    fwd, bwd, sib = ring_pairs(seq_count, 1), ring_pairs(seq_count, -1), sibling_pairs(seq_count)
    k, v = keys, values
    own, other = ([], []), ([], [])
    for t in range(n):
        if t > 0:
            k = lax.ppermute(k, "seq", fwd)
            v = lax.ppermute(v, "seq", bwd)
        own[0].append(k)
        own[1].append(v)
        other[0].append(lax.ppermute(k, "seq", sib))
        other[1].append(lax.ppermute(v, "seq", sib))
    return own[0] + other[0], own[1] + other[1]


def sorted_entries(slot, slots):
    count = slot.shape[-1]
    at = jnp.arange(count, dtype=jnp.int32)
    before = (slot[:, None, :] < slot[:, :, None]) | ((slot[:, None, :] == slot[:, :, None]) & (at[None, None, :] < at[None, :, None]))
    rank = jnp.sum(before.astype(jnp.int32), 2)
    order = jnp.sum(jnp.where(rank[:, None, :] == at[None, :, None], at[None, None, :], 0), 2)
    begin = jnp.sum((slot[:, None, :] < jnp.arange(slots + 1, dtype=jnp.int32)[None, :, None]).astype(jnp.int32), 2)
    return order, begin


def block_tables(block_list, blk_seq, seq_count, calls):
    order = ring_order(seq_count)
    n = len(order)
    inverse = [0] * n
    for i, chip in enumerate(order):
        inverse[chip] = i
    inverse = jnp.asarray(inverse, jnp.int32)
    me = lax.axis_index("seq")
    place = inverse[me // 2]
    owner = block_list // blk_seq
    local = (block_list % blk_seq).reshape(calls, -1)
    other = inverse[owner // 2]
    flag = ((owner ^ me) & 1) * n
    kslot = (flag + lax.rem(place - other + n, n)).reshape(calls, -1)
    vslot = (flag + lax.rem(other - place + n, n)).reshape(calls, -1)
    return (local,) + sorted_entries(kslot, 2 * n) + sorted_entries(vslot, 2 * n)


def attention_kernel(degree, heads, sources, local, korder, kbegin, vorder, vbegin, q_ref, *refs):
    k_refs, v_refs = refs[:sources], refs[sources : 2 * sources]
    out_ref, k_all, v_all, sems = refs[2 * sources :]
    block_len = k_all.shape[2] // degree

    def fetch(source, dest, order, begin, s, sem):
        def one(r, carry):
            e = order[r]
            at = pl.ds(pl.multiple_of(local[e] * block_len, block_len), block_len)
            to = pl.ds(pl.multiple_of(lax.rem(e, degree) * block_len, block_len), block_len)
            pltpu.make_async_copy(source.at[:, at], dest.at[lax.div(e, degree), :, to], sem).start()
            return carry

        lax.fori_loop(begin[s], begin[s + 1], one, 0)

    for s in range(sources):
        fetch(k_refs[s], k_all, korder, kbegin, s, sems.at[0])
    for s in range(sources):
        fetch(v_refs[s], v_all, vorder, vbegin, s, sems.at[1])
    pltpu.make_async_copy(k_all, k_all, sems.at[0]).wait()
    pltpu.make_async_copy(v_all, v_all, sems.at[1]).wait()
    factor = math.log2(math.e) / math.sqrt(HD)

    feat = heads * HD
    head_row = lax.broadcasted_iota(jnp.int32, (feat, heads * block_len), 0) // HD
    head_col = lax.broadcasted_iota(jnp.int32, (feat, heads * block_len), 1) // block_len
    diagonal = head_row == head_col

    def one_block(b, carry):
        nodes = pl.ds(pl.multiple_of(b * block_len, block_len), block_len)
        q = jnp.concatenate([q_ref[:, nodes]] * heads, 1)
        scores = contract(k_all[b], jnp.where(diagonal, q, jnp.zeros_like(q)), 0, 0)
        top = jnp.max(scores, 0, keepdims=True)
        probs = jnp.exp2((scores - top) * factor)
        total = jnp.sum(probs, 0, keepdims=True)
        probs = probs.astype(bf16)
        cols = []
        for h in range(heads):
            rows, own = slice(h * HD, (h + 1) * HD), slice(h * block_len, (h + 1) * block_len)
            cols.append(jnp.dot(v_all[b, rows, :], probs[:, own], preferred_element_type=f32) / total[:, own])
        out_ref[nodes, :] = jnp.concatenate(cols, 0).T.astype(bf16)
        return carry

    count = k_all.shape[0]
    lax.fori_loop(0, count, one_block, 0, unroll=4 if count % 4 == 0 else 1)


def attention(queries, keys, values, tables, call, count, block_len, degree):
    feat = queries.shape[0]
    return pl.pallas_call(
        functools.partial(attention_kernel, degree, feat // HD, len(keys)),
        grid_spec=pltpu.PrefetchScalarGridSpec(
            num_scalar_prefetch=5,
            grid=(1,),
            in_specs=[pl.BlockSpec((feat, count * block_len), lambda i, *_: (0, call))]
            + [pl.BlockSpec(memory_space=pl.ANY)] * (2 * len(keys)),
            out_specs=pl.BlockSpec((count * block_len, feat), lambda i, *_: (0, 0)),
            scratch_shapes=[pltpu.VMEM((count, feat, degree * block_len), bf16)] * 2 + [pltpu.SemaphoreType.DMA((2,))],
        ),
        out_shape=jax.ShapeDtypeStruct((count * block_len, feat), bf16),
        compiler_params=params(56),
        cost_estimate=pl.CostEstimate(
            flops=4 * count * block_len * degree * block_len * feat,
            bytes_accessed=2 * count * feat * block_len * (2 * degree + 2),
            transcendentals=count * block_len * degree * block_len * feat // HD,
        ),
        name="attention",
    )(*[t[call] for t in tables], queries, *keys, *values)


def place_of(part, line, lines):
    differ = jnp.bitwise_xor(part, line)
    place = 0
    step = 1
    while step < lines:
        place = place * 2 + jnp.bitwise_and(lax.div(differ, step), 1)
        step *= 2
    return place


def window_base(starts, i, e):
    return pl.multiple_of((starts[i, e] // 16) * 16, 16)


def further_windows(starts, i, e):
    left = starts[i + 1, e] - window_base(starts, i, e)
    return jnp.maximum((left + WINDOW - 1) // WINDOW, 1)


def any_further(starts, i, first, count):
    most = further_windows(starts, i, first)
    for e in range(first + 1, first + count):
        most = jnp.maximum(most, further_windows(starts, i, e))
    return most > 1


def one_hot(rank_row, base):
    place = lax.broadcasted_iota(jnp.int32, (WINDOW, rank_row.shape[1]), 0)
    return jnp.where(place == rank_row - base, 1.0, 0.0).astype(bf16)


def stack_hot(starts, rank, i, first, count):
    return jnp.concatenate([one_hot(rank[e : e + 1, :], window_base(starts, i, e)) for e in range(first, first + count)], 0)


def group_kernel(first, count, pieces, after, chunk, lines, owners, counts, ids, perm, starts, order, place, *refs):
    refs = list(refs)
    rank_ref, cot_ref, gain_ref, router_ref, win_ref, wout_ref, rcol_ref = [refs.pop(0) for _ in range(7)]
    if pieces:
        res_ref = refs.pop(0)
        atts = [refs.pop(0) for _ in range(pieces)]
        projs = [refs.pop(0) for _ in range(pieces)]
        stream_ref = None
    else:
        stream_ref = refs.pop(0)
        partial_refs = [refs.pop(0) for _ in range(owners)]
        del refs[: after]
    if pieces:
        out_stream = refs.pop(0)
    out_refs = [refs.pop(0) for _ in range(owners)]
    grad_refs, (rows_ref, slots, acc_in, acc_out) = refs[:-4], refs[-4:]
    nodes, width = cot_ref.shape
    step = pl.program_id(0)

    @pl.when(step == 0)
    def _():
        slots[...] = jnp.zeros_like(slots)

        def dispatch(i, carry):
            at = pl.ds(pl.multiple_of(i * chunk, chunk), chunk)
            if pieces:
                projected = jnp.dot(atts[0][at, :], projs[0][...], preferred_element_type=f32)
                for a, w in zip(atts[1:], projs[1:]):
                    projected = projected + jnp.dot(a[at, :], w[...], preferred_element_type=f32)
                stream = (res_ref[at, :].astype(f32) + projected).astype(bf16)
                out_stream[at, :] = stream
            else:
                stream = stream_ref[at, :]
            wide = stream.astype(f32)
            inverse_rms = lax.rsqrt(jnp.mean(wide * wide, -1, keepdims=True) + norm_eps)
            rows_ref[:, :width] = (wide * inverse_rms * gain_ref[...]).astype(bf16)
            rows_ref[:, width:] = cot_ref[at, :]
            rank = rank_ref[:, at]
            packed = jnp.dot(stack_hot(starts, rank, i, first, count), rows_ref[...], preferred_element_type=f32).astype(bf16)
            for e in range(count):
                to = pl.ds(window_base(starts, i, first + e), WINDOW)
                slots[e, to, :] = slots[e, to, :] + packed[e * WINDOW : (e + 1) * WINDOW]

            @pl.when(any_further(starts, i, first, count))
            def _():
                for e in range(count):

                    def more(w, carry, e=e):
                        base = pl.multiple_of(window_base(starts, i, first + e) + w * WINDOW, 16)
                        hot = one_hot(rank[first + e : first + e + 1, :], base)
                        got = jnp.dot(hot, rows_ref[...], preferred_element_type=f32)
                        to = pl.ds(base, WINDOW)
                        slots[e, to, :] = slots[e, to, :] + got.astype(bf16)
                        return carry

                    lax.fori_loop(1, further_windows(starts, i, first + e), more, 0)

            return carry

        lax.fori_loop(0, nodes // chunk, dispatch, 0)

    e = step + first
    tiles = (counts[e] + TILE - 1) // TILE
    acc_in[...] = jnp.zeros_like(acc_in)
    acc_out[...] = jnp.zeros_like(acc_out)
    w_in = win_ref[0]
    w_out = wout_ref[0]
    mine = lax.broadcasted_iota(jnp.int32, (TILE, router_ref.shape[1]), 1) == ids[e]
    column = rcol_ref[0]

    def one(t, carry):
        at = pl.ds(pl.multiple_of(t * TILE, TILE), TILE)
        x = slots[step, at, :width]
        cot = slots[step, at, width:]
        cot_wide = cot.astype(f32)
        logits = jnp.dot(x, router_ref[...], preferred_element_type=f32)
        logit = jnp.sum(jnp.where(mine, logits, 0.0), 1, keepdims=True)
        gate = 1.0 / (1.0 + jnp.exp(-logit))
        scaled = (gate * cot_wide).astype(bf16)
        a = jnp.dot(x, w_in, preferred_element_type=f32)
        grad_hidden = contract(scaled, w_out, 1, 1)
        a2 = a * a
        t1 = jnp.tanh(a * (root_two_pi + (root_two_pi * cubic_term) * a2))
        half = 0.5 + 0.5 * t1
        hidden = (a * half).astype(bf16)
        slope = half + (a * (1.0 - t1 * t1)) * (0.5 * root_two_pi + (1.5 * root_two_pi * cubic_term) * a2)
        grad_pre = (grad_hidden * slope).astype(bf16)
        acc_out[...] += contract(hidden, scaled, 0, 0)
        acc_in[...] += contract(x, grad_pre, 0, 0)
        produced = jnp.dot(hidden, w_out, preferred_element_type=f32).astype(bf16).astype(f32)
        grad_rows = contract(grad_pre, w_in, 1, 1).astype(bf16).astype(f32)
        grad_logit = jnp.sum(cot_wide * produced, 1, keepdims=True) * gate * (1.0 - gate)
        slots[step, at, :width] = (gate * produced).astype(bf16)
        slots[step, at, width:] = (grad_rows + grad_logit * column).astype(bf16)
        return carry

    lax.fori_loop(0, tiles, one, 0)

    ff = acc_in.shape[1]

    def write(grad_ref, with_in, with_out):
        part = grad_ref.shape[1] // lines
        for p in range(lines):
            at = pl.ds(pl.multiple_of(place_of(p, place[0], lines) * part, part), part)
            low = p * part
            if with_in and low < width:
                grad_ref[0, at, :] = acc_in[low : low + part, :].astype(bf16)
            else:
                low = low - width if with_in else low
                for j in range(ff // width):
                    cols = slice(j * width, (j + 1) * width)
                    grad_ref[0, at, cols] = acc_out[j * width + low : j * width + low + part, :].astype(bf16)

    if count > 2:
        each = count // 4
        for k, grad_ref in enumerate(grad_refs):
            pl.when((step >= k * each) & (step < (k + 1) * each))(functools.partial(write, grad_ref, True, True))
    else:
        for k in range(2):
            for column in range(2):

                @pl.when((step == k) & (place[1] == column))
                def _(k=k, column=column):
                    other, own = grad_refs[2 * k], grad_refs[2 * k + 1]
                    write((own, other)[column], True, False)
                    write((other, own)[column], False, True)

    @pl.when(step == count - 1)
    def _():
        chunks = nodes // chunk // owners

        for d in range(owners):

            def gather(c, carry, d=d):
                i = order[d] * chunks + c
                rank = rank_ref[:, pl.ds(pl.multiple_of(i * chunk, chunk), chunk)]
                windows = [slots[e, pl.ds(window_base(starts, i, first + e), WINDOW), :] for e in range(count)]
                total = contract(stack_hot(starts, rank, i, first, count), jnp.concatenate(windows, 0), 0, 0)

                def further(total):
                    for e in range(count):

                        def more(w, acc, e=e):
                            base = pl.multiple_of(window_base(starts, i, first + e) + w * WINDOW, 16)
                            hot = one_hot(rank[first + e : first + e + 1, :], base)
                            return acc + contract(hot, slots[e, pl.ds(base, WINDOW), :], 0, 0)

                        total = lax.fori_loop(1, further_windows(starts, i, first + e), more, total)
                    return total

                total = lax.cond(any_further(starts, i, first, count), further, lambda total: total, total)
                at = pl.ds(pl.multiple_of(c * chunk, chunk), chunk)
                if not pieces:
                    total = total + partial_refs[d][at, :].astype(f32)
                out_refs[d][at, :] = total.astype(bf16)
                return carry

            lax.fori_loop(0, chunks, gather, 0)


def expert_group(scalars, common, weights, first, count, head, tail, lines, slot_rows, chunk):
    counts, ids, perm, starts, order, place = scalars
    rank, cotangent, gain, router = common
    w_in, w_out, columns = weights
    nodes, width = cotangent.shape
    ff = w_in.shape[2]
    owners = order.shape[0]
    whole = lambda a: pl.BlockSpec(a.shape, lambda i, *_: (0,) * a.ndim)
    listed = lambda *shape: pl.BlockSpec((1,) + shape, lambda i, c, d, perm, *_: (perm[i + first], 0, 0))
    args = [rank, cotangent, gain, router, w_in, w_out, columns]
    specs = [whole(a) for a in args[:4]] + [listed(width, ff), listed(ff, width), listed(1, width)]
    out_shape, out_specs = [], []
    if head:
        residual, atts, projs = head
        extra = [residual, *atts, *projs]
        specs += [whole(a) for a in extra]
        out_shape.append(jax.ShapeDtypeStruct((nodes, width), bf16))
        pieces = len(atts)
    else:
        stream, partials, after = tail
        extra = [stream, *partials, *after]
        specs += [whole(stream)] + [whole(p) for p in partials] + [pl.BlockSpec(memory_space=pl.ANY)] * len(after)
        pieces = 0
    out_shape += [jax.ShapeDtypeStruct((nodes // owners, 2 * width), bf16)] * owners
    out_specs = [pl.BlockSpec(o.shape, lambda i, *_: (0, 0)) for o in out_shape]
    each = max(1, count // 4)
    block = (1, 2 * width if count > 2 else width, ff)
    out_shape += [jax.ShapeDtypeStruct((each,) + block[1:], bf16)] * 4
    for k in range(4):
        first_step = k * each if count > 2 else k // 2
        out_specs.append(pl.BlockSpec(block, lambda i, *_, at=first_step: (jnp.clip(i - at, 0, each - 1), 0, 0)))
    return pl.pallas_call(
        functools.partial(group_kernel, first, count, pieces, 0 if head else len(after), chunk, lines, owners),
        grid_spec=pltpu.PrefetchScalarGridSpec(
            num_scalar_prefetch=6,
            grid=(count,),
            in_specs=specs,
            out_specs=out_specs,
            scratch_shapes=[
                pltpu.VMEM((chunk, 2 * width), bf16),
                pltpu.VMEM((count, slot_rows, 2 * width), bf16),
                pltpu.VMEM((width, ff), f32),
                pltpu.VMEM((ff, width), f32),
            ],
        ),
        out_shape=out_shape,
        compiler_params=params(),
        cost_estimate=pl.CostEstimate(flops=1000, bytes_accessed=1000, transcendentals=0),
        name="experts",
    )(counts, ids, perm, starts, order, place, *args, *extra)


def home_kernel(parts, stream_ref, cot_ref, gain_ref, *refs):
    layer_ref, grad_ref = refs[parts:]
    total = refs[0][...].astype(f32)
    for g in refs[1:parts]:
        total = total + g[...].astype(f32)
    width = stream_ref.shape[1]
    stream = stream_ref[...].astype(f32)
    inverse_rms = lax.rsqrt(jnp.mean(stream * stream, -1, keepdims=True) + norm_eps)
    layer_ref[...] = (stream + total[:, :width]).astype(bf16)
    gained = total[:, width:] * gain_ref[...]
    mean = jnp.mean(stream * gained, -1, keepdims=True)
    grad = cot_ref[...].astype(f32) + inverse_rms * gained - stream * (inverse_rms * inverse_rms * inverse_rms) * mean
    grad_ref[...] = grad.astype(bf16)


def at_home(me, stream, cotangent, gain, parts, chunk, after):
    tok_dev, width = cotangent.shape
    steps = tok_dev // chunk
    fresh = lambda w: pl.BlockSpec((chunk, w), lambda i, me: (i, 0))
    return pl.pallas_call(
        lambda me, *refs: home_kernel(len(parts), *refs[:-3], *refs[-2:]),
        grid_spec=pltpu.PrefetchScalarGridSpec(
            num_scalar_prefetch=1,
            grid=(steps,),
            in_specs=[
                pl.BlockSpec((chunk, width), lambda i, me: (me[0] * steps + i, 0)),
                fresh(width),
                pl.BlockSpec(gain.shape, lambda i, me: (0, 0)),
            ]
            + [fresh(2 * width) for _ in parts]
            + [pl.BlockSpec(memory_space=pl.ANY)],
            out_specs=[fresh(width), fresh(width)],
        ),
        out_shape=[jax.ShapeDtypeStruct((tok_dev, width), bf16)] * 2,
        compiler_params=params(),
        cost_estimate=pl.CostEstimate(
            flops=EAGER * tok_dev * width * 1000, bytes_accessed=tok_dev * width * 16, transcendentals=0
        ),
        name="at_home",
    )(me.reshape(1), stream, cotangent, gain, *parts, after)


def line_pairs(seq_count, d):
    return [(z * 4 + r, (z ^ d) * 4 + r) for z in range(seq_count // 4) for r in range(4)]


def seq_place():
    s = lax.axis_index("seq")
    return s % 2, (s // 2) % 2, s // 4


def sum_kernel(terms, cuts, *refs):
    total = refs[0][...].astype(f32)
    for r in refs[1:terms]:
        total = total + r[...].astype(f32)
    total = total.astype(bf16)
    part = total.shape[1] // cuts
    for k, out in enumerate(refs[len(refs) - cuts :]):
        out[...] = total[:, k * part : (k + 1) * part]


def sum_blocks(terms, cuts, after, name):
    shape = terms[0].shape
    whole = lambda s: pl.BlockSpec(s, lambda i: (0, 0, 0))
    piece = (shape[0], shape[1] // cuts, shape[2])
    return pl.pallas_call(
        functools.partial(sum_kernel, len(terms), cuts),
        grid=(1,),
        in_specs=[whole(shape)] * len(terms) + [pl.BlockSpec(memory_space=pl.ANY)] * len(after),
        out_specs=[whole(piece)] * cuts,
        out_shape=[jax.ShapeDtypeStruct(piece, bf16)] * cuts,
        compiler_params=params(16),
        cost_estimate=pl.CostEstimate(flops=1000, bytes_accessed=1000, transcendentals=0),
        name=name,
    )(*terms, *after)


def stack_kernel(count, *refs):
    rows = refs[0].shape[0]
    for k in range(count):
        refs[-1][k * rows : (k + 1) * rows] = refs[k][...]


def stack_pieces(pieces, after):
    shape = pieces[0].shape
    whole = lambda s: pl.BlockSpec(s, lambda i: (0, 0, 0, 0))
    stacked = (len(pieces) * shape[0],) + shape[1:]
    return pl.pallas_call(
        functools.partial(stack_kernel, len(pieces)),
        grid=(1,),
        in_specs=[whole(shape)] * len(pieces) + [pl.BlockSpec(memory_space=pl.ANY)] * len(after),
        out_specs=whole(stacked),
        out_shape=jax.ShapeDtypeStruct(stacked, bf16),
        compiler_params=params(16),
        cost_estimate=pl.CostEstimate(flops=1000, bytes_accessed=1000, transcendentals=0),
        name="stack_pieces",
    )(*pieces, *after)


class SeqSum:
    def __init__(self, grads, seq_count):
        self.grads, self.seq_count, self.lines = grads, seq_count, seq_count // 4
        self.cross = [(i, i ^ 2) for i in range(seq_count)]
        self.got = [self.to_sibling(g) for g in grads[:2]]
        bits = self.lines.bit_length() - 1
        self.left = [self.over_core, self.over_x]
        self.left += [functools.partial(self.over_line, 1 << k) for k in range(bits)]
        self.left += [functools.partial(self.back_line, 1 << k) for k in reversed(range(bits))]

    def step(self, after):
        return [self.left.pop(0)(after)]

    def to_sibling(self, x):
        return lax.ppermute(x, "seq", sibling_pairs(self.seq_count))

    def to_line(self, x, step):
        return lax.ppermute(x, "seq", line_pairs(self.seq_count, step))

    def over_core(self, after):
        (first,) = sum_blocks([self.grads[2], self.got[0]], 1, after, "sum_core")
        self.crossed = lax.ppermute(first, "seq", self.cross)
        return first

    def over_x(self, after):
        self.kept, sent = sum_blocks([self.grads[3], self.got[1], self.crossed], 2, after, "sum_x")
        self.arriving = self.to_line(sent, 1)
        return sent

    def over_line(self, step, after):
        if 2 * step < self.lines:
            self.kept, sent = sum_blocks([self.kept, self.arriving], 2, after, "sum_line")
            self.arriving = self.to_line(sent, 2 * step)
            return sent
        (shard,) = sum_blocks([self.kept, self.arriving], 1, after, "sum_line")
        self.own = shard[None]
        self.arriving = self.to_line(self.own, step)
        return shard

    def back_line(self, step, after):
        self.own = stack_pieces([self.own, self.arriving], after)
        if step > 1:
            self.arriving = self.to_line(self.own, step // 2)
        else:
            self.other = lax.ppermute(self.own, "seq", self.cross)
        return self.own

    def blocks(self, after):
        other = stack_pieces([self.other], after) if after else self.other
        return [self.own, other, self.to_sibling(self.own), self.to_sibling(other)]


def step_order(sums):
    left = [len(s.left) for s in sums]
    order = []
    while any(left):
        for g in range(len(sums)):
            if left[g]:
                order.append(g)
                left[g] -= 1
    return order


def unpack_kernel(lines, each, width, where, place, *refs):
    win_ref, wout_ref, token_ref = refs[-3:]
    token_ref[...] = jnp.zeros_like(token_ref)
    step = pl.program_id(0)

    def read(ref, i, with_in, with_out):
        for p in range(lines):
            block = ref[place_of(p, place[0], lines), i].astype(f32)
            part, ff = block.shape
            low = p * part
            if with_in and low < width:
                win_ref[0, low : low + part, :] = block
            else:
                low = low - width if with_in else low
                for j in range(ff // width):
                    wout_ref[0, j * width + low : j * width + low + part, :] = block[:, j * width : (j + 1) * width]

    if refs[0].shape[2] * lines > width:
        for a in range(4):
            for i in range(each):
                pl.when(step == a * each + i)(functools.partial(read, refs[a], i, True, True))
    else:
        for k in range(2):
            for column in range(2):

                @pl.when((step == k) & (place[1] == column))
                def _(k=k, column=column):
                    own, other = refs[2 * k], refs[2 * k + 1]
                    read((own, other)[column], 0, True, False)
                    read((other, own)[column], 0, False, True)


def unpack(where, place, blocks, experts, width, ff, into):
    lines, each = blocks[0].shape[:2]
    whole = pl.BlockSpec(blocks[0].shape, lambda i, *_: (0, 0, 0, 0))
    out = lambda *shape: pl.BlockSpec((1,) + shape, lambda i, where, place: (where[i], 0, 0))
    return pl.pallas_call(
        functools.partial(unpack_kernel, lines, each, width),
        grid_spec=pltpu.PrefetchScalarGridSpec(
            num_scalar_prefetch=2,
            grid=where.shape,
            in_specs=[whole] * 4 + [pl.BlockSpec(memory_space=pl.ANY)] * len(into),
            out_specs=[out(width, ff), out(ff, width), pl.BlockSpec((8, 128), lambda i, *_: (0, 0))],
        ),
        out_shape=[
            jax.ShapeDtypeStruct((experts, width, ff), f32),
            jax.ShapeDtypeStruct((experts, ff, width), f32),
            jax.ShapeDtypeStruct((8, 128), f32),
        ],
        input_output_aliases={6 + i: i for i in range(len(into))},
        compiler_params=params(16),
        cost_estimate=pl.CostEstimate(
            flops=EAGER * where.shape[0] * 2 * width * ff * 6, bytes_accessed=where.shape[0] * 2 * width * ff * 6, transcendentals=0
        ),
        name="unpack",
    )(where, place, *blocks, *into)


def shards(
    query_cols,
    key_cols,
    value_cols,
    block_list,
    residual,
    out_proj,
    norm_gain,
    router_weight,
    expert_ids,
    expert_in,
    expert_out,
    cotangent,
):
    seq_count = lax.axis_size("seq")
    exp_count = lax.axis_size("expert")
    me = lax.axis_index("expert")
    feat, nodes = query_cols.shape
    blk_seq, degree = block_list.shape
    block_len = nodes // blk_seq
    tok_dev, width = residual.shape
    expert_total = router_weight.shape[1]
    experts = expert_in.shape[0]
    ff = expert_in.shape[2]
    topk = expert_ids.shape[1]
    chunk = min(256, tok_dev)
    capacity = 2 * tok_dev * topk // expert_total * exp_count
    slot_rows = capacity + WINDOW

    calls = 2 if blk_seq % 2 == 0 else 1
    keys, values = ring_gather(key_cols, value_cols, seq_count)
    tables = block_tables(block_list, blk_seq, seq_count, calls)

    residual_all = gather_expert_axis(residual, exp_count)
    cotangent_all = gather_expert_axis(cotangent, exp_count)
    ids_all = gather_expert_axis(expert_ids.T, exp_count, 1)
    gain = norm_gain.reshape(1, width)
    core, column, line = seq_place()
    lines = seq_count // 4
    place = jnp.stack([line, column]).astype(jnp.int32)
    groups = [4] * (experts // 4)
    groups += [2] * ((experts - sum(groups)) // 2)
    dests = [(1 - core, 1 - column), (1 - core, column), (core, 1 - column), (core, column)]
    perm, wheres, first = [], [], 0
    for count in groups:
        if count == 4:
            perm += [first + 2 * c + x for c, x in dests]
            wheres.append([first + 2 * c + x for c, x in (dests[3], dests[2], dests[1], dests[0])])
        else:
            perm += [first + 1 - core, first + core]
            wheres.append([first + core, first + 1 - core])
        first += count
    perm = jnp.stack(perm).astype(jnp.int32)
    wheres = [jnp.stack(w).astype(jnp.int32) for w in wheres]
    local_ids = me * experts + perm
    hot = jnp.sum((ids_all[None, :, :] == local_ids[:, None, None]).astype(jnp.int32), 1)
    running = jnp.cumsum(hot, 1)
    rank = jnp.where(hot > 0, running - 1, -(1 << 20))
    ends = running[:, chunk - 1 :: chunk]
    starts = jnp.concatenate([jnp.zeros((experts, 1), jnp.int32), ends], 1).T
    counts = running[:, -1]
    router = jnp.pad(router_weight, ((0, 0), (0, -expert_total % 128)))
    columns = lax.dynamic_slice_in_dim(router_weight.T, me * experts, experts, 0).astype(f32).reshape(experts, 1, width)
    projs = [
        lax.dynamic_slice_in_dim(out_proj, lax.rem(me + exp_count - d, exp_count) * feat, feat, 0)
        for d in range(exp_count)
    ]
    owner_order = lax.rem(me + jnp.arange(exp_count, dtype=jnp.int32), exp_count)

    per_call = blk_seq // calls
    pieces = [[] for _ in range(exp_count)]
    for c in range(calls):
        part = attention(query_cols, keys, values, tables, c, per_call, block_len, degree)
        pieces[0].append(part)
        for d in range(1, exp_count):
            pieces[d].append(lax.ppermute(part, "expert", shift_pairs(exp_count, d)))
    atts = [jnp.concatenate(p, 0) for p in pieces]

    scalars = (counts, local_ids, perm, starts, owner_order, place)
    common = (rank, cotangent_all, gain, router)
    weights = (expert_in, expert_out, columns)
    sums, last, stream, partials, first = [], [], None, None, 0
    for g, count in enumerate(groups):
        head = (residual_all, atts, projs) if g == 0 else None
        found = list(expert_group(scalars, common, weights, first, count, head, (stream, partials, last), lines, slot_rows, chunk))
        first += count
        if g == 0:
            stream = found.pop(0)
        partials, grads = found[:exp_count], found[exp_count:]
        sums.append(SeqSum(grads, seq_count))
        if g == 0:
            last = sums[0].step(last)
    parts = partials[:1] + [lax.ppermute(partials[d], "expert", shift_pairs(exp_count, d)) for d in range(1, exp_count)]
    steps = step_order(sums)
    for k, g in enumerate(steps):
        last = sums[g].step(last)
        if k == len(steps) // 2:
            layer_out, grad_stream = at_home(me, stream, cotangent, gain, parts, chunk, last[0])
            last = [layer_out]
    into, token = [], []
    for g, each_sum in enumerate(sums):
        blocks = each_sum.blocks(token if g == len(sums) - 1 else [])
        *into, done = unpack(wheres[g], place, blocks, experts, width, ff, into)
        token = [done]
    grad_w_in, grad_w_out = into
    return layer_out, grad_stream, grad_w_in, grad_w_out


def solution(mesh):
    return jax.shard_map(
        shards,
        mesh=mesh,
        in_specs=(
            P("expert", "seq"),
            P("expert", "seq"),
            P("expert", "seq"),
            P("seq", None),
            P(("seq", "expert"), None),
            P(),
            P(),
            P(),
            P(("seq", "expert"), None),
            P("expert", None, None),
            P("expert", None, None),
            P(("seq", "expert"), None),
        ),
        out_specs=(
            P(("seq", "expert"), None),
            P(("seq", "expert"), None),
            P("expert", None, None),
            P("expert", None, None),
        ),
        check_vma=False,
    )
```

```python
import functools
import math

import jax
import jax.numpy as jnp
from jax import lax
from jax.experimental import pallas as pl
from jax.experimental.pallas import tpu as pltpu
from jax.sharding import PartitionSpec as P

HD = 32
WINDOW = 128
TILE = 256
EAGER = 32

norm_eps = 1e-05
root_two_pi = 0.7978845608028654
cubic_term = 0.044715

bf16 = jnp.bfloat16
f32 = jnp.float32


def params(mebibytes=32):
    return pltpu.CompilerParams(vmem_limit_bytes=mebibytes * 1024 * 1024)


def contract(a, b, da, db):
    return lax.dot_general(a, b, (((da,), (db,)), ((), ())), preferred_element_type=f32)


def ring_order(seq_count):
    rows = max(1, seq_count // 4)
    if seq_count % 4:
        return list(range(seq_count // 2))
    return [2 * z for z in range(rows)] + [2 * z + 1 for z in reversed(range(rows))]


def ring_pairs(seq_count, step):
    order = ring_order(seq_count)
    n = len(order)
    return [(2 * order[i] + c, 2 * order[(i + step) % n] + c) for i in range(n) for c in range(2)]


def sibling_pairs(seq_count):
    return [(s, s ^ 1) for s in range(seq_count)]


def shift_pairs(count, d):
    return [(i, (i + d) % count) for i in range(count)]


def gather_expert_axis(x, exp_count, axis=0):
    me = lax.axis_index("expert")
    size = x.shape[axis]
    shape = list(x.shape)
    shape[axis] = size * exp_count
    out = jnp.zeros(shape, x.dtype)
    out = lax.dynamic_update_slice_in_dim(out, x, me * size, axis)
    for d in range(1, exp_count):
        got = lax.ppermute(x, "expert", shift_pairs(exp_count, d))
        out = lax.dynamic_update_slice_in_dim(out, got, lax.rem(me + exp_count - d, exp_count) * size, axis)
    return out


def ring_gather(keys, values, seq_count):
    n = seq_count // 2
    fwd, bwd, sib = ring_pairs(seq_count, 1), ring_pairs(seq_count, -1), sibling_pairs(seq_count)
    k, v = keys, values
    own, other = ([], []), ([], [])
    for t in range(n):
        if t > 0:
            k = lax.ppermute(k, "seq", fwd)
            v = lax.ppermute(v, "seq", bwd)
        own[0].append(k)
        own[1].append(v)
        other[0].append(lax.ppermute(k, "seq", sib))
        other[1].append(lax.ppermute(v, "seq", sib))
    return own[0] + other[0], own[1] + other[1]


def sorted_entries(slot, slots):
    count = slot.shape[-1]
    at = jnp.arange(count, dtype=jnp.int32)
    before = (slot[:, None, :] < slot[:, :, None]) | ((slot[:, None, :] == slot[:, :, None]) & (at[None, None, :] < at[None, :, None]))
    rank = jnp.sum(before.astype(jnp.int32), 2)
    order = jnp.sum(jnp.where(rank[:, None, :] == at[None, :, None], at[None, None, :], 0), 2)
    begin = jnp.sum((slot[:, None, :] < jnp.arange(slots + 1, dtype=jnp.int32)[None, :, None]).astype(jnp.int32), 2)
    return order, begin


def block_tables(block_list, blk_seq, seq_count, calls):
    order = ring_order(seq_count)
    n = len(order)
    inverse = [0] * n
    for i, chip in enumerate(order):
        inverse[chip] = i
    inverse = jnp.asarray(inverse, jnp.int32)
    me = lax.axis_index("seq")
    place = inverse[me // 2]
    owner = block_list // blk_seq
    local = (block_list % blk_seq).reshape(calls, -1)
    other = inverse[owner // 2]
    flag = ((owner ^ me) & 1) * n
    kslot = (flag + lax.rem(place - other + n, n)).reshape(calls, -1)
    vslot = (flag + lax.rem(other - place + n, n)).reshape(calls, -1)
    return (local,) + sorted_entries(kslot, 2 * n) + sorted_entries(vslot, 2 * n)


def attention_kernel(degree, heads, sources, local, korder, kbegin, vorder, vbegin, q_ref, *refs):
    k_refs, v_refs = refs[:sources], refs[sources : 2 * sources]
    out_ref, k_all, v_all, sems = refs[2 * sources :]
    block_len = k_all.shape[2] // degree

    def fetch(source, dest, order, begin, s, sem):
        def one(r, carry):
            e = order[r]
            at = pl.ds(pl.multiple_of(local[e] * block_len, block_len), block_len)
            to = pl.ds(pl.multiple_of(lax.rem(e, degree) * block_len, block_len), block_len)
            pltpu.make_async_copy(source.at[:, at], dest.at[lax.div(e, degree), :, to], sem).start()
            return carry

        lax.fori_loop(begin[s], begin[s + 1], one, 0)

    for s in range(sources):
        fetch(k_refs[s], k_all, korder, kbegin, s, sems.at[0])
    for s in range(sources):
        fetch(v_refs[s], v_all, vorder, vbegin, s, sems.at[1])
    pltpu.make_async_copy(k_all, k_all, sems.at[0]).wait()
    pltpu.make_async_copy(v_all, v_all, sems.at[1]).wait()
    factor = math.log2(math.e) / math.sqrt(HD)

    feat = heads * HD
    head_row = lax.broadcasted_iota(jnp.int32, (feat, heads * block_len), 0) // HD
    head_col = lax.broadcasted_iota(jnp.int32, (feat, heads * block_len), 1) // block_len
    diagonal = head_row == head_col

    def one_block(b, carry):
        nodes = pl.ds(pl.multiple_of(b * block_len, block_len), block_len)
        q = jnp.concatenate([q_ref[:, nodes]] * heads, 1)
        scores = contract(k_all[b], jnp.where(diagonal, q, jnp.zeros_like(q)), 0, 0)
        top = jnp.max(scores, 0, keepdims=True)
        probs = jnp.exp2((scores - top) * factor)
        total = jnp.sum(probs, 0, keepdims=True)
        probs = probs.astype(bf16)
        cols = []
        for h in range(heads):
            rows, own = slice(h * HD, (h + 1) * HD), slice(h * block_len, (h + 1) * block_len)
            cols.append(jnp.dot(v_all[b, rows, :], probs[:, own], preferred_element_type=f32) / total[:, own])
        out_ref[nodes, :] = jnp.concatenate(cols, 0).T.astype(bf16)
        return carry

    count = k_all.shape[0]
    lax.fori_loop(0, count, one_block, 0, unroll=4 if count % 4 == 0 else 1)


def attention(queries, keys, values, tables, call, count, block_len, degree):
    feat = queries.shape[0]
    return pl.pallas_call(
        functools.partial(attention_kernel, degree, feat // HD, len(keys)),
        grid_spec=pltpu.PrefetchScalarGridSpec(
            num_scalar_prefetch=5,
            grid=(1,),
            in_specs=[pl.BlockSpec((feat, count * block_len), lambda i, *_: (0, call))]
            + [pl.BlockSpec(memory_space=pl.ANY)] * (2 * len(keys)),
            out_specs=pl.BlockSpec((count * block_len, feat), lambda i, *_: (0, 0)),
            scratch_shapes=[pltpu.VMEM((count, feat, degree * block_len), bf16)] * 2 + [pltpu.SemaphoreType.DMA((2,))],
        ),
        out_shape=jax.ShapeDtypeStruct((count * block_len, feat), bf16),
        compiler_params=params(56),
        cost_estimate=pl.CostEstimate(
            flops=4 * count * block_len * degree * block_len * feat,
            bytes_accessed=2 * count * feat * block_len * (2 * degree + 2),
            transcendentals=count * block_len * degree * block_len * feat // HD,
        ),
        name="attention",
    )(*[t[call] for t in tables], queries, *keys, *values)


def place_of(part, line, lines):
    differ = jnp.bitwise_xor(part, line)
    place = 0
    step = 1
    while step < lines:
        place = place * 2 + jnp.bitwise_and(lax.div(differ, step), 1)
        step *= 2
    return place


def window_base(starts, i, e):
    return pl.multiple_of((starts[i, e] // 16) * 16, 16)


def further_windows(starts, i, e):
    left = starts[i + 1, e] - window_base(starts, i, e)
    return jnp.maximum((left + WINDOW - 1) // WINDOW, 1)


def any_further(starts, i, first, count):
    most = further_windows(starts, i, first)
    for e in range(first + 1, first + count):
        most = jnp.maximum(most, further_windows(starts, i, e))
    return most > 1


def one_hot(rank_row, base):
    place = lax.broadcasted_iota(jnp.int32, (WINDOW, rank_row.shape[1]), 0)
    return jnp.where(place == rank_row - base, 1.0, 0.0).astype(bf16)


def stack_hot(starts, rank, i, first, count):
    return jnp.concatenate([one_hot(rank[e : e + 1, :], window_base(starts, i, e)) for e in range(first, first + count)], 0)


def group_kernel(first, count, pieces, after, chunk, lines, counts, ids, perm, starts, place, *refs):
    refs = list(refs)
    rank_ref, cot_ref, gain_ref, router_ref, win_ref, wout_ref, rcol_ref = [refs.pop(0) for _ in range(7)]
    if pieces:
        res_ref = refs.pop(0)
        atts = [refs.pop(0) for _ in range(pieces)]
        projs = [refs.pop(0) for _ in range(pieces)]
        stream_ref = None
    else:
        stream_ref = refs.pop(0)
        del refs[:after]
    if pieces:
        out_stream = refs.pop(0)
    out_rows = refs.pop(0)
    grad_refs, (rows_ref, slots, acc_in, acc_out) = refs[:-4], refs[-4:]
    nodes, width = cot_ref.shape
    step = pl.program_id(0)

    @pl.when(step == 0)
    def _():
        slots[...] = jnp.zeros_like(slots)

        def dispatch(i, carry):
            at = pl.ds(pl.multiple_of(i * chunk, chunk), chunk)
            if pieces:
                projected = jnp.dot(atts[0][at, :], projs[0][...], preferred_element_type=f32)
                for a, w in zip(atts[1:], projs[1:]):
                    projected = projected + jnp.dot(a[at, :], w[...], preferred_element_type=f32)
                stream = (res_ref[at, :].astype(f32) + projected).astype(bf16)
                out_stream[at, :] = stream
            else:
                stream = stream_ref[at, :]
            wide = stream.astype(f32)
            inverse_rms = lax.rsqrt(jnp.mean(wide * wide, -1, keepdims=True) + norm_eps)
            rows_ref[:, :width] = (wide * inverse_rms * gain_ref[...]).astype(bf16)
            rows_ref[:, width:] = cot_ref[at, :]
            rank = rank_ref[:, at]
            packed = jnp.dot(stack_hot(starts, rank, i, first, count), rows_ref[...], preferred_element_type=f32).astype(bf16)
            for e in range(count):
                to = pl.ds(window_base(starts, i, first + e), WINDOW)
                slots[e, to, :] = slots[e, to, :] + packed[e * WINDOW : (e + 1) * WINDOW]

            @pl.when(any_further(starts, i, first, count))
            def _():
                for e in range(count):

                    def more(w, carry, e=e):
                        base = pl.multiple_of(window_base(starts, i, first + e) + w * WINDOW, 16)
                        hot = one_hot(rank[first + e : first + e + 1, :], base)
                        got = jnp.dot(hot, rows_ref[...], preferred_element_type=f32)
                        to = pl.ds(base, WINDOW)
                        slots[e, to, :] = slots[e, to, :] + got.astype(bf16)
                        return carry

                    lax.fori_loop(1, further_windows(starts, i, first + e), more, 0)

            return carry

        lax.fori_loop(0, nodes // chunk, dispatch, 0)

    e = step + first
    tiles = (counts[e] + TILE - 1) // TILE
    acc_in[...] = jnp.zeros_like(acc_in)
    acc_out[...] = jnp.zeros_like(acc_out)
    w_in = win_ref[0]
    w_out = wout_ref[0]
    mine = lax.broadcasted_iota(jnp.int32, (TILE, router_ref.shape[1]), 1) == ids[e]
    column = rcol_ref[0]

    def one(t, carry):
        at = pl.ds(pl.multiple_of(t * TILE, TILE), TILE)
        x = slots[step, at, :width]
        cot = slots[step, at, width:]
        cot_wide = cot.astype(f32)
        logits = jnp.dot(x, router_ref[...], preferred_element_type=f32)
        logit = jnp.sum(jnp.where(mine, logits, 0.0), 1, keepdims=True)
        gate = 1.0 / (1.0 + jnp.exp(-logit))
        scaled = (gate * cot_wide).astype(bf16)
        a = jnp.dot(x, w_in, preferred_element_type=f32)
        grad_hidden = contract(scaled, w_out, 1, 1)
        a2 = a * a
        t1 = jnp.tanh(a * (root_two_pi + (root_two_pi * cubic_term) * a2))
        half = 0.5 + 0.5 * t1
        hidden = (a * half).astype(bf16)
        slope = half + (a * (1.0 - t1 * t1)) * (0.5 * root_two_pi + (1.5 * root_two_pi * cubic_term) * a2)
        grad_pre = (grad_hidden * slope).astype(bf16)
        acc_out[...] += contract(hidden, scaled, 0, 0)
        acc_in[...] += contract(x, grad_pre, 0, 0)
        produced = jnp.dot(hidden, w_out, preferred_element_type=f32).astype(bf16).astype(f32)
        grad_rows = contract(grad_pre, w_in, 1, 1).astype(bf16).astype(f32)
        grad_logit = jnp.sum(cot_wide * produced, 1, keepdims=True) * gate * (1.0 - gate)
        out_rows[0, at, :width] = (gate * produced).astype(bf16)
        out_rows[0, at, width:] = (grad_rows + grad_logit * column).astype(bf16)
        return carry

    lax.fori_loop(0, tiles, one, 0)

    def blank(t, carry):
        at = pl.ds(pl.multiple_of(t * WINDOW, WINDOW), WINDOW)
        out_rows[0, at, :] = jnp.zeros((WINDOW, 2 * width), bf16)
        return carry

    lax.fori_loop(tiles * TILE // WINDOW, out_rows.shape[1] // WINDOW, blank, 0)

    ff = acc_in.shape[1]

    def write(grad_ref, with_in, with_out):
        part = grad_ref.shape[1] // lines
        for p in range(lines):
            at = pl.ds(pl.multiple_of(place_of(p, place[0], lines) * part, part), part)
            low = p * part
            if with_in and low < width:
                grad_ref[0, at, :] = acc_in[low : low + part, :].astype(bf16)
            else:
                low = low - width if with_in else low
                for j in range(ff // width):
                    cols = slice(j * width, (j + 1) * width)
                    grad_ref[0, at, cols] = acc_out[j * width + low : j * width + low + part, :].astype(bf16)

    if count > 2:
        each = count // 4
        for k, grad_ref in enumerate(grad_refs):
            pl.when((step >= k * each) & (step < (k + 1) * each))(functools.partial(write, grad_ref, True, True))
    else:
        for k in range(2):
            for column in range(2):

                @pl.when((step == k) & (place[1] == column))
                def _(k=k, column=column):
                    other, own = grad_refs[2 * k], grad_refs[2 * k + 1]
                    write((own, other)[column], True, False)
                    write((other, own)[column], False, True)


def expert_group(scalars, common, weights, first, count, head, tail, lines, slot_rows, chunk):
    counts, ids, perm, starts, place = scalars
    rank, cotangent, gain, router = common
    w_in, w_out, columns = weights
    nodes, width = cotangent.shape
    ff = w_in.shape[2]
    whole = lambda a: pl.BlockSpec(a.shape, lambda i, *_: (0,) * a.ndim)
    listed = lambda *shape: pl.BlockSpec((1,) + shape, lambda i, c, d, perm, *_: (perm[i + first], 0, 0))
    args = [rank, cotangent, gain, router, w_in, w_out, columns]
    specs = [whole(a) for a in args[:4]] + [listed(width, ff), listed(ff, width), listed(1, width)]
    out_shape, out_specs = [], []
    if head:
        residual, atts, projs = head
        extra = [residual, *atts, *projs]
        specs += [whole(a) for a in extra]
        out_shape.append(jax.ShapeDtypeStruct((nodes, width), bf16))
        pieces = len(atts)
    else:
        stream, after = tail
        extra = [stream, *after]
        specs += [whole(stream)] + [pl.BlockSpec(memory_space=pl.ANY)] * len(after)
        pieces = 0
    out_specs = [pl.BlockSpec(o.shape, lambda i, *_: (0, 0)) for o in out_shape]
    out_shape.append(jax.ShapeDtypeStruct((count, slot_rows, 2 * width), bf16))
    out_specs.append(pl.BlockSpec((1, slot_rows, 2 * width), lambda i, *_: (i, 0, 0)))
    each = max(1, count // 4)
    block = (1, 2 * width if count > 2 else width, ff)
    out_shape += [jax.ShapeDtypeStruct((each,) + block[1:], bf16)] * 4
    for k in range(4):
        first_step = k * each if count > 2 else k // 2
        out_specs.append(pl.BlockSpec(block, lambda i, *_, at=first_step: (jnp.clip(i - at, 0, each - 1), 0, 0)))
    return pl.pallas_call(
        functools.partial(group_kernel, first, count, pieces, 0 if head else len(after), chunk, lines),
        grid_spec=pltpu.PrefetchScalarGridSpec(
            num_scalar_prefetch=5,
            grid=(count,),
            in_specs=specs,
            out_specs=out_specs,
            scratch_shapes=[
                pltpu.VMEM((chunk, 2 * width), bf16),
                pltpu.VMEM((count, slot_rows, 2 * width), bf16),
                pltpu.VMEM((width, ff), f32),
                pltpu.VMEM((ff, width), f32),
            ],
        ),
        out_shape=out_shape,
        compiler_params=params(),
        cost_estimate=pl.CostEstimate(flops=1000, bytes_accessed=1000, transcendentals=0),
        name="experts",
    )(counts, ids, perm, starts, place, *args, *extra)


def combine_kernel(parts, owners, chunk, starts, order, rank_ref, *refs):
    rows_refs, out_refs = refs[:parts], refs[len(refs) - owners :]
    held = [(r, j) for r in rows_refs for j in range(r.shape[0])]
    experts = len(held)
    chunks = out_refs[0].shape[0] // chunk

    for d in range(owners):

        def gather(c, carry, d=d):
            i = order[d] * chunks + c
            rank = rank_ref[:, pl.ds(pl.multiple_of(i * chunk, chunk), chunk)]
            windows = [r[j, pl.ds(window_base(starts, i, e), WINDOW), :] for e, (r, j) in enumerate(held)]
            total = contract(stack_hot(starts, rank, i, 0, experts), jnp.concatenate(windows, 0), 0, 0)

            def further(total):
                for e, (r, j) in enumerate(held):

                    def more(w, acc, e=e, r=r, j=j):
                        base = pl.multiple_of(window_base(starts, i, e) + w * WINDOW, 16)
                        return acc + contract(one_hot(rank[e : e + 1, :], base), r[j, pl.ds(base, WINDOW), :], 0, 0)

                    total = lax.fori_loop(1, further_windows(starts, i, e), more, total)
                return total

            total = lax.cond(any_further(starts, i, 0, experts), further, lambda total: total, total)
            out_refs[d][pl.ds(pl.multiple_of(c * chunk, chunk), chunk), :] = total.astype(bf16)
            return carry

        lax.fori_loop(0, chunks, gather, 0)


def combine(starts, order, rank, rows_parts, chunk, after):
    owners = order.shape[0]
    nodes, double = rank.shape[1], rows_parts[0].shape[2]
    whole = lambda a: pl.BlockSpec(a.shape, lambda i, *_: (0,) * a.ndim)
    out = jax.ShapeDtypeStruct((nodes // owners, double), bf16)
    return pl.pallas_call(
        functools.partial(combine_kernel, len(rows_parts), owners, chunk),
        grid_spec=pltpu.PrefetchScalarGridSpec(
            num_scalar_prefetch=2,
            grid=(1,),
            in_specs=[whole(rank)] + [whole(r) for r in rows_parts] + [pl.BlockSpec(memory_space=pl.ANY)] * len(after),
            out_specs=[whole(out)] * owners,
        ),
        out_shape=[out] * owners,
        compiler_params=params(),
        cost_estimate=pl.CostEstimate(flops=EAGER * 10**9, bytes_accessed=10**7, transcendentals=0),
        name="combine",
    )(starts, order, rank, *rows_parts, *after)


def home_kernel(parts, stream_ref, cot_ref, gain_ref, *refs):
    layer_ref, grad_ref, token_ref = refs[parts:]
    token_ref[...] = jnp.zeros_like(token_ref)
    total = refs[0][...].astype(f32)
    for g in refs[1:parts]:
        total = total + g[...].astype(f32)
    width = stream_ref.shape[1]
    stream = stream_ref[...].astype(f32)
    inverse_rms = lax.rsqrt(jnp.mean(stream * stream, -1, keepdims=True) + norm_eps)
    layer_ref[...] = (stream + total[:, :width]).astype(bf16)
    gained = total[:, width:] * gain_ref[...]
    mean = jnp.mean(stream * gained, -1, keepdims=True)
    grad = cot_ref[...].astype(f32) + inverse_rms * gained - stream * (inverse_rms * inverse_rms * inverse_rms) * mean
    grad_ref[...] = grad.astype(bf16)


def at_home(me, stream, cotangent, gain, parts, chunk, after):
    tok_dev, width = cotangent.shape
    steps = tok_dev // chunk
    fresh = lambda w: pl.BlockSpec((chunk, w), lambda i, me: (i, 0))
    return pl.pallas_call(
        lambda me, *refs: home_kernel(len(parts), *refs[:-4], *refs[-3:]),
        grid_spec=pltpu.PrefetchScalarGridSpec(
            num_scalar_prefetch=1,
            grid=(steps,),
            in_specs=[
                pl.BlockSpec((chunk, width), lambda i, me: (me[0] * steps + i, 0)),
                fresh(width),
                pl.BlockSpec(gain.shape, lambda i, me: (0, 0)),
            ]
            + [fresh(2 * width) for _ in parts]
            + [pl.BlockSpec(memory_space=pl.ANY)],
            out_specs=[fresh(width), fresh(width), pl.BlockSpec((8, 128), lambda i, me: (0, 0))],
        ),
        out_shape=[jax.ShapeDtypeStruct((tok_dev, width), bf16)] * 2 + [jax.ShapeDtypeStruct((8, 128), f32)],
        compiler_params=params(),
        cost_estimate=pl.CostEstimate(
            flops=EAGER * tok_dev * width * 1000, bytes_accessed=tok_dev * width * 16, transcendentals=0
        ),
        name="at_home",
    )(me.reshape(1), stream, cotangent, gain, *parts, after)


def line_pairs(seq_count, d):
    return [(z * 4 + r, (z ^ d) * 4 + r) for z in range(seq_count // 4) for r in range(4)]


def seq_place():
    s = lax.axis_index("seq")
    return s % 2, (s // 2) % 2, s // 4


def sum_kernel(terms, cuts, *refs):
    total = refs[0][...].astype(f32)
    for r in refs[1:terms]:
        total = total + r[...].astype(f32)
    total = total.astype(bf16)
    part = total.shape[1] // cuts
    for k, out in enumerate(refs[len(refs) - cuts :]):
        out[...] = total[:, k * part : (k + 1) * part]


def sum_blocks(terms, cuts, after, name):
    shape = terms[0].shape
    whole = lambda s: pl.BlockSpec(s, lambda i: (0, 0, 0))
    piece = (shape[0], shape[1] // cuts, shape[2])
    return pl.pallas_call(
        functools.partial(sum_kernel, len(terms), cuts),
        grid=(1,),
        in_specs=[whole(shape)] * len(terms) + [pl.BlockSpec(memory_space=pl.ANY)] * len(after),
        out_specs=[whole(piece)] * cuts,
        out_shape=[jax.ShapeDtypeStruct(piece, bf16)] * cuts,
        compiler_params=params(16),
        cost_estimate=pl.CostEstimate(flops=1000, bytes_accessed=1000, transcendentals=0),
        name=name,
    )(*terms, *after)


def stack_kernel(count, *refs):
    rows = refs[0].shape[0]
    for k in range(count):
        refs[-1][k * rows : (k + 1) * rows] = refs[k][...]


def stack_pieces(pieces, after):
    shape = pieces[0].shape
    whole = lambda s: pl.BlockSpec(s, lambda i: (0, 0, 0, 0))
    stacked = (len(pieces) * shape[0],) + shape[1:]
    return pl.pallas_call(
        functools.partial(stack_kernel, len(pieces)),
        grid=(1,),
        in_specs=[whole(shape)] * len(pieces) + [pl.BlockSpec(memory_space=pl.ANY)] * len(after),
        out_specs=whole(stacked),
        out_shape=jax.ShapeDtypeStruct(stacked, bf16),
        compiler_params=params(16),
        cost_estimate=pl.CostEstimate(flops=1000, bytes_accessed=1000, transcendentals=0),
        name="stack_pieces",
    )(*pieces, *after)


class SeqSum:
    def __init__(self, grads, seq_count):
        self.grads, self.seq_count, self.lines = grads, seq_count, seq_count // 4
        self.cross = [(i, i ^ 2) for i in range(seq_count)]
        self.got = [self.to_sibling(g) for g in grads[:2]]
        bits = self.lines.bit_length() - 1
        self.left = [self.over_core, self.over_x]
        self.left += [functools.partial(self.over_line, 1 << k) for k in range(bits)]
        self.left += [functools.partial(self.back_line, 1 << k) for k in reversed(range(bits))]

    def step(self, after):
        return [self.left.pop(0)(after)]

    def to_sibling(self, x):
        return lax.ppermute(x, "seq", sibling_pairs(self.seq_count))

    def to_line(self, x, step):
        return lax.ppermute(x, "seq", line_pairs(self.seq_count, step))

    def over_core(self, after):
        (first,) = sum_blocks([self.grads[2], self.got[0]], 1, after, "sum_core")
        self.crossed = lax.ppermute(first, "seq", self.cross)
        return first

    def over_x(self, after):
        self.kept, sent = sum_blocks([self.grads[3], self.got[1], self.crossed], 2, after, "sum_x")
        self.arriving = self.to_line(sent, 1)
        return sent

    def over_line(self, step, after):
        if 2 * step < self.lines:
            self.kept, sent = sum_blocks([self.kept, self.arriving], 2, after, "sum_line")
            self.arriving = self.to_line(sent, 2 * step)
            return sent
        (shard,) = sum_blocks([self.kept, self.arriving], 1, after, "sum_line")
        self.own = shard[None]
        self.arriving = self.to_line(self.own, step)
        return shard

    def back_line(self, step, after):
        self.own = stack_pieces([self.own, self.arriving], after)
        if step > 1:
            self.arriving = self.to_line(self.own, step // 2)
        else:
            self.other = lax.ppermute(self.own, "seq", self.cross)
        return self.own

    def blocks(self, after):
        other = stack_pieces([self.other], after) if after else self.other
        return [self.own, other, self.to_sibling(self.own), self.to_sibling(other)]


def step_order(sums):
    left = [len(s.left) for s in sums]
    order = []
    while any(left):
        for g in range(len(sums)):
            if left[g]:
                order.append(g)
                left[g] -= 1
    return order


def unpack_kernel(lines, each, width, where, place, *refs):
    win_ref, wout_ref, token_ref = refs[-3:]
    token_ref[...] = jnp.zeros_like(token_ref)
    step = pl.program_id(0)

    def read(ref, i, with_in, with_out):
        for p in range(lines):
            block = ref[place_of(p, place[0], lines), i].astype(f32)
            part, ff = block.shape
            low = p * part
            if with_in and low < width:
                win_ref[0, low : low + part, :] = block
            else:
                low = low - width if with_in else low
                for j in range(ff // width):
                    wout_ref[0, j * width + low : j * width + low + part, :] = block[:, j * width : (j + 1) * width]

    if refs[0].shape[2] * lines > width:
        for a in range(4):
            for i in range(each):
                pl.when(step == a * each + i)(functools.partial(read, refs[a], i, True, True))
    else:
        for k in range(2):
            for column in range(2):

                @pl.when((step == k) & (place[1] == column))
                def _(k=k, column=column):
                    own, other = refs[2 * k], refs[2 * k + 1]
                    read((own, other)[column], 0, True, False)
                    read((other, own)[column], 0, False, True)


def unpack(where, place, blocks, experts, width, ff, into):
    lines, each = blocks[0].shape[:2]
    whole = pl.BlockSpec(blocks[0].shape, lambda i, *_: (0, 0, 0, 0))
    out = lambda *shape: pl.BlockSpec((1,) + shape, lambda i, where, place: (where[i], 0, 0))
    return pl.pallas_call(
        functools.partial(unpack_kernel, lines, each, width),
        grid_spec=pltpu.PrefetchScalarGridSpec(
            num_scalar_prefetch=2,
            grid=where.shape,
            in_specs=[whole] * 4 + [pl.BlockSpec(memory_space=pl.ANY)] * len(into),
            out_specs=[out(width, ff), out(ff, width), pl.BlockSpec((8, 128), lambda i, *_: (0, 0))],
        ),
        out_shape=[
            jax.ShapeDtypeStruct((experts, width, ff), f32),
            jax.ShapeDtypeStruct((experts, ff, width), f32),
            jax.ShapeDtypeStruct((8, 128), f32),
        ],
        input_output_aliases={6 + i: i for i in range(len(into))},
        compiler_params=params(16),
        cost_estimate=pl.CostEstimate(
            flops=EAGER * where.shape[0] * 2 * width * ff * 6, bytes_accessed=where.shape[0] * 2 * width * ff * 6, transcendentals=0
        ),
        name="unpack",
    )(where, place, *blocks, *into)


def shards(
    query_cols,
    key_cols,
    value_cols,
    block_list,
    residual,
    out_proj,
    norm_gain,
    router_weight,
    expert_ids,
    expert_in,
    expert_out,
    cotangent,
):
    seq_count = lax.axis_size("seq")
    exp_count = lax.axis_size("expert")
    me = lax.axis_index("expert")
    feat, nodes = query_cols.shape
    blk_seq, degree = block_list.shape
    block_len = nodes // blk_seq
    tok_dev, width = residual.shape
    expert_total = router_weight.shape[1]
    experts = expert_in.shape[0]
    ff = expert_in.shape[2]
    topk = expert_ids.shape[1]
    chunk = min(256, tok_dev)
    capacity = 2 * tok_dev * topk // expert_total * exp_count
    slot_rows = capacity + WINDOW

    calls = 2 if blk_seq % 2 == 0 else 1
    keys, values = ring_gather(key_cols, value_cols, seq_count)
    tables = block_tables(block_list, blk_seq, seq_count, calls)

    residual_all = gather_expert_axis(residual, exp_count)
    cotangent_all = gather_expert_axis(cotangent, exp_count)
    ids_all = gather_expert_axis(expert_ids.T, exp_count, 1)
    gain = norm_gain.reshape(1, width)
    core, column, line = seq_place()
    lines = seq_count // 4
    place = jnp.stack([line, column]).astype(jnp.int32)
    groups = [4] * (experts // 4)
    groups += [2] * ((experts - sum(groups)) // 2)
    dests = [(1 - core, 1 - column), (1 - core, column), (core, 1 - column), (core, column)]
    perm, wheres, first = [], [], 0
    for count in groups:
        if count == 4:
            perm += [first + 2 * c + x for c, x in dests]
            wheres.append([first + 2 * c + x for c, x in (dests[3], dests[2], dests[1], dests[0])])
        else:
            perm += [first + 1 - core, first + core]
            wheres.append([first + core, first + 1 - core])
        first += count
    perm = jnp.stack(perm).astype(jnp.int32)
    wheres = [jnp.stack(w).astype(jnp.int32) for w in wheres]
    local_ids = me * experts + perm
    hot = jnp.sum((ids_all[None, :, :] == local_ids[:, None, None]).astype(jnp.int32), 1)
    running = jnp.cumsum(hot, 1)
    rank = jnp.where(hot > 0, running - 1, -(1 << 20))
    ends = running[:, chunk - 1 :: chunk]
    starts = jnp.concatenate([jnp.zeros((experts, 1), jnp.int32), ends], 1).T
    counts = running[:, -1]
    router = jnp.pad(router_weight, ((0, 0), (0, -expert_total % 128)))
    columns = lax.dynamic_slice_in_dim(router_weight.T, me * experts, experts, 0).astype(f32).reshape(experts, 1, width)
    projs = [
        lax.dynamic_slice_in_dim(out_proj, lax.rem(me + exp_count - d, exp_count) * feat, feat, 0)
        for d in range(exp_count)
    ]
    owner_order = lax.rem(me + jnp.arange(exp_count, dtype=jnp.int32), exp_count)

    per_call = blk_seq // calls
    pieces = [[] for _ in range(exp_count)]
    for c in range(calls):
        part = attention(query_cols, keys, values, tables, c, per_call, block_len, degree)
        pieces[0].append(part)
        for d in range(1, exp_count):
            pieces[d].append(lax.ppermute(part, "expert", shift_pairs(exp_count, d)))
    atts = [jnp.concatenate(p, 0) for p in pieces]

    scalars = (counts, local_ids, perm, starts, place)
    common = (rank, cotangent_all, gain, router)
    weights = (expert_in, expert_out, columns)
    sums, last, stream, rows_parts, first = [], [], None, [], 0
    for g, count in enumerate(groups):
        head = (residual_all, atts, projs) if g == 0 else None
        found = list(expert_group(scalars, common, weights, first, count, head, (stream, last), lines, slot_rows, chunk))
        first += count
        if g == 0:
            stream = found.pop(0)
        rows_parts.append(found[0])
        sums.append(SeqSum(found[1:], seq_count))
        if g == 0:
            last = sums[0].step(last)
    steps = step_order(sums)
    for k, g in enumerate(steps):
        last = sums[g].step(last)
        if k == len(groups) - 1:
            partials = list(combine(starts, owner_order, rank, rows_parts, chunk, last))
            last = [partials[0]]
            parts = partials[:1] + [
                lax.ppermute(partials[d], "expert", shift_pairs(exp_count, d)) for d in range(1, exp_count)
            ]
    layer_out, grad_stream, home = at_home(me, stream, cotangent, gain, parts, chunk, last[0])
    into, token = [], []
    for g, each_sum in enumerate(sums):
        blocks = each_sum.blocks(token + [home] if g == len(sums) - 1 else [])
        *into, done = unpack(wheres[g], place, blocks, experts, width, ff, into)
        token = [done]
    grad_w_in, grad_w_out = into
    return layer_out, grad_stream, grad_w_in, grad_w_out


def solution(mesh):
    return jax.shard_map(
        shards,
        mesh=mesh,
        in_specs=(
            P("expert", "seq"),
            P("expert", "seq"),
            P("expert", "seq"),
            P("seq", None),
            P(("seq", "expert"), None),
            P(),
            P(),
            P(),
            P(("seq", "expert"), None),
            P("expert", None, None),
            P("expert", None, None),
            P(("seq", "expert"), None),
        ),
        out_specs=(
            P(("seq", "expert"), None),
            P(("seq", "expert"), None),
            P("expert", None, None),
            P("expert", None, None),
        ),
        check_vma=False,
    )
```

```python
import functools
import math

import jax
import jax.numpy as jnp
from jax import lax
from jax.experimental import pallas as pl
from jax.experimental.pallas import tpu as pltpu
from jax.sharding import PartitionSpec as P

HD = 32
WINDOW = 128
TILE = 256
EAGER = 32

norm_eps = 1e-05
root_two_pi = 0.7978845608028654
cubic_term = 0.044715

bf16 = jnp.bfloat16
f32 = jnp.float32


def params(mebibytes=32):
    return pltpu.CompilerParams(vmem_limit_bytes=mebibytes * 1024 * 1024)


def contract(a, b, da, db):
    return lax.dot_general(a, b, (((da,), (db,)), ((), ())), preferred_element_type=f32)


def ring_order(seq_count):
    rows = max(1, seq_count // 4)
    if seq_count % 4:
        return list(range(seq_count // 2))
    return [2 * z for z in range(rows)] + [2 * z + 1 for z in reversed(range(rows))]


def ring_pairs(seq_count, step):
    order = ring_order(seq_count)
    n = len(order)
    return [(2 * order[i] + c, 2 * order[(i + step) % n] + c) for i in range(n) for c in range(2)]


def sibling_pairs(seq_count):
    return [(s, s ^ 1) for s in range(seq_count)]


def shift_pairs(count, d):
    return [(i, (i + d) % count) for i in range(count)]


def gather_expert_axis(x, exp_count, axis=0):
    me = lax.axis_index("expert")
    size = x.shape[axis]
    shape = list(x.shape)
    shape[axis] = size * exp_count
    out = jnp.zeros(shape, x.dtype)
    out = lax.dynamic_update_slice_in_dim(out, x, me * size, axis)
    for d in range(1, exp_count):
        got = lax.ppermute(x, "expert", shift_pairs(exp_count, d))
        out = lax.dynamic_update_slice_in_dim(out, got, lax.rem(me + exp_count - d, exp_count) * size, axis)
    return out


def ring_gather(keys, values, seq_count):
    n = seq_count // 2
    fwd, bwd, sib = ring_pairs(seq_count, 1), ring_pairs(seq_count, -1), sibling_pairs(seq_count)
    k, v = keys, values
    own, other = ([], []), ([], [])
    for t in range(n):
        if t > 0:
            k = lax.ppermute(k, "seq", fwd)
            v = lax.ppermute(v, "seq", bwd)
        own[0].append(k)
        own[1].append(v)
        other[0].append(lax.ppermute(k, "seq", sib))
        other[1].append(lax.ppermute(v, "seq", sib))
    return own[0] + other[0], own[1] + other[1]


def sorted_entries(slot, slots):
    count = slot.shape[-1]
    at = jnp.arange(count, dtype=jnp.int32)
    before = (slot[:, None, :] < slot[:, :, None]) | ((slot[:, None, :] == slot[:, :, None]) & (at[None, None, :] < at[None, :, None]))
    rank = jnp.sum(before.astype(jnp.int32), 2)
    order = jnp.sum(jnp.where(rank[:, None, :] == at[None, :, None], at[None, None, :], 0), 2)
    begin = jnp.sum((slot[:, None, :] < jnp.arange(slots + 1, dtype=jnp.int32)[None, :, None]).astype(jnp.int32), 2)
    return order, begin


def block_tables(block_list, blk_seq, seq_count, cuts):
    order = ring_order(seq_count)
    n = len(order)
    inverse = [0] * n
    for i, chip in enumerate(order):
        inverse[chip] = i
    inverse = jnp.asarray(inverse, jnp.int32)
    me = lax.axis_index("seq")
    place = inverse[me // 2]
    owner = block_list // blk_seq
    local = block_list % blk_seq
    other = inverse[owner // 2]
    flag = ((owner ^ me) & 1) * n
    kslot = flag + lax.rem(place - other + n, n)
    vslot = flag + lax.rem(other - place + n, n)
    tables = []
    for low, high in zip(cuts[:-1], cuts[1:]):
        entries = [x[low:high].reshape(1, -1) for x in (local, kslot, vslot)]
        found = (entries[0],) + sorted_entries(entries[1], 2 * n) + sorted_entries(entries[2], 2 * n)
        tables.append([x[0] for x in found])
    return tables


def attention_kernel(degree, heads, sources, first, local, korder, kbegin, vorder, vbegin, q_ref, *refs):
    k_refs, v_refs = refs[:sources], refs[sources : 2 * sources]
    out_ref, k_all, v_all, sems = refs[2 * sources :]
    block_len = k_all.shape[2] // degree

    def fetch(source, dest, order, begin, s, sem):
        def one(r, carry):
            e = order[r]
            at = pl.ds(pl.multiple_of(local[e] * block_len, block_len), block_len)
            to = pl.ds(pl.multiple_of(lax.rem(e, degree) * block_len, block_len), block_len)
            pltpu.make_async_copy(source.at[:, at], dest.at[lax.div(e, degree), :, to], sem).start()
            return carry

        lax.fori_loop(begin[s], begin[s + 1], one, 0)

    for s in range(sources):
        fetch(k_refs[s], k_all, korder, kbegin, s, sems.at[0])
    for s in range(sources):
        fetch(v_refs[s], v_all, vorder, vbegin, s, sems.at[1])
    pltpu.make_async_copy(k_all, k_all, sems.at[0]).wait()
    pltpu.make_async_copy(v_all, v_all, sems.at[1]).wait()
    factor = math.log2(math.e) / math.sqrt(HD)

    feat = heads * HD
    head_row = lax.broadcasted_iota(jnp.int32, (feat, heads * block_len), 0) // HD
    head_col = lax.broadcasted_iota(jnp.int32, (feat, heads * block_len), 1) // block_len
    diagonal = head_row == head_col

    def one_block(b, carry):
        nodes = pl.ds(pl.multiple_of(b * block_len, block_len), block_len)
        asked = pl.ds(pl.multiple_of((b + first) * block_len, block_len), block_len)
        q = jnp.concatenate([q_ref[:, asked]] * heads, 1)
        scores = contract(k_all[b], jnp.where(diagonal, q, jnp.zeros_like(q)), 0, 0)
        top = jnp.max(scores, 0, keepdims=True)
        probs = jnp.exp2((scores - top) * factor)
        total = jnp.sum(probs, 0, keepdims=True)
        probs = probs.astype(bf16)
        cols = []
        for h in range(heads):
            rows, own = slice(h * HD, (h + 1) * HD), slice(h * block_len, (h + 1) * block_len)
            cols.append(jnp.dot(v_all[b, rows, :], probs[:, own], preferred_element_type=f32) / total[:, own])
        out_ref[nodes, :] = jnp.concatenate(cols, 0).T.astype(bf16)
        return carry

    count = k_all.shape[0]
    lax.fori_loop(0, count, one_block, 0, unroll=next(u for u in (4, 3, 2, 1) if count % u == 0))


def attention(queries, keys, values, tables, first, count, block_len, degree):
    feat = queries.shape[0]
    return pl.pallas_call(
        functools.partial(attention_kernel, degree, feat // HD, len(keys), first),
        grid_spec=pltpu.PrefetchScalarGridSpec(
            num_scalar_prefetch=5,
            grid=(1,),
            in_specs=[pl.BlockSpec(queries.shape, lambda i, *_: (0, 0))]
            + [pl.BlockSpec(memory_space=pl.ANY)] * (2 * len(keys)),
            out_specs=pl.BlockSpec((count * block_len, feat), lambda i, *_: (0, 0)),
            scratch_shapes=[pltpu.VMEM((count, feat, degree * block_len), bf16)] * 2 + [pltpu.SemaphoreType.DMA((2,))],
        ),
        out_shape=jax.ShapeDtypeStruct((count * block_len, feat), bf16),
        compiler_params=params(56),
        cost_estimate=pl.CostEstimate(
            flops=4 * count * block_len * degree * block_len * feat,
            bytes_accessed=2 * count * feat * block_len * (2 * degree + 2),
            transcendentals=count * block_len * degree * block_len * feat // HD,
        ),
        name="attention",
    )(*tables, queries, *keys, *values)


def place_of(part, line, lines):
    differ = jnp.bitwise_xor(part, line)
    place = 0
    step = 1
    while step < lines:
        place = place * 2 + jnp.bitwise_and(lax.div(differ, step), 1)
        step *= 2
    return place


def window_base(starts, i, e):
    return pl.multiple_of((starts[i, e] // 16) * 16, 16)


def further_windows(starts, i, e):
    left = starts[i + 1, e] - window_base(starts, i, e)
    return jnp.maximum((left + WINDOW - 1) // WINDOW, 1)


def any_further(starts, i, first, count):
    most = further_windows(starts, i, first)
    for e in range(first + 1, first + count):
        most = jnp.maximum(most, further_windows(starts, i, e))
    return most > 1


def one_hot(rank_row, base):
    place = lax.broadcasted_iota(jnp.int32, (WINDOW, rank_row.shape[1]), 0)
    return jnp.where(place == rank_row - base, 1.0, 0.0).astype(bf16)


def stack_hot(starts, rank, i, first, count):
    return jnp.concatenate([one_hot(rank[e : e + 1, :], window_base(starts, i, e)) for e in range(first, first + count)], 0)


def group_kernel(first, count, pieces, after, chunk, lines, counts, ids, perm, starts, place, *refs):
    refs = list(refs)
    rank_ref, cot_ref, gain_ref, router_ref, win_ref, wout_ref, rcol_ref = [refs.pop(0) for _ in range(7)]
    if pieces:
        res_ref = refs.pop(0)
        atts = [refs.pop(0) for _ in range(pieces)]
        projs = [refs.pop(0) for _ in range(pieces)]
        stream_ref = None
    else:
        stream_ref = refs.pop(0)
        del refs[:after]
    if pieces:
        out_stream = refs.pop(0)
    out_rows = refs.pop(0)
    grad_refs, (rows_ref, slots, acc_in, acc_out) = refs[:-4], refs[-4:]
    nodes, width = cot_ref.shape
    step = pl.program_id(0)

    @pl.when(step == 0)
    def _():
        slots[...] = jnp.zeros_like(slots)

        def dispatch(i, carry):
            at = pl.ds(pl.multiple_of(i * chunk, chunk), chunk)
            if pieces:
                projected = jnp.dot(atts[0][at, :], projs[0][...], preferred_element_type=f32)
                for a, w in zip(atts[1:], projs[1:]):
                    projected = projected + jnp.dot(a[at, :], w[...], preferred_element_type=f32)
                stream = (res_ref[at, :].astype(f32) + projected).astype(bf16)
                out_stream[at, :] = stream
            else:
                stream = stream_ref[at, :]
            wide = stream.astype(f32)
            inverse_rms = lax.rsqrt(jnp.mean(wide * wide, -1, keepdims=True) + norm_eps)
            rows_ref[:, :width] = (wide * inverse_rms * gain_ref[...]).astype(bf16)
            rows_ref[:, width:] = cot_ref[at, :]
            rank = rank_ref[:, at]
            packed = jnp.dot(stack_hot(starts, rank, i, first, count), rows_ref[...], preferred_element_type=f32).astype(bf16)
            for e in range(count):
                to = pl.ds(window_base(starts, i, first + e), WINDOW)
                slots[e, to, :] = slots[e, to, :] + packed[e * WINDOW : (e + 1) * WINDOW]

            @pl.when(any_further(starts, i, first, count))
            def _():
                for e in range(count):

                    def more(w, carry, e=e):
                        base = pl.multiple_of(window_base(starts, i, first + e) + w * WINDOW, 16)
                        hot = one_hot(rank[first + e : first + e + 1, :], base)
                        got = jnp.dot(hot, rows_ref[...], preferred_element_type=f32)
                        to = pl.ds(base, WINDOW)
                        slots[e, to, :] = slots[e, to, :] + got.astype(bf16)
                        return carry

                    lax.fori_loop(1, further_windows(starts, i, first + e), more, 0)

            return carry

        lax.fori_loop(0, nodes // chunk, dispatch, 0)

    e = step + first
    tiles = (counts[e] + TILE - 1) // TILE
    acc_in[...] = jnp.zeros_like(acc_in)
    acc_out[...] = jnp.zeros_like(acc_out)
    w_in = win_ref[0]
    w_out = wout_ref[0]
    mine = lax.broadcasted_iota(jnp.int32, (TILE, router_ref.shape[1]), 1) == ids[e]
    column = rcol_ref[0]

    def one(t, carry):
        at = pl.ds(pl.multiple_of(t * TILE, TILE), TILE)
        x = slots[step, at, :width]
        cot = slots[step, at, width:]
        cot_wide = cot.astype(f32)
        logits = jnp.dot(x, router_ref[...], preferred_element_type=f32)
        logit = jnp.sum(jnp.where(mine, logits, 0.0), 1, keepdims=True)
        gate = 1.0 / (1.0 + jnp.exp(-logit))
        scaled = (gate * cot_wide).astype(bf16)
        a = jnp.dot(x, w_in, preferred_element_type=f32)
        grad_hidden = contract(scaled, w_out, 1, 1)
        a2 = a * a
        t1 = jnp.tanh(a * (root_two_pi + (root_two_pi * cubic_term) * a2))
        half = 0.5 + 0.5 * t1
        hidden = (a * half).astype(bf16)
        slope = half + (a * (1.0 - t1 * t1)) * (0.5 * root_two_pi + (1.5 * root_two_pi * cubic_term) * a2)
        grad_pre = (grad_hidden * slope).astype(bf16)
        acc_out[...] += contract(hidden, scaled, 0, 0)
        acc_in[...] += contract(x, grad_pre, 0, 0)
        produced = jnp.dot(hidden, w_out, preferred_element_type=f32).astype(bf16).astype(f32)
        grad_rows = contract(grad_pre, w_in, 1, 1).astype(bf16).astype(f32)
        grad_logit = jnp.sum(cot_wide * produced, 1, keepdims=True) * gate * (1.0 - gate)
        out_rows[0, at, :width] = (gate * produced).astype(bf16)
        out_rows[0, at, width:] = (grad_rows + grad_logit * column).astype(bf16)
        return carry

    lax.fori_loop(0, tiles, one, 0)

    def blank(t, carry):
        at = pl.ds(pl.multiple_of(t * WINDOW, WINDOW), WINDOW)
        out_rows[0, at, :] = jnp.zeros((WINDOW, 2 * width), bf16)
        return carry

    lax.fori_loop(tiles * TILE // WINDOW, out_rows.shape[1] // WINDOW, blank, 0)

    ff = acc_in.shape[1]

    def write(grad_ref, with_in, with_out):
        part = grad_ref.shape[1] // lines
        for p in range(lines):
            at = pl.ds(pl.multiple_of(place_of(p, place[0], lines) * part, part), part)
            low = p * part
            if with_in and low < width:
                grad_ref[0, at, :] = acc_in[low : low + part, :].astype(bf16)
            else:
                low = low - width if with_in else low
                for j in range(ff // width):
                    cols = slice(j * width, (j + 1) * width)
                    grad_ref[0, at, cols] = acc_out[j * width + low : j * width + low + part, :].astype(bf16)

    if count > 2:
        each = count // 4
        for k, grad_ref in enumerate(grad_refs):
            pl.when((step >= k * each) & (step < (k + 1) * each))(functools.partial(write, grad_ref, True, True))
    else:
        for k in range(2):
            for column in range(2):

                @pl.when((step == k) & (place[1] == column))
                def _(k=k, column=column):
                    other, own = grad_refs[2 * k], grad_refs[2 * k + 1]
                    write((own, other)[column], True, False)
                    write((other, own)[column], False, True)


def expert_group(scalars, common, weights, first, count, head, tail, lines, slot_rows, chunk):
    counts, ids, perm, starts, place = scalars
    rank, cotangent, gain, router = common
    w_in, w_out, columns = weights
    nodes, width = cotangent.shape
    ff = w_in.shape[2]
    whole = lambda a: pl.BlockSpec(a.shape, lambda i, *_: (0,) * a.ndim)
    listed = lambda *shape: pl.BlockSpec((1,) + shape, lambda i, c, d, perm, *_: (perm[i + first], 0, 0))
    args = [rank, cotangent, gain, router, w_in, w_out, columns]
    specs = [whole(a) for a in args[:4]] + [listed(width, ff), listed(ff, width), listed(1, width)]
    out_shape, out_specs = [], []
    if head:
        residual, atts, projs = head
        extra = [residual, *atts, *projs]
        specs += [whole(a) for a in extra]
        out_shape.append(jax.ShapeDtypeStruct((nodes, width), bf16))
        pieces = len(atts)
    else:
        stream, after = tail
        extra = [stream, *after]
        specs += [whole(stream)] + [pl.BlockSpec(memory_space=pl.ANY)] * len(after)
        pieces = 0
    out_specs = [pl.BlockSpec(o.shape, lambda i, *_: (0, 0)) for o in out_shape]
    out_shape.append(jax.ShapeDtypeStruct((count, slot_rows, 2 * width), bf16))
    out_specs.append(pl.BlockSpec((1, slot_rows, 2 * width), lambda i, *_: (i, 0, 0)))
    each = max(1, count // 4)
    block = (1, 2 * width if count > 2 else width, ff)
    out_shape += [jax.ShapeDtypeStruct((each,) + block[1:], bf16)] * 4
    for k in range(4):
        first_step = k * each if count > 2 else k // 2
        out_specs.append(pl.BlockSpec(block, lambda i, *_, at=first_step: (jnp.clip(i - at, 0, each - 1), 0, 0)))
    return pl.pallas_call(
        functools.partial(group_kernel, first, count, pieces, 0 if head else len(after), chunk, lines),
        grid_spec=pltpu.PrefetchScalarGridSpec(
            num_scalar_prefetch=5,
            grid=(count,),
            in_specs=specs,
            out_specs=out_specs,
            scratch_shapes=[
                pltpu.VMEM((chunk, 2 * width), bf16),
                pltpu.VMEM((count, slot_rows, 2 * width), bf16),
                pltpu.VMEM((width, ff), f32),
                pltpu.VMEM((ff, width), f32),
            ],
        ),
        out_shape=out_shape,
        compiler_params=params(),
        cost_estimate=pl.CostEstimate(flops=1000, bytes_accessed=1000, transcendentals=0),
        name="experts",
    )(counts, ids, perm, starts, place, *args, *extra)


def combine_kernel(parts, owners, chunk, starts, order, rank_ref, *refs):
    rows_refs, out_refs = refs[:parts], refs[len(refs) - owners :]
    held = [(r, j) for r in rows_refs for j in range(r.shape[0])]
    experts = len(held)
    chunks = out_refs[0].shape[0] // chunk

    for d in range(owners):

        def gather(c, carry, d=d):
            i = order[d] * chunks + c
            rank = rank_ref[:, pl.ds(pl.multiple_of(i * chunk, chunk), chunk)]
            windows = [r[j, pl.ds(window_base(starts, i, e), WINDOW), :] for e, (r, j) in enumerate(held)]
            total = contract(stack_hot(starts, rank, i, 0, experts), jnp.concatenate(windows, 0), 0, 0)

            def further(total):
                for e, (r, j) in enumerate(held):

                    def more(w, acc, e=e, r=r, j=j):
                        base = pl.multiple_of(window_base(starts, i, e) + w * WINDOW, 16)
                        return acc + contract(one_hot(rank[e : e + 1, :], base), r[j, pl.ds(base, WINDOW), :], 0, 0)

                    total = lax.fori_loop(1, further_windows(starts, i, e), more, total)
                return total

            total = lax.cond(any_further(starts, i, 0, experts), further, lambda total: total, total)
            out_refs[d][pl.ds(pl.multiple_of(c * chunk, chunk), chunk), :] = total.astype(bf16)
            return carry

        lax.fori_loop(0, chunks, gather, 0)


def combine(starts, order, rank, rows_parts, chunk, after):
    owners = order.shape[0]
    nodes, double = rank.shape[1], rows_parts[0].shape[2]
    whole = lambda a: pl.BlockSpec(a.shape, lambda i, *_: (0,) * a.ndim)
    out = jax.ShapeDtypeStruct((nodes // owners, double), bf16)
    return pl.pallas_call(
        functools.partial(combine_kernel, len(rows_parts), owners, chunk),
        grid_spec=pltpu.PrefetchScalarGridSpec(
            num_scalar_prefetch=2,
            grid=(1,),
            in_specs=[whole(rank)] + [whole(r) for r in rows_parts] + [pl.BlockSpec(memory_space=pl.ANY)] * len(after),
            out_specs=[whole(out)] * owners,
        ),
        out_shape=[out] * owners,
        compiler_params=params(),
        cost_estimate=pl.CostEstimate(flops=EAGER * 10**9, bytes_accessed=10**7, transcendentals=0),
        name="combine",
    )(starts, order, rank, *rows_parts, *after)


def home_kernel(parts, stream_ref, cot_ref, gain_ref, *refs):
    layer_ref, grad_ref, token_ref = refs[parts:]
    token_ref[...] = jnp.zeros_like(token_ref)
    total = refs[0][...].astype(f32)
    for g in refs[1:parts]:
        total = total + g[...].astype(f32)
    width = stream_ref.shape[1]
    stream = stream_ref[...].astype(f32)
    inverse_rms = lax.rsqrt(jnp.mean(stream * stream, -1, keepdims=True) + norm_eps)
    layer_ref[...] = (stream + total[:, :width]).astype(bf16)
    gained = total[:, width:] * gain_ref[...]
    mean = jnp.mean(stream * gained, -1, keepdims=True)
    grad = cot_ref[...].astype(f32) + inverse_rms * gained - stream * (inverse_rms * inverse_rms * inverse_rms) * mean
    grad_ref[...] = grad.astype(bf16)


def at_home(me, stream, cotangent, gain, parts, chunk, after):
    tok_dev, width = cotangent.shape
    steps = tok_dev // chunk
    fresh = lambda w: pl.BlockSpec((chunk, w), lambda i, me: (i, 0))
    return pl.pallas_call(
        lambda me, *refs: home_kernel(len(parts), *refs[:-4], *refs[-3:]),
        grid_spec=pltpu.PrefetchScalarGridSpec(
            num_scalar_prefetch=1,
            grid=(steps,),
            in_specs=[
                pl.BlockSpec((chunk, width), lambda i, me: (me[0] * steps + i, 0)),
                fresh(width),
                pl.BlockSpec(gain.shape, lambda i, me: (0, 0)),
            ]
            + [fresh(2 * width) for _ in parts]
            + [pl.BlockSpec(memory_space=pl.ANY)],
            out_specs=[fresh(width), fresh(width), pl.BlockSpec((8, 128), lambda i, me: (0, 0))],
        ),
        out_shape=[jax.ShapeDtypeStruct((tok_dev, width), bf16)] * 2 + [jax.ShapeDtypeStruct((8, 128), f32)],
        compiler_params=params(),
        cost_estimate=pl.CostEstimate(
            flops=EAGER * tok_dev * width * 1000, bytes_accessed=tok_dev * width * 16, transcendentals=0
        ),
        name="at_home",
    )(me.reshape(1), stream, cotangent, gain, *parts, after)


def line_pairs(seq_count, d):
    return [(z * 4 + r, (z ^ d) * 4 + r) for z in range(seq_count // 4) for r in range(4)]


def seq_place():
    s = lax.axis_index("seq")
    return s % 2, (s // 2) % 2, s // 4


def sum_kernel(terms, cuts, *refs):
    total = refs[0][...].astype(f32)
    for r in refs[1:terms]:
        total = total + r[...].astype(f32)
    total = total.astype(bf16)
    part = total.shape[1] // cuts
    for k, out in enumerate(refs[len(refs) - cuts :]):
        out[...] = total[:, k * part : (k + 1) * part]


def sum_blocks(terms, cuts, after, name):
    shape = terms[0].shape
    whole = lambda s: pl.BlockSpec(s, lambda i: (0, 0, 0))
    piece = (shape[0], shape[1] // cuts, shape[2])
    return pl.pallas_call(
        functools.partial(sum_kernel, len(terms), cuts),
        grid=(1,),
        in_specs=[whole(shape)] * len(terms) + [pl.BlockSpec(memory_space=pl.ANY)] * len(after),
        out_specs=[whole(piece)] * cuts,
        out_shape=[jax.ShapeDtypeStruct(piece, bf16)] * cuts,
        compiler_params=params(16),
        cost_estimate=pl.CostEstimate(flops=1000, bytes_accessed=1000, transcendentals=0),
        name=name,
    )(*terms, *after)


def stack_kernel(count, *refs):
    rows = refs[0].shape[0]
    for k in range(count):
        refs[-1][k * rows : (k + 1) * rows] = refs[k][...]


def stack_pieces(pieces, after):
    shape = pieces[0].shape
    whole = lambda s: pl.BlockSpec(s, lambda i: (0, 0, 0, 0))
    stacked = (len(pieces) * shape[0],) + shape[1:]
    return pl.pallas_call(
        functools.partial(stack_kernel, len(pieces)),
        grid=(1,),
        in_specs=[whole(shape)] * len(pieces) + [pl.BlockSpec(memory_space=pl.ANY)] * len(after),
        out_specs=whole(stacked),
        out_shape=jax.ShapeDtypeStruct(stacked, bf16),
        compiler_params=params(16),
        cost_estimate=pl.CostEstimate(flops=1000, bytes_accessed=1000, transcendentals=0),
        name="stack_pieces",
    )(*pieces, *after)


class SeqSum:
    def __init__(self, grads, seq_count):
        self.grads, self.seq_count, self.lines = grads, seq_count, seq_count // 4
        self.cross = [(i, i ^ 2) for i in range(seq_count)]
        self.got = [self.to_sibling(g) for g in grads[:2]]
        bits = self.lines.bit_length() - 1
        self.left = [self.over_core, self.over_x]
        self.left += [functools.partial(self.over_line, 1 << k) for k in range(bits)]
        self.left += [functools.partial(self.back_line, 1 << k) for k in reversed(range(bits))]

    def step(self, after):
        return [self.left.pop(0)(after)]

    def to_sibling(self, x):
        return lax.ppermute(x, "seq", sibling_pairs(self.seq_count))

    def to_line(self, x, step):
        return lax.ppermute(x, "seq", line_pairs(self.seq_count, step))

    def over_core(self, after):
        (first,) = sum_blocks([self.grads[2], self.got[0]], 1, after, "sum_core")
        self.crossed = lax.ppermute(first, "seq", self.cross)
        return first

    def over_x(self, after):
        self.kept, sent = sum_blocks([self.grads[3], self.got[1], self.crossed], 2, after, "sum_x")
        self.arriving = self.to_line(sent, 1)
        return sent

    def over_line(self, step, after):
        if 2 * step < self.lines:
            self.kept, sent = sum_blocks([self.kept, self.arriving], 2, after, "sum_line")
            self.arriving = self.to_line(sent, 2 * step)
            return sent
        (shard,) = sum_blocks([self.kept, self.arriving], 1, after, "sum_line")
        self.own = shard[None]
        self.arriving = self.to_line(self.own, step)
        return shard

    def back_line(self, step, after):
        self.own = stack_pieces([self.own, self.arriving], after)
        if step > 1:
            self.arriving = self.to_line(self.own, step // 2)
        else:
            self.other = lax.ppermute(self.own, "seq", self.cross)
        return self.own

    def near_blocks(self):
        return [self.own, self.to_sibling(self.own)]

    def far_blocks(self, after):
        other = stack_pieces([self.other], after) if after else self.other
        return [other, self.to_sibling(other)]


def step_order(sums):
    left = [len(s.left) for s in sums]
    order = []
    while any(left):
        for g in range(len(sums)):
            if left[g]:
                order.append(g)
                left[g] -= 1
    return order


def unpack_kernel(blocks, lines, each, width, where, place, *refs):
    win_ref, wout_ref, token_ref = refs[-3:]
    token_ref[...] = jnp.zeros_like(token_ref)
    step = pl.program_id(0)

    def read(ref, i, with_in, with_out):
        for p in range(lines):
            block = ref[place_of(p, place[0], lines), i].astype(f32)
            part, ff = block.shape
            low = p * part
            if with_in and low < width:
                win_ref[0, low : low + part, :] = block
            else:
                low = low - width if with_in else low
                for j in range(ff // width):
                    wout_ref[0, j * width + low : j * width + low + part, :] = block[:, j * width : (j + 1) * width]

    if refs[0].shape[2] * lines > width:
        for a in range(blocks):
            for i in range(each):
                pl.when(step == a * each + i)(functools.partial(read, refs[a], i, True, True))
    else:
        for k in range(2):
            for column in range(2):

                @pl.when((step == k) & (place[1] == column))
                def _(k=k, column=column):
                    own, other = refs[2 * k], refs[2 * k + 1]
                    read((own, other)[column], 0, True, False)
                    read((other, own)[column], 0, False, True)


def unpack(where, place, blocks, experts, width, ff, into):
    lines, each = blocks[0].shape[:2]
    whole = pl.BlockSpec(blocks[0].shape, lambda i, *_: (0, 0, 0, 0))
    out = lambda *shape: pl.BlockSpec((1,) + shape, lambda i, where, place: (where[i], 0, 0))
    return pl.pallas_call(
        functools.partial(unpack_kernel, len(blocks), lines, each, width),
        grid_spec=pltpu.PrefetchScalarGridSpec(
            num_scalar_prefetch=2,
            grid=where.shape,
            in_specs=[whole] * len(blocks) + [pl.BlockSpec(memory_space=pl.ANY)] * len(into),
            out_specs=[out(width, ff), out(ff, width), pl.BlockSpec((8, 128), lambda i, *_: (0, 0))],
        ),
        out_shape=[
            jax.ShapeDtypeStruct((experts, width, ff), f32),
            jax.ShapeDtypeStruct((experts, ff, width), f32),
            jax.ShapeDtypeStruct((8, 128), f32),
        ],
        input_output_aliases={2 + len(blocks) + i: i for i in range(len(into))},
        compiler_params=params(16),
        cost_estimate=pl.CostEstimate(
            flops=EAGER * where.shape[0] * 2 * width * ff * 6, bytes_accessed=where.shape[0] * 2 * width * ff * 6, transcendentals=0
        ),
        name="unpack",
    )(where, place, *blocks, *into)


def shards(
    query_cols,
    key_cols,
    value_cols,
    block_list,
    residual,
    out_proj,
    norm_gain,
    router_weight,
    expert_ids,
    expert_in,
    expert_out,
    cotangent,
):
    seq_count = lax.axis_size("seq")
    exp_count = lax.axis_size("expert")
    me = lax.axis_index("expert")
    feat, nodes = query_cols.shape
    blk_seq, degree = block_list.shape
    block_len = nodes // blk_seq
    tok_dev, width = residual.shape
    expert_total = router_weight.shape[1]
    experts = expert_in.shape[0]
    ff = expert_in.shape[2]
    topk = expert_ids.shape[1]
    chunk = min(256, tok_dev)
    capacity = 2 * tok_dev * topk // expert_total * exp_count
    slot_rows = capacity + WINDOW

    cuts = [0, blk_seq * 5 // 8, blk_seq]
    keys, values = ring_gather(key_cols, value_cols, seq_count)
    tables = block_tables(block_list, blk_seq, seq_count, cuts)

    residual_all = gather_expert_axis(residual, exp_count)
    cotangent_all = gather_expert_axis(cotangent, exp_count)
    ids_all = gather_expert_axis(expert_ids.T, exp_count, 1)
    gain = norm_gain.reshape(1, width)
    core, column, line = seq_place()
    lines = seq_count // 4
    place = jnp.stack([line, column]).astype(jnp.int32)
    groups = [4] * (experts // 4)
    groups += [2] * ((experts - sum(groups)) // 2)
    dests = [(1 - core, 1 - column), (1 - core, column), (core, 1 - column), (core, column)]
    perm, wheres, first = [], [], 0
    for count in groups:
        if count == 4:
            perm += [first + 2 * c + x for c, x in dests]
            wheres.append([first + 2 * c + x for c, x in (dests[3], dests[2], dests[1], dests[0])])
        else:
            perm += [first + 1 - core, first + core]
            wheres.append([first + core, first + 1 - core])
        first += count
    perm = jnp.stack(perm).astype(jnp.int32)
    wheres = [jnp.stack(w).astype(jnp.int32) for w in wheres]
    local_ids = me * experts + perm
    hot = jnp.sum((ids_all[None, :, :] == local_ids[:, None, None]).astype(jnp.int32), 1)
    running = jnp.cumsum(hot, 1)
    rank = jnp.where(hot > 0, running - 1, -(1 << 20))
    ends = running[:, chunk - 1 :: chunk]
    starts = jnp.concatenate([jnp.zeros((experts, 1), jnp.int32), ends], 1).T
    counts = running[:, -1]
    router = jnp.pad(router_weight, ((0, 0), (0, -expert_total % 128)))
    columns = lax.dynamic_slice_in_dim(router_weight.T, me * experts, experts, 0).astype(f32).reshape(experts, 1, width)
    projs = [
        lax.dynamic_slice_in_dim(out_proj, lax.rem(me + exp_count - d, exp_count) * feat, feat, 0)
        for d in range(exp_count)
    ]
    owner_order = lax.rem(me + jnp.arange(exp_count, dtype=jnp.int32), exp_count)

    pieces = [[] for _ in range(exp_count)]
    for table, low, high in zip(tables, cuts[:-1], cuts[1:]):
        part = attention(query_cols, keys, values, table, low, high - low, block_len, degree)
        pieces[0].append(part)
        for d in range(1, exp_count):
            pieces[d].append(lax.ppermute(part, "expert", shift_pairs(exp_count, d)))
    atts = [jnp.concatenate(p, 0) for p in pieces]

    scalars = (counts, local_ids, perm, starts, place)
    common = (rank, cotangent_all, gain, router)
    weights = (expert_in, expert_out, columns)
    sums, last, stream, rows_parts, first = [], [], None, [], 0
    for g, count in enumerate(groups):
        head = (residual_all, atts, projs) if g == 0 else None
        found = list(expert_group(scalars, common, weights, first, count, head, (stream, last), lines, slot_rows, chunk))
        first += count
        if g == 0:
            stream = found.pop(0)
        rows_parts.append(found[0])
        sums.append(SeqSum(found[1:], seq_count))
        if g == 0:
            last = sums[0].step(last)
    steps = step_order(sums)
    for k, g in enumerate(steps):
        last = sums[g].step(last)
        if k == len(groups) - 1:
            partials = list(combine(starts, owner_order, rank, rows_parts, chunk, last))
            last = [partials[0]]
            parts = partials[:1] + [
                lax.ppermute(partials[d], "expert", shift_pairs(exp_count, d)) for d in range(1, exp_count)
            ]
    layer_out, grad_stream, home = at_home(me, stream, cotangent, gain, parts, chunk, last[0])
    into, done = [], []
    for g, (count, each_sum) in enumerate(zip(groups, sums)):
        where, after = wheres[g], []
        if g == len(groups) - 1:
            after = done + [home]
            if count > 2:
                near = jnp.concatenate([where[: count // 4], where[count // 2 : 3 * count // 4]])
                *into, token = unpack(near, place, each_sum.near_blocks(), experts, width, ff, into)
                where = jnp.concatenate([where[count // 4 : count // 2], where[3 * count // 4 :]])
                after = [token, home]
        blocks = each_sum.far_blocks(after)
        if where is wheres[g]:
            own, other = each_sum.near_blocks(), blocks
            blocks = [own[0], other[0], own[1], other[1]]
        *into, token = unpack(where, place, blocks, experts, width, ff, into)
        done = [token]
    grad_w_in, grad_w_out = into
    return layer_out, grad_stream, grad_w_in, grad_w_out


def solution(mesh):
    return jax.shard_map(
        shards,
        mesh=mesh,
        in_specs=(
            P("expert", "seq"),
            P("expert", "seq"),
            P("expert", "seq"),
            P("seq", None),
            P(("seq", "expert"), None),
            P(),
            P(),
            P(),
            P(("seq", "expert"), None),
            P("expert", None, None),
            P("expert", None, None),
            P(("seq", "expert"), None),
        ),
        out_specs=(
            P(("seq", "expert"), None),
            P(("seq", "expert"), None),
            P("expert", None, None),
            P("expert", None, None),
        ),
        check_vma=False,
    )
```

```python
import functools
import math

import jax
import jax.numpy as jnp
from jax import lax
from jax.experimental import pallas as pl
from jax.experimental.pallas import tpu as pltpu
from jax.sharding import PartitionSpec as P

HD = 32
WINDOW = 128
TILE = 256
EAGER = 32

norm_eps = 1e-05
root_two_pi = 0.7978845608028654
cubic_term = 0.044715

bf16 = jnp.bfloat16
f32 = jnp.float32


def params(mebibytes=32):
    return pltpu.CompilerParams(vmem_limit_bytes=mebibytes * 1024 * 1024)


def contract(a, b, da, db):
    return lax.dot_general(a, b, (((da,), (db,)), ((), ())), preferred_element_type=f32)


def ring_order(seq_count):
    rows = max(1, seq_count // 4)
    if seq_count % 4:
        return list(range(seq_count // 2))
    return [2 * z for z in range(rows)] + [2 * z + 1 for z in reversed(range(rows))]


def ring_pairs(seq_count, step):
    order = ring_order(seq_count)
    n = len(order)
    return [(2 * order[i] + c, 2 * order[(i + step) % n] + c) for i in range(n) for c in range(2)]


def sibling_pairs(seq_count):
    return [(s, s ^ 1) for s in range(seq_count)]


def shift_pairs(count, d):
    return [(i, (i + d) % count) for i in range(count)]


def gather_expert_axis(x, exp_count, axis=0):
    me = lax.axis_index("expert")
    size = x.shape[axis]
    shape = list(x.shape)
    shape[axis] = size * exp_count
    out = jnp.zeros(shape, x.dtype)
    out = lax.dynamic_update_slice_in_dim(out, x, me * size, axis)
    for d in range(1, exp_count):
        got = lax.ppermute(x, "expert", shift_pairs(exp_count, d))
        out = lax.dynamic_update_slice_in_dim(out, got, lax.rem(me + exp_count - d, exp_count) * size, axis)
    return out


def ring_gather(keys, values, seq_count):
    n = seq_count // 2
    fwd, bwd, sib = ring_pairs(seq_count, 1), ring_pairs(seq_count, -1), sibling_pairs(seq_count)
    k, v = keys, values
    own, other = ([], []), ([], [])
    for t in range(n):
        if t > 0:
            k = lax.ppermute(k, "seq", fwd)
            v = lax.ppermute(v, "seq", bwd)
        own[0].append(k)
        own[1].append(v)
        other[0].append(lax.ppermute(k, "seq", sib))
        other[1].append(lax.ppermute(v, "seq", sib))
    return own[0] + other[0], own[1] + other[1]


def sorted_entries(slot, slots):
    count = slot.shape[-1]
    at = jnp.arange(count, dtype=jnp.int32)
    before = (slot[:, None, :] < slot[:, :, None]) | ((slot[:, None, :] == slot[:, :, None]) & (at[None, None, :] < at[None, :, None]))
    rank = jnp.sum(before.astype(jnp.int32), 2)
    order = jnp.sum(jnp.where(rank[:, None, :] == at[None, :, None], at[None, None, :], 0), 2)
    begin = jnp.sum((slot[:, None, :] < jnp.arange(slots + 1, dtype=jnp.int32)[None, :, None]).astype(jnp.int32), 2)
    return order, begin


def block_tables(block_list, blk_seq, seq_count, cuts):
    order = ring_order(seq_count)
    n = len(order)
    inverse = [0] * n
    for i, chip in enumerate(order):
        inverse[chip] = i
    inverse = jnp.asarray(inverse, jnp.int32)
    me = lax.axis_index("seq")
    place = inverse[me // 2]
    owner = block_list // blk_seq
    local = block_list % blk_seq
    other = inverse[owner // 2]
    flag = ((owner ^ me) & 1) * n
    kslot = flag + lax.rem(place - other + n, n)
    vslot = flag + lax.rem(other - place + n, n)
    tables = []
    for low, high in zip(cuts[:-1], cuts[1:]):
        entries = [x[low:high].reshape(1, -1) for x in (local, kslot, vslot)]
        found = (entries[0],) + sorted_entries(entries[1], 2 * n) + sorted_entries(entries[2], 2 * n)
        tables.append([x[0] for x in found])
    return tables


def attention_kernel(degree, heads, sources, first, local, korder, kbegin, vorder, vbegin, q_ref, *refs):
    k_refs, v_refs = refs[:sources], refs[sources : 2 * sources]
    out_ref, k_all, v_all, sems = refs[2 * sources :]
    block_len = k_all.shape[2] // degree

    def fetch(source, dest, order, begin, s, sem):
        def one(r, carry):
            e = order[r]
            at = pl.ds(pl.multiple_of(local[e] * block_len, block_len), block_len)
            to = pl.ds(pl.multiple_of(lax.rem(e, degree) * block_len, block_len), block_len)
            pltpu.make_async_copy(source.at[:, at], dest.at[lax.div(e, degree), :, to], sem).start()
            return carry

        lax.fori_loop(begin[s], begin[s + 1], one, 0)

    for s in range(sources):
        fetch(k_refs[s], k_all, korder, kbegin, s, sems.at[0])
    for s in range(sources):
        fetch(v_refs[s], v_all, vorder, vbegin, s, sems.at[1])
    pltpu.make_async_copy(k_all, k_all, sems.at[0]).wait()
    pltpu.make_async_copy(v_all, v_all, sems.at[1]).wait()
    factor = math.log2(math.e) / math.sqrt(HD)

    feat = heads * HD
    head_row = lax.broadcasted_iota(jnp.int32, (feat, heads * block_len), 0) // HD
    head_col = lax.broadcasted_iota(jnp.int32, (feat, heads * block_len), 1) // block_len
    diagonal = head_row == head_col

    def one_block(b, carry):
        nodes = pl.ds(pl.multiple_of(b * block_len, block_len), block_len)
        asked = pl.ds(pl.multiple_of((b + first) * block_len, block_len), block_len)
        q = jnp.concatenate([q_ref[:, asked]] * heads, 1)
        scores = contract(k_all[b], jnp.where(diagonal, q, jnp.zeros_like(q)), 0, 0)
        top = jnp.max(scores, 0, keepdims=True)
        probs = jnp.exp2((scores - top) * factor)
        total = jnp.sum(probs, 0, keepdims=True)
        probs = probs.astype(bf16)
        cols = []
        for h in range(heads):
            rows, own = slice(h * HD, (h + 1) * HD), slice(h * block_len, (h + 1) * block_len)
            cols.append(jnp.dot(v_all[b, rows, :], probs[:, own], preferred_element_type=f32) / total[:, own])
        out_ref[nodes, :] = jnp.concatenate(cols, 0).T.astype(bf16)
        return carry

    count = k_all.shape[0]
    lax.fori_loop(0, count, one_block, 0, unroll=next(u for u in (4, 3, 2, 1) if count % u == 0))


def attention(queries, keys, values, tables, first, count, block_len, degree):
    feat = queries.shape[0]
    return pl.pallas_call(
        functools.partial(attention_kernel, degree, feat // HD, len(keys), first),
        grid_spec=pltpu.PrefetchScalarGridSpec(
            num_scalar_prefetch=5,
            grid=(1,),
            in_specs=[pl.BlockSpec(queries.shape, lambda i, *_: (0, 0))]
            + [pl.BlockSpec(memory_space=pl.ANY)] * (2 * len(keys)),
            out_specs=pl.BlockSpec((count * block_len, feat), lambda i, *_: (0, 0)),
            scratch_shapes=[pltpu.VMEM((count, feat, degree * block_len), bf16)] * 2 + [pltpu.SemaphoreType.DMA((2,))],
        ),
        out_shape=jax.ShapeDtypeStruct((count * block_len, feat), bf16),
        compiler_params=params(56),
        cost_estimate=pl.CostEstimate(
            flops=4 * count * block_len * degree * block_len * feat,
            bytes_accessed=2 * count * feat * block_len * (2 * degree + 2),
            transcendentals=count * block_len * degree * block_len * feat // HD,
        ),
        name="attention",
    )(*tables, queries, *keys, *values)


def place_of(part, line, lines):
    differ = jnp.bitwise_xor(part, line)
    place = 0
    step = 1
    while step < lines:
        place = place * 2 + jnp.bitwise_and(lax.div(differ, step), 1)
        step *= 2
    return place


def window_base(starts, i, e):
    return pl.multiple_of((starts[i, e] // 16) * 16, 16)


def further_windows(starts, i, e):
    left = starts[i + 1, e] - window_base(starts, i, e)
    return jnp.maximum((left + WINDOW - 1) // WINDOW, 1)


def any_further(starts, i, first, count):
    most = further_windows(starts, i, first)
    for e in range(first + 1, first + count):
        most = jnp.maximum(most, further_windows(starts, i, e))
    return most > 1


def one_hot(rank_row, base):
    place = lax.broadcasted_iota(jnp.int32, (WINDOW, rank_row.shape[1]), 0)
    return jnp.where(place == rank_row - base, 1.0, 0.0).astype(bf16)


def stack_hot(starts, rank, i, first, count):
    return jnp.concatenate([one_hot(rank[e : e + 1, :], window_base(starts, i, e)) for e in range(first, first + count)], 0)


def group_kernel(first, count, pieces, after, chunk, lines, counts, ids, perm, starts, place, *refs):
    refs = list(refs)
    rank_ref, cot_ref, gain_ref, router_ref, win_ref, wout_ref, rcol_ref = [refs.pop(0) for _ in range(7)]
    if pieces:
        res_ref = refs.pop(0)
        atts = [refs.pop(0) for _ in range(pieces)]
        projs = [refs.pop(0) for _ in range(pieces)]
        stream_ref = None
    else:
        stream_ref = refs.pop(0)
        del refs[:after]
    if pieces:
        out_stream = refs.pop(0)
    out_rows = refs.pop(0)
    grad_refs, (rows_ref, slots, acc_in, acc_out) = refs[:-4], refs[-4:]
    nodes, width = cot_ref.shape
    step = pl.program_id(0)

    @pl.when(step == 0)
    def _():
        slots[...] = jnp.zeros_like(slots)

        def dispatch(i, carry):
            at = pl.ds(pl.multiple_of(i * chunk, chunk), chunk)
            if pieces:
                if atts[0].shape[1] % 128 == 0:
                    gathered = jnp.concatenate([a[at, :] for a in atts], 1)
                    weights = jnp.concatenate([w[...] for w in projs], 0)
                    projected = jnp.dot(gathered, weights, preferred_element_type=f32)
                else:
                    projected = jnp.dot(atts[0][at, :], projs[0][...], preferred_element_type=f32)
                    for a, w in zip(atts[1:], projs[1:]):
                        projected = projected + jnp.dot(a[at, :], w[...], preferred_element_type=f32)
                stream = (res_ref[at, :].astype(f32) + projected).astype(bf16)
                out_stream[at, :] = stream
            else:
                stream = stream_ref[at, :]
            wide = stream.astype(f32)
            inverse_rms = lax.rsqrt(jnp.mean(wide * wide, -1, keepdims=True) + norm_eps)
            rows_ref[:, :width] = (wide * inverse_rms * gain_ref[...]).astype(bf16)
            rows_ref[:, width:] = cot_ref[at, :]
            rank = rank_ref[:, at]
            packed = jnp.dot(stack_hot(starts, rank, i, first, count), rows_ref[...], preferred_element_type=f32).astype(bf16)
            for e in range(count):
                to = pl.ds(window_base(starts, i, first + e), WINDOW)
                slots[e, to, :] = slots[e, to, :] + packed[e * WINDOW : (e + 1) * WINDOW]

            @pl.when(any_further(starts, i, first, count))
            def _():
                for e in range(count):

                    def more(w, carry, e=e):
                        base = pl.multiple_of(window_base(starts, i, first + e) + w * WINDOW, 16)
                        hot = one_hot(rank[first + e : first + e + 1, :], base)
                        got = jnp.dot(hot, rows_ref[...], preferred_element_type=f32)
                        to = pl.ds(base, WINDOW)
                        slots[e, to, :] = slots[e, to, :] + got.astype(bf16)
                        return carry

                    lax.fori_loop(1, further_windows(starts, i, first + e), more, 0)

            return carry

        lax.fori_loop(0, nodes // chunk, dispatch, 0)

    e = step + first
    tiles = (counts[e] + TILE - 1) // TILE
    acc_in[...] = jnp.zeros_like(acc_in)
    acc_out[...] = jnp.zeros_like(acc_out)
    w_in = win_ref[0]
    w_out = wout_ref[0]
    mine = lax.broadcasted_iota(jnp.int32, (TILE, router_ref.shape[1]), 1) == ids[e]
    column = rcol_ref[0]

    def one(t, carry):
        at = pl.ds(pl.multiple_of(t * TILE, TILE), TILE)
        x = slots[step, at, :width]
        cot = slots[step, at, width:]
        cot_wide = cot.astype(f32)
        logits = jnp.dot(x, router_ref[...], preferred_element_type=f32)
        logit = jnp.sum(jnp.where(mine, logits, 0.0), 1, keepdims=True)
        gate = 1.0 / (1.0 + jnp.exp(-logit))
        scaled = (gate * cot_wide).astype(bf16)
        a = jnp.dot(x, w_in, preferred_element_type=f32)
        grad_hidden = contract(scaled, w_out, 1, 1)
        a2 = a * a
        t1 = jnp.tanh(a * (root_two_pi + (root_two_pi * cubic_term) * a2))
        half = 0.5 + 0.5 * t1
        hidden = (a * half).astype(bf16)
        slope = half + (a * (1.0 - t1 * t1)) * (0.5 * root_two_pi + (1.5 * root_two_pi * cubic_term) * a2)
        grad_pre = (grad_hidden * slope).astype(bf16)
        acc_out[...] += contract(hidden, scaled, 0, 0)
        acc_in[...] += contract(x, grad_pre, 0, 0)
        produced = jnp.dot(hidden, w_out, preferred_element_type=f32).astype(bf16).astype(f32)
        grad_rows = contract(grad_pre, w_in, 1, 1).astype(bf16).astype(f32)
        grad_logit = jnp.sum(cot_wide * produced, 1, keepdims=True) * gate * (1.0 - gate)
        out_rows[0, at, :width] = (gate * produced).astype(bf16)
        out_rows[0, at, width:] = (grad_rows + grad_logit * column).astype(bf16)
        return carry

    lax.fori_loop(0, tiles, one, 0)

    def blank(t, carry):
        at = pl.ds(pl.multiple_of(t * WINDOW, WINDOW), WINDOW)
        out_rows[0, at, :] = jnp.zeros((WINDOW, 2 * width), bf16)
        return carry

    lax.fori_loop(tiles * TILE // WINDOW, out_rows.shape[1] // WINDOW, blank, 0)

    ff = acc_in.shape[1]

    def write(grad_ref, with_in, with_out):
        part = grad_ref.shape[1] // lines
        for p in range(lines):
            at = pl.ds(pl.multiple_of(place_of(p, place[0], lines) * part, part), part)
            low = p * part
            if with_in and low < width:
                grad_ref[0, at, :] = acc_in[low : low + part, :].astype(bf16)
            else:
                low = low - width if with_in else low
                for j in range(ff // width):
                    cols = slice(j * width, (j + 1) * width)
                    grad_ref[0, at, cols] = acc_out[j * width + low : j * width + low + part, :].astype(bf16)

    if count > 2:
        each = count // 4
        for k, grad_ref in enumerate(grad_refs):
            pl.when((step >= k * each) & (step < (k + 1) * each))(functools.partial(write, grad_ref, True, True))
    else:
        for k in range(2):
            for column in range(2):

                @pl.when((step == k) & (place[1] == column))
                def _(k=k, column=column):
                    other, own = grad_refs[2 * k], grad_refs[2 * k + 1]
                    write((own, other)[column], True, False)
                    write((other, own)[column], False, True)


def expert_group(scalars, common, weights, first, count, head, tail, lines, slot_rows, chunk):
    counts, ids, perm, starts, place = scalars
    rank, cotangent, gain, router = common
    w_in, w_out, columns = weights
    nodes, width = cotangent.shape
    ff = w_in.shape[2]
    whole = lambda a: pl.BlockSpec(a.shape, lambda i, *_: (0,) * a.ndim)
    listed = lambda *shape: pl.BlockSpec((1,) + shape, lambda i, c, d, perm, *_: (perm[i + first], 0, 0))
    args = [rank, cotangent, gain, router, w_in, w_out, columns]
    specs = [whole(a) for a in args[:4]] + [listed(width, ff), listed(ff, width), listed(1, width)]
    out_shape, out_specs = [], []
    if head:
        residual, atts, projs = head
        extra = [residual, *atts, *projs]
        specs += [whole(a) for a in extra]
        out_shape.append(jax.ShapeDtypeStruct((nodes, width), bf16))
        pieces = len(atts)
    else:
        stream, after = tail
        extra = [stream, *after]
        specs += [whole(stream)] + [pl.BlockSpec(memory_space=pl.ANY)] * len(after)
        pieces = 0
    out_specs = [pl.BlockSpec(o.shape, lambda i, *_: (0, 0)) for o in out_shape]
    out_shape.append(jax.ShapeDtypeStruct((count, slot_rows, 2 * width), bf16))
    out_specs.append(pl.BlockSpec((1, slot_rows, 2 * width), lambda i, *_: (i, 0, 0)))
    each = max(1, count // 4)
    block = (1, 2 * width if count > 2 else width, ff)
    out_shape += [jax.ShapeDtypeStruct((each,) + block[1:], bf16)] * 4
    for k in range(4):
        first_step = k * each if count > 2 else k // 2
        out_specs.append(pl.BlockSpec(block, lambda i, *_, at=first_step: (jnp.clip(i - at, 0, each - 1), 0, 0)))
    return pl.pallas_call(
        functools.partial(group_kernel, first, count, pieces, 0 if head else len(after), chunk, lines),
        grid_spec=pltpu.PrefetchScalarGridSpec(
            num_scalar_prefetch=5,
            grid=(count,),
            in_specs=specs,
            out_specs=out_specs,
            scratch_shapes=[
                pltpu.VMEM((chunk, 2 * width), bf16),
                pltpu.VMEM((count, slot_rows, 2 * width), bf16),
                pltpu.VMEM((width, ff), f32),
                pltpu.VMEM((ff, width), f32),
            ],
        ),
        out_shape=out_shape,
        compiler_params=params(),
        cost_estimate=pl.CostEstimate(flops=1000, bytes_accessed=1000, transcendentals=0),
        name="experts",
    )(counts, ids, perm, starts, place, *args, *extra)


def combine_kernel(parts, owners, chunk, starts, order, rank_ref, *refs):
    rows_refs, out_refs = refs[:parts], refs[len(refs) - owners :]
    held = [(r, j) for r in rows_refs for j in range(r.shape[0])]
    experts = len(held)
    chunks = out_refs[0].shape[0] // chunk

    for d in range(owners):

        def gather(c, carry, d=d):
            i = order[d] * chunks + c
            rank = rank_ref[:, pl.ds(pl.multiple_of(i * chunk, chunk), chunk)]
            windows = [r[j, pl.ds(window_base(starts, i, e), WINDOW), :] for e, (r, j) in enumerate(held)]
            total = contract(stack_hot(starts, rank, i, 0, experts), jnp.concatenate(windows, 0), 0, 0)

            def further(total):
                for e, (r, j) in enumerate(held):

                    def more(w, acc, e=e, r=r, j=j):
                        base = pl.multiple_of(window_base(starts, i, e) + w * WINDOW, 16)
                        return acc + contract(one_hot(rank[e : e + 1, :], base), r[j, pl.ds(base, WINDOW), :], 0, 0)

                    total = lax.fori_loop(1, further_windows(starts, i, e), more, total)
                return total

            total = lax.cond(any_further(starts, i, 0, experts), further, lambda total: total, total)
            out_refs[d][pl.ds(pl.multiple_of(c * chunk, chunk), chunk), :] = total.astype(bf16)
            return carry

        lax.fori_loop(0, chunks, gather, 0)


def combine(starts, order, rank, rows_parts, chunk, after):
    owners = order.shape[0]
    nodes, double = rank.shape[1], rows_parts[0].shape[2]
    whole = lambda a: pl.BlockSpec(a.shape, lambda i, *_: (0,) * a.ndim)
    out = jax.ShapeDtypeStruct((nodes // owners, double), bf16)
    return pl.pallas_call(
        functools.partial(combine_kernel, len(rows_parts), owners, chunk),
        grid_spec=pltpu.PrefetchScalarGridSpec(
            num_scalar_prefetch=2,
            grid=(1,),
            in_specs=[whole(rank)] + [whole(r) for r in rows_parts] + [pl.BlockSpec(memory_space=pl.ANY)] * len(after),
            out_specs=[whole(out)] * owners,
        ),
        out_shape=[out] * owners,
        compiler_params=params(),
        cost_estimate=pl.CostEstimate(flops=EAGER * 10**9, bytes_accessed=10**7, transcendentals=0),
        name="combine",
    )(starts, order, rank, *rows_parts, *after)


def home_kernel(parts, stream_ref, cot_ref, gain_ref, *refs):
    layer_ref, grad_ref, token_ref = refs[parts:]
    token_ref[...] = jnp.zeros_like(token_ref)
    total = refs[0][...].astype(f32)
    for g in refs[1:parts]:
        total = total + g[...].astype(f32)
    width = stream_ref.shape[1]
    stream = stream_ref[...].astype(f32)
    inverse_rms = lax.rsqrt(jnp.mean(stream * stream, -1, keepdims=True) + norm_eps)
    layer_ref[...] = (stream + total[:, :width]).astype(bf16)
    gained = total[:, width:] * gain_ref[...]
    mean = jnp.mean(stream * gained, -1, keepdims=True)
    grad = cot_ref[...].astype(f32) + inverse_rms * gained - stream * (inverse_rms * inverse_rms * inverse_rms) * mean
    grad_ref[...] = grad.astype(bf16)


def at_home(me, stream, cotangent, gain, parts, chunk, after):
    tok_dev, width = cotangent.shape
    steps = tok_dev // chunk
    fresh = lambda w: pl.BlockSpec((chunk, w), lambda i, me: (i, 0))
    return pl.pallas_call(
        lambda me, *refs: home_kernel(len(parts), *refs[:-4], *refs[-3:]),
        grid_spec=pltpu.PrefetchScalarGridSpec(
            num_scalar_prefetch=1,
            grid=(steps,),
            in_specs=[
                pl.BlockSpec((chunk, width), lambda i, me: (me[0] * steps + i, 0)),
                fresh(width),
                pl.BlockSpec(gain.shape, lambda i, me: (0, 0)),
            ]
            + [fresh(2 * width) for _ in parts]
            + [pl.BlockSpec(memory_space=pl.ANY)],
            out_specs=[fresh(width), fresh(width), pl.BlockSpec((8, 128), lambda i, me: (0, 0))],
        ),
        out_shape=[jax.ShapeDtypeStruct((tok_dev, width), bf16)] * 2 + [jax.ShapeDtypeStruct((8, 128), f32)],
        compiler_params=params(),
        cost_estimate=pl.CostEstimate(
            flops=EAGER * tok_dev * width * 1000, bytes_accessed=tok_dev * width * 16, transcendentals=0
        ),
        name="at_home",
    )(me.reshape(1), stream, cotangent, gain, *parts, after)


def line_pairs(seq_count, d):
    return [(z * 4 + r, (z ^ d) * 4 + r) for z in range(seq_count // 4) for r in range(4)]


def seq_place():
    s = lax.axis_index("seq")
    return s % 2, (s // 2) % 2, s // 4


def sum_kernel(terms, cuts, *refs):
    total = refs[0][...].astype(f32)
    for r in refs[1:terms]:
        total = total + r[...].astype(f32)
    total = total.astype(bf16)
    part = total.shape[1] // cuts
    for k, out in enumerate(refs[len(refs) - cuts :]):
        out[...] = total[:, k * part : (k + 1) * part]


def sum_blocks(terms, cuts, after, name):
    shape = terms[0].shape
    whole = lambda s: pl.BlockSpec(s, lambda i: (0, 0, 0))
    piece = (shape[0], shape[1] // cuts, shape[2])
    return pl.pallas_call(
        functools.partial(sum_kernel, len(terms), cuts),
        grid=(1,),
        in_specs=[whole(shape)] * len(terms) + [pl.BlockSpec(memory_space=pl.ANY)] * len(after),
        out_specs=[whole(piece)] * cuts,
        out_shape=[jax.ShapeDtypeStruct(piece, bf16)] * cuts,
        compiler_params=params(16),
        cost_estimate=pl.CostEstimate(flops=1000, bytes_accessed=1000, transcendentals=0),
        name=name,
    )(*terms, *after)


def stack_kernel(count, *refs):
    rows = refs[0].shape[0]
    for k in range(count):
        refs[-1][k * rows : (k + 1) * rows] = refs[k][...]


def stack_pieces(pieces, after):
    shape = pieces[0].shape
    whole = lambda s: pl.BlockSpec(s, lambda i: (0, 0, 0, 0))
    stacked = (len(pieces) * shape[0],) + shape[1:]
    return pl.pallas_call(
        functools.partial(stack_kernel, len(pieces)),
        grid=(1,),
        in_specs=[whole(shape)] * len(pieces) + [pl.BlockSpec(memory_space=pl.ANY)] * len(after),
        out_specs=whole(stacked),
        out_shape=jax.ShapeDtypeStruct(stacked, bf16),
        compiler_params=params(16),
        cost_estimate=pl.CostEstimate(flops=1000, bytes_accessed=1000, transcendentals=0),
        name="stack_pieces",
    )(*pieces, *after)


class SeqSum:
    def __init__(self, grads, seq_count):
        self.grads, self.seq_count, self.lines = grads, seq_count, seq_count // 4
        self.cross = [(i, i ^ 2) for i in range(seq_count)]
        self.got = [self.to_sibling(g) for g in grads[:2]]
        bits = self.lines.bit_length() - 1
        self.left = [self.over_core, self.over_x]
        self.left += [functools.partial(self.over_line, 1 << k) for k in range(bits)]
        self.left += [functools.partial(self.back_line, 1 << k) for k in reversed(range(bits))]

    def step(self, after):
        return [self.left.pop(0)(after)]

    def to_sibling(self, x):
        return lax.ppermute(x, "seq", sibling_pairs(self.seq_count))

    def to_line(self, x, step):
        return lax.ppermute(x, "seq", line_pairs(self.seq_count, step))

    def over_core(self, after):
        (first,) = sum_blocks([self.grads[2], self.got[0]], 1, after, "sum_core")
        self.crossed = lax.ppermute(first, "seq", self.cross)
        return first

    def over_x(self, after):
        self.kept, sent = sum_blocks([self.grads[3], self.got[1], self.crossed], 2, after, "sum_x")
        self.arriving = self.to_line(sent, 1)
        return sent

    def over_line(self, step, after):
        if 2 * step < self.lines:
            self.kept, sent = sum_blocks([self.kept, self.arriving], 2, after, "sum_line")
            self.arriving = self.to_line(sent, 2 * step)
            return sent
        (shard,) = sum_blocks([self.kept, self.arriving], 1, after, "sum_line")
        self.own = shard[None]
        self.arriving = self.to_line(self.own, step)
        return shard

    def back_line(self, step, after):
        self.own = stack_pieces([self.own, self.arriving], after)
        if step > 1:
            self.arriving = self.to_line(self.own, step // 2)
        else:
            self.other = lax.ppermute(self.own, "seq", self.cross)
        return self.own

    def near_blocks(self):
        return [self.own, self.to_sibling(self.own)]

    def far_blocks(self, after):
        other = stack_pieces([self.other], after) if after else self.other
        return [other, self.to_sibling(other)]


def step_order(sums):
    left = [len(s.left) for s in sums]
    order = []
    while any(left):
        for g in range(len(sums)):
            if left[g]:
                order.append(g)
                left[g] -= 1
    return order


def unpack_kernel(blocks, lines, each, width, where, place, *refs):
    win_ref, wout_ref, token_ref = refs[-3:]
    token_ref[...] = jnp.zeros_like(token_ref)
    step = pl.program_id(0)

    def read(ref, i, with_in, with_out):
        for p in range(lines):
            block = ref[place_of(p, place[0], lines), i].astype(f32)
            part, ff = block.shape
            low = p * part
            if with_in and low < width:
                win_ref[0, low : low + part, :] = block
            else:
                low = low - width if with_in else low
                for j in range(ff // width):
                    wout_ref[0, j * width + low : j * width + low + part, :] = block[:, j * width : (j + 1) * width]

    if refs[0].shape[2] * lines > width:
        for a in range(blocks):
            for i in range(each):
                pl.when(step == a * each + i)(functools.partial(read, refs[a], i, True, True))
    else:
        for k in range(2):
            for column in range(2):

                @pl.when((step == k) & (place[1] == column))
                def _(k=k, column=column):
                    own, other = refs[2 * k], refs[2 * k + 1]
                    read((own, other)[column], 0, True, False)
                    read((other, own)[column], 0, False, True)


def unpack(where, place, blocks, experts, width, ff, into):
    lines, each = blocks[0].shape[:2]
    whole = pl.BlockSpec(blocks[0].shape, lambda i, *_: (0, 0, 0, 0))
    out = lambda *shape: pl.BlockSpec((1,) + shape, lambda i, where, place: (where[i], 0, 0))
    return pl.pallas_call(
        functools.partial(unpack_kernel, len(blocks), lines, each, width),
        grid_spec=pltpu.PrefetchScalarGridSpec(
            num_scalar_prefetch=2,
            grid=where.shape,
            in_specs=[whole] * len(blocks) + [pl.BlockSpec(memory_space=pl.ANY)] * len(into),
            out_specs=[out(width, ff), out(ff, width), pl.BlockSpec((8, 128), lambda i, *_: (0, 0))],
        ),
        out_shape=[
            jax.ShapeDtypeStruct((experts, width, ff), f32),
            jax.ShapeDtypeStruct((experts, ff, width), f32),
            jax.ShapeDtypeStruct((8, 128), f32),
        ],
        input_output_aliases={2 + len(blocks) + i: i for i in range(len(into))},
        compiler_params=params(16),
        cost_estimate=pl.CostEstimate(
            flops=EAGER * where.shape[0] * 2 * width * ff * 6, bytes_accessed=where.shape[0] * 2 * width * ff * 6, transcendentals=0
        ),
        name="unpack",
    )(where, place, *blocks, *into)


def shards(
    query_cols,
    key_cols,
    value_cols,
    block_list,
    residual,
    out_proj,
    norm_gain,
    router_weight,
    expert_ids,
    expert_in,
    expert_out,
    cotangent,
):
    seq_count = lax.axis_size("seq")
    exp_count = lax.axis_size("expert")
    me = lax.axis_index("expert")
    feat, nodes = query_cols.shape
    blk_seq, degree = block_list.shape
    block_len = nodes // blk_seq
    tok_dev, width = residual.shape
    expert_total = router_weight.shape[1]
    experts = expert_in.shape[0]
    ff = expert_in.shape[2]
    topk = expert_ids.shape[1]
    chunk = min(256, tok_dev)
    capacity = 2 * tok_dev * topk // expert_total * exp_count
    slot_rows = capacity + WINDOW

    cuts = [0, blk_seq * 5 // 8, blk_seq]
    keys, values = ring_gather(key_cols, value_cols, seq_count)
    tables = block_tables(block_list, blk_seq, seq_count, cuts)

    residual_all = gather_expert_axis(residual, exp_count)
    cotangent_all = gather_expert_axis(cotangent, exp_count)
    ids_all = gather_expert_axis(expert_ids.T, exp_count, 1)
    gain = norm_gain.reshape(1, width)
    core, column, line = seq_place()
    lines = seq_count // 4
    place = jnp.stack([line, column]).astype(jnp.int32)
    groups = [4] * (experts // 4)
    groups += [2] * ((experts - sum(groups)) // 2)
    dests = [(1 - core, 1 - column), (1 - core, column), (core, 1 - column), (core, column)]
    perm, wheres, first = [], [], 0
    for count in groups:
        if count == 4:
            perm += [first + 2 * c + x for c, x in dests]
            wheres.append([first + 2 * c + x for c, x in (dests[3], dests[2], dests[1], dests[0])])
        else:
            perm += [first + 1 - core, first + core]
            wheres.append([first + core, first + 1 - core])
        first += count
    perm = jnp.stack(perm).astype(jnp.int32)
    wheres = [jnp.stack(w).astype(jnp.int32) for w in wheres]
    local_ids = me * experts + perm
    hot = jnp.sum((ids_all[None, :, :] == local_ids[:, None, None]).astype(jnp.int32), 1)
    running = jnp.cumsum(hot, 1)
    rank = jnp.where(hot > 0, running - 1, -(1 << 20))
    ends = running[:, chunk - 1 :: chunk]
    starts = jnp.concatenate([jnp.zeros((experts, 1), jnp.int32), ends], 1).T
    counts = running[:, -1]
    router = jnp.pad(router_weight, ((0, 0), (0, -expert_total % 128)))
    columns = lax.dynamic_slice_in_dim(router_weight.T, me * experts, experts, 0).astype(f32).reshape(experts, 1, width)
    projs = [
        lax.dynamic_slice_in_dim(out_proj, lax.rem(me + exp_count - d, exp_count) * feat, feat, 0)
        for d in range(exp_count)
    ]
    owner_order = lax.rem(me + jnp.arange(exp_count, dtype=jnp.int32), exp_count)

    pieces = [[] for _ in range(exp_count)]
    for table, low, high in zip(tables, cuts[:-1], cuts[1:]):
        part = attention(query_cols, keys, values, table, low, high - low, block_len, degree)
        pieces[0].append(part)
        for d in range(1, exp_count):
            pieces[d].append(lax.ppermute(part, "expert", shift_pairs(exp_count, d)))
    atts = [jnp.concatenate(p, 0) for p in pieces]

    scalars = (counts, local_ids, perm, starts, place)
    common = (rank, cotangent_all, gain, router)
    weights = (expert_in, expert_out, columns)
    sums, last, stream, rows_parts, first = [], [], None, [], 0
    for g, count in enumerate(groups):
        head = (residual_all, atts, projs) if g == 0 else None
        found = list(expert_group(scalars, common, weights, first, count, head, (stream, last), lines, slot_rows, chunk))
        first += count
        if g == 0:
            stream = found.pop(0)
        rows_parts.append(found[0])
        sums.append(SeqSum(found[1:], seq_count))
        if g == 0:
            last = sums[0].step(last)
    steps = step_order(sums)
    for k, g in enumerate(steps):
        last = sums[g].step(last)
        if k == len(groups) - 1:
            partials = list(combine(starts, owner_order, rank, rows_parts, chunk, last))
            last = [partials[0]]
            parts = partials[:1] + [
                lax.ppermute(partials[d], "expert", shift_pairs(exp_count, d)) for d in range(1, exp_count)
            ]
    layer_out, grad_stream, home = at_home(me, stream, cotangent, gain, parts, chunk, last[0])
    into, done = [], []
    for g, (count, each_sum) in enumerate(zip(groups, sums)):
        where, after = wheres[g], []
        if g == len(groups) - 1:
            after = done + [home]
            if count > 2:
                near = jnp.concatenate([where[: count // 4], where[count // 2 : 3 * count // 4]])
                *into, token = unpack(near, place, each_sum.near_blocks(), experts, width, ff, into)
                where = jnp.concatenate([where[count // 4 : count // 2], where[3 * count // 4 :]])
                after = [token, home]
        blocks = each_sum.far_blocks(after)
        if where is wheres[g]:
            own, other = each_sum.near_blocks(), blocks
            blocks = [own[0], other[0], own[1], other[1]]
        *into, token = unpack(where, place, blocks, experts, width, ff, into)
        done = [token]
    grad_w_in, grad_w_out = into
    return layer_out, grad_stream, grad_w_in, grad_w_out


def solution(mesh):
    return jax.shard_map(
        shards,
        mesh=mesh,
        in_specs=(
            P("expert", "seq"),
            P("expert", "seq"),
            P("expert", "seq"),
            P("seq", None),
            P(("seq", "expert"), None),
            P(),
            P(),
            P(),
            P(("seq", "expert"), None),
            P("expert", None, None),
            P("expert", None, None),
            P(("seq", "expert"), None),
        ),
        out_specs=(
            P(("seq", "expert"), None),
            P(("seq", "expert"), None),
            P("expert", None, None),
            P("expert", None, None),
        ),
        check_vma=False,
    )
```
